32 devices in a mesh: dp: 8 (over z, y), tensor: 4 (over x, core).
Axes of the slice: x: 2, y: 2, z: 4, core: 2. Of those that a mesh axis runs over, the one named last changes fastest.
Arguments:
- tokens: bfloat16 [8192, 2048], P(('dp', 'tensor')), may hold values from -6 to 6
- ln_gain: float32 [2048], replicated, may hold values from 0.1 to 1.9
- ln_bias: float32 [2048], replicated, may hold values from -1.75 to 1.75
- w_qkv: bfloat16 [2048, 3, 2048], P('dp', None, 'tensor'), may hold values from -0.125 to 0.125
- b_qkv: float32 [3, 2048], P(None, 'tensor'), may hold values from -3 to 3
- w_out: bfloat16 [2048, 2048], P('tensor', 'dp'), may hold values from -0.5 to 0.5
- w_up: bfloat16 [2048, 8192], P('dp', 'tensor'), may hold values from -0.125 to 0.125
- b_up: float32 [8192], P('tensor'), may hold values from -3 to 3
- w_down: bfloat16 [8192, 2048], P('tensor', 'dp'), may hold values from -0.0625 to 0.0625
- out_bias: float32 [2048], replicated, may hold values from -3 to 3
- cotangent: bfloat16 [8192, 2048], P(('dp', 'tensor')), may hold values from -12 to 12, as said below
Outputs:
- output: bfloat16 [8192, 2048], P(('dp', 'tensor'))
- grad_tokens: float32 [8192, 2048], P(('dp', 'tensor'))
- grad_ln_gain: float32 [2048], replicated
- grad_ln_bias: float32 [2048], replicated
- grad_w_qkv: float32 [2048, 3, 2048], P('dp', None, 'tensor')
- grad_b_qkv: float32 [3, 2048], P(None, 'tensor')
- grad_w_out: float32 [2048, 2048], P('tensor', 'dp')
- grad_w_up: float32 [2048, 8192], P('dp', 'tensor')
- grad_b_up: float32 [8192], P('tensor')
- grad_w_down: float32 [8192, 2048], P('tensor', 'dp')
- grad_out_bias: float32 [2048], replicated
The draws below stay inside these ranges and needn't reach their ends.
Inputs may be any that keep to these rules, and one draw needn't show every extreme that they name: cotangent of the block's output.
All inputs are finite; a program needn't handle non-finite values.
Results may differ from the reference program's by a relative error of at most 0.012.
The reference program's roundings to bfloat16 on the way count: a program that leaves them out, or rounds other values in their place, can miss the bound.
Values may be sent and summed in bfloat16 or wider, within the bound.
A program may use at most 256 MiB of HBM per device.

```python
import jax
import jax.numpy as jnp
from jax import lax

D = 2048
HEADS = 32
HEAD_DIM = 64
FF = 8192
ROT = 32
LEN = 1024
TOKENS = 8192
N_DP = 8


def draw_cotangent(key, part):
    key = jax.random.fold_in(key, 11)
    row_pos = jnp.arange(TOKENS).astype(jnp.float32) / TOKENS
    rising = 1.0 + 2.0 * row_pos
    base = jnp.clip(jax.random.normal(key, (TOKENS, D), jnp.float32), -4.0, 4.0)
    values = base * rising[:, None]
    return values.astype(jnp.bfloat16)


def block_levels(own_key, shape, split, low, largest):
    def one(position, parts):
        steps = jax.random.uniform(jax.random.fold_in(jax.random.fold_in(own_key, 6), position), (parts,), jnp.float32, low / len(split), largest / len(split))
        return jnp.repeat(jnp.exp(steps), shape[position] // parts).reshape((-1,) + (1,) * (len(shape) - position - 1))

    level = one(*split[0])
    for cut in split[1:]:
        level = level * one(*cut)
    return level


def centred(own_key, shape, scale, most, shards=(), dtype=jnp.bfloat16):
    values = jax.random.normal(own_key, shape, jnp.float32) * scale
    if len(shards) > 0:
        values = block_levels(own_key, shape, shards, -0.22, 0.18) * values
    return jnp.clip(values, min=-most, max=most).astype(dtype)


def setup_inputs(seed: int = 0) -> dict:
    streams_of = jax.random.split(jax.random.key(seed), 12)
    return {
        "tokens": centred(streams_of[0], (TOKENS, D), 1.0, 6.0, ((0, 32),)),
        "ln_gain": jnp.clip(1.0 + 0.18 * jax.random.normal(streams_of[1], (D,), jnp.float32), 0.1, 1.9),
        "ln_bias": centred(streams_of[2], (D,), 0.3, 1.75, (), jnp.float32),
        "w_qkv": centred(streams_of[3], (D, 3, D), D ** -0.5, 0.125, ((0, 8), (2, 4))),
        "b_qkv": centred(streams_of[4], (3, D), 0.5, 3.0, ((1, 4),), jnp.float32),
        "w_out": centred(streams_of[5], (D, D), (D // 16) ** -0.5, 0.5, ((0, 4), (1, 8))),
        "w_up": centred(streams_of[6], (D, FF), D ** -0.5, 0.125, ((0, 8), (1, 4))),
        "b_up": centred(streams_of[7], (FF,), 0.5, 3.0, ((0, 4),), jnp.float32),
        "w_down": centred(streams_of[8], (FF, D), FF ** -0.5, 0.0625, ((0, 4), (1, 8))),
        "out_bias": centred(streams_of[9], (D,), 0.5, 3.0, (), jnp.float32),
        "cotangent": draw_cotangent(jax.random.fold_in(streams_of[11], 71), 0),
    }


highest = lax.Precision.HIGHEST
epsilon = 1e-05

@jax.custom_vjp
def low(v):
    return lax.optimization_barrier(v.astype(jnp.bfloat16)).astype(jnp.float32)

@jax.custom_vjp
def low_back(v):
    return v

def low_keep(v):
    return (low(v), None)

def low_pass(kept, grad):
    return (grad,)

def back_keep(v):
    return (v, None)

def back_low(kept, grad):
    return (low(grad),)
low.defvjp(low_keep, low_pass)
low_back.defvjp(back_keep, back_low)

def rotary_tables(row_count):
    half_rot = ROT // 2
    positions = jnp.arange(row_count).astype(jnp.float32)
    freqs = 10000.0 ** (-(2.0 * jnp.arange(half_rot).astype(jnp.float32)) / ROT)
    angles = positions[:, None] * freqs[None, :]
    return (jnp.cos(angles)[:, None, :], jnp.sin(angles)[:, None, :])

def rotate(field, cosines, sines):
    half_rot = ROT // 2
    first = field[..., :half_rot]
    second = field[..., half_rot:ROT]
    return jnp.concatenate([first * cosines - second * sines, second * cosines + first * sines, field[..., ROT:]], axis=-1)

def attention(queries, key_rows, value_rows):
    row_count = key_rows.shape[0]
    block_len = min(row_count, 512)
    n_blocks = row_count // block_len
    scaling = HEAD_DIM ** (-0.5)
    key_pos = jnp.arange(row_count)
    query_blocks = queries.reshape(n_blocks, block_len, HEADS, HEAD_DIM)

    def one_block(item):
        query_block, block_index = item
        query_pos = block_index * block_len + jnp.arange(block_len)
        raw = jnp.einsum('qhd,khd->hqk', query_block, key_rows, precision=highest)
        scores = low_back(raw) * scaling
        scores = jnp.where(key_pos[None, None, :] <= query_pos[None, :, None], scores, -1e+30)
        probability = low(jax.nn.softmax(scores, axis=2))
        return jnp.einsum('hqk,khd->qhd', probability, value_rows, precision=highest)
    outputs = lax.map(jax.checkpoint(one_block), (query_blocks, jnp.arange(n_blocks)))
    return outputs.reshape(row_count, HEADS * HEAD_DIM)

def forward(activ, ln_gain, ln_bias, w_qkv, b_qkv, w_out, w_up, b_up, w_down, out_bias):
    row_count = activ.shape[0]
    average = lax.optimization_barrier(jnp.mean(activ, axis=1, keepdims=True))
    centered = activ - average
    variance = lax.optimization_barrier(jnp.mean(centered * centered, axis=1, keepdims=True))
    normed = low(centered * lax.rsqrt(variance + epsilon) * ln_gain + ln_bias)
    project = low_back(jnp.einsum('td,dcf->tcf', normed, w_qkv, precision=highest) + b_qkv)
    cosines, sines = rotary_tables(row_count)
    head_shape = (row_count, HEADS, HEAD_DIM)
    queries = low(rotate(project[:, 0].reshape(head_shape), cosines, sines))
    key_rows = low(rotate(project[:, 1].reshape(head_shape), cosines, sines))
    value_rows = low(project[:, 2].reshape(head_shape))
    attended = low(low_back(attention(queries, key_rows, value_rows)))
    hidden = low_back(jnp.dot(normed, w_up, precision=highest) + b_up)
    activated = low(jax.nn.gelu(hidden, approximate=True))
    branch_attn = jnp.dot(attended, w_out, precision=highest)
    branch_mlp = jnp.dot(activated, w_down, precision=highest)
    return activ + branch_attn + branch_mlp + out_bias

def reference(tokens, ln_gain, ln_bias, w_qkv, b_qkv, w_out, w_up, b_up, w_down, out_bias, cotangent):
    params = (ln_gain.astype(jnp.float32), ln_bias.astype(jnp.float32), w_qkv.astype(jnp.float32), b_qkv.astype(jnp.float32), w_out.astype(jnp.float32), w_up.astype(jnp.float32), b_up.astype(jnp.float32), w_down.astype(jnp.float32), out_bias.astype(jnp.float32))
    sequences = tokens.astype(jnp.float32).reshape(N_DP, LEN, D)
    cot_seqs = cotangent.astype(jnp.float32).reshape(N_DP, LEN, D)

    def one_sequence(carry, item):
        activ, cot_rows = item
        result, pull = jax.vjp(forward, activ, *params)
        grads = pull(cot_rows)
        summed = tuple((total + grad for total, grad in zip(carry, grads[1:])))
        return (summed, (result, grads[0]))
    zeros = tuple((jnp.zeros_like(param) for param in params))
    sums, (results, grad_rows) = lax.scan(one_sequence, zeros, (sequences, cot_seqs))
    output = results.reshape(TOKENS, D).astype(jnp.bfloat16)
    grad_tokens = grad_rows.reshape(TOKENS, D)
    return (output, grad_tokens, sums[0], sums[1], sums[2], sums[3], sums[4], sums[5], sums[6], sums[7], sums[8])
```

```python
import functools
import math

import jax
import jax.numpy as jnp
from jax import lax
from jax.experimental import pallas as pl
from jax.experimental.pallas import tpu as pltpu
from jax.sharding import PartitionSpec as P

HEAD_DIM = 64
ROT = 32
epsilon = 1e-05
big_negative = -1e30

f32 = jnp.float32
bf16 = jnp.bfloat16
NN = (((1,), (0,)), ((), ()))
NT = (((1,), (1,)), ((), ()))
TN = (((0,), (0,)), ((), ()))
dot = functools.partial(lax.dot_general, preferred_element_type=f32)

GELU_A = math.sqrt(2.0 / math.pi)
GELU_B = 0.044715
CHUNK = 512
Q_BLOCK = 128
LANES = 128


def gelu(h):
    return 0.5 * h * (1.0 + jnp.tanh(GELU_A * (h + GELU_B * h * h * h)))


def gelu_slope(h):
    t = jnp.tanh(GELU_A * (h + GELU_B * h * h * h))
    return 0.5 * (1.0 + t) + 0.5 * h * (1.0 - t * t) * (GELU_A * (1.0 + 3.0 * GELU_B * h * h))


def rotary_tables(row_count):
    half_rot = ROT // 2
    positions = jnp.arange(row_count).astype(f32)
    freqs = 10000.0 ** (-(2.0 * jnp.arange(half_rot).astype(f32)) / ROT)
    angles = positions[:, None] * freqs[None, :]
    cosines, sines = jnp.cos(angles), jnp.sin(angles)
    rest = jnp.zeros((row_count, HEAD_DIM - ROT), f32)
    c_head = jnp.concatenate([cosines, cosines, rest + 1.0], axis=1)
    s_head = jnp.concatenate([-sines, sines, rest], axis=1)
    return jnp.concatenate([c_head, c_head], axis=1), jnp.concatenate([s_head, s_head], axis=1)


def rotate(field, cosines, sines):
    half = ROT // 2
    lane = lax.broadcasted_iota(jnp.int32, field.shape, 1)
    first = lax.rem(lane, HEAD_DIM) < half
    partner = jnp.where(
        first, pltpu.roll(field, LANES - half, 1), pltpu.roll(field, half, 1)
    )
    return field * cosines + partner * sines


def block_kernel(
    tokens, cot, gain, shift, out_bias, wq_in, wo_in, wu_in, wd_in, bq_in, bu_in, cos_t, sin_t,
    o_out, o_gt, o_vec, o_gq, o_go, o_gu, o_gd, ry, rm, rc, rx, rl,
    XN, G, WU, WD, WQ, WO, ACT, DH, ATT, DP, YS, FF, RING, LD, VEC, SV, SS, SR,
    ssem, rsem, lsem,
):
    T, D = tokens.shape
    R = wu_in.shape[0]
    F = wu_in.shape[1] // 2
    H = wo_in.shape[0] // 2
    ROWS = 8 * T
    LEN = 4 * T
    half_d = D // 2

    dp = lax.axis_index("dp")
    tp = lax.axis_index("tensor")
    hi = lax.div(dp, 4)
    lo = lax.rem(lax.div(dp, 2), 2)
    y = lax.rem(dp, 2)
    x = lax.div(tp, 2)
    c = lax.rem(tp, 2)

    def device(hi_=None, lo_=None, y_=None, x_=None, c_=None):
        a = hi if hi_ is None else hi_
        b = lo if lo_ is None else lo_
        d = y if y_ is None else y_
        e = x if x_ is None else x_
        g = c if c_ is None else c_
        return {"dp": (a * 2 + b) * 2 + d, "tensor": e * 2 + g}

    to_x = device(x_=1 - x)
    to_c = device(c_=1 - c)
    to_lo = device(lo_=1 - lo)
    to_y = device(y_=1 - y)
    to_hi = device(hi_=1 - hi)
    to_hilo = device(hi_=1 - hi, lo_=1 - lo)
    partners = [to_x, to_c, to_lo, to_y, to_hi, to_hilo]

    def mult(v, n):
        return pl.multiple_of(v, n)

    n_copies = [0]
    n_local = [0]
    pending = []

    class Send:
        def __init__(self, src, dst, dev):
            i = n_copies[0]
            n_copies[0] += 1
            self.d = pltpu.make_async_remote_copy(
                src_ref=src, dst_ref=dst, send_sem=ssem.at[i], recv_sem=rsem.at[i],
                device_id=dev, device_id_type=pl.DeviceIdType.MESH,
            )
            self.open = False

        def start(self):
            self.d.start()
            self.open = True
            pending.append(self)
            return self

        def got(self):
            self.d.wait_recv()

        def sent(self):
            if self.open:
                self.d.wait_send()
                self.open = False

    class Local:
        def __init__(self, src, dst):
            i = n_local[0]
            n_local[0] += 1
            self.d = pltpu.make_async_copy(src, dst, lsem.at[i])
            self.d.start()
            self.open = True

        def wait(self):
            if self.open:
                self.d.wait()
                self.open = False

    def col(p, low):
        return mult(p * 2 * R + low * R, R)

    def abs_block(p, low):
        hi_ = hi if p < 2 else 1 - hi
        y_ = y if p % 2 == 0 else 1 - y
        return mult(((hi_ * 2 + low) * 2 + y_) * R, R)

    def row(low, xx, cc):
        return mult((low * 4 + xx * 2 + cc) * T, T)

    own_row = row(lo, x, c)
    own_rows = pl.ds(own_row, T)

    tok_loads, cot_loads = [], []
    for p in range(4):
        for low in range(2):
            dst = pl.ds(p * 2 * R + low * R, R)
            src = pl.ds(abs_block(p, low), R)
            tok_loads.append(Local(tokens.at[:, src], RING.at[0, :, dst]))
            cot_loads.append(Local(cot.at[:, src], G.at[own_rows, dst]))

    barrier = pltpu.get_barrier_semaphore()
    for dev in partners:
        pl.semaphore_signal(barrier, inc=1, device_id=dev, device_id_type=pl.DeviceIdType.MESH)
    pl.semaphore_wait(barrier, len(partners))

    class Weight:
        def __init__(self, src, land):
            self.own = Local(src(lo), land(0, lo))
            self.a = Send(src(1 - lo), land(0, lo), to_lo)
            self.c = Send(src(lo), land(2, lo), to_hi)
            self.e = Send(src(1 - lo), land(2, lo), to_hilo)
            self.dd = Send(src(lo), land(1, lo), to_y)
            self.f = Send(land(0, 1 - lo), land(1, 1 - lo), to_y)
            self.g = Send(land(2, lo), land(3, lo), to_y)
            self.h = Send(land(2, 1 - lo), land(3, 1 - lo), to_y)

        def open(self):
            self.a.start()
            self.dd.start()

        def far(self):
            self.c.start()
            self.e.start()

        def relay_near(self):
            self.a.got()
            self.f.start()

        def relay_far(self):
            self.c.got()
            self.g.start()
            self.e.got()
            self.h.start()

        def ready(self):
            self.own.wait()
            for s in (self.dd, self.f, self.g, self.h):
                s.got()

    w_up = Weight(
        lambda h: wu_in.at[:, pl.ds(mult(h * F, F), F)],
        lambda p, low: WU.at[pl.ds(col(p, low), R), :],
    )
    w_q = Weight(lambda h: wq_in.at[h], lambda p, low: WQ.at[pl.ds(col(p, low), R), :])
    w_o = Weight(
        lambda h: wo_in.at[pl.ds(mult(h * H, H), H), :],
        lambda p, low: WO.at[:, pl.ds(col(p, low), R)],
    )
    w_dn = Weight(
        lambda h: wd_in.at[pl.ds(mult(h * F, F), F), :],
        lambda p, low: WD.at[:, pl.ds(col(p, low), R)],
    )
    w_up.far()
    w_up.open()

    class Rows:
        def __init__(self, buf):
            def at(low, xx, cc):
                return buf.at[pl.ds(row(low, xx, cc), T), :]

            self.lo_own = Send(at(lo, x, c), at(lo, x, c), to_lo)
            self.x_own = Send(at(lo, x, c), at(lo, x, c), to_x)
            self.x_lo = Send(at(1 - lo, x, c), at(1 - lo, x, c), to_x)
            self.c_own = Send(at(lo, x, c), at(lo, x, c), to_c)
            self.c_lo = Send(at(1 - lo, x, c), at(1 - lo, x, c), to_c)
            self.c_x = Send(at(lo, 1 - x, c), at(lo, 1 - x, c), to_c)
            self.c_xlo = Send(at(1 - lo, 1 - x, c), at(1 - lo, 1 - x, c), to_c)

        def open(self):
            self.lo_own.start()
            self.x_own.start()
            self.c_own.start()

        def relay_lo(self):
            self.lo_own.got()
            self.x_lo.start()
            self.c_lo.start()

        def relay_x(self):
            self.x_own.got()
            self.c_x.start()

        def relay_xlo(self):
            self.x_lo.got()
            self.c_xlo.start()

        def ready(self):
            for s in (self.c_own, self.c_lo, self.c_x, self.c_xlo):
                s.got()

    rows_n = Rows(XN)
    rows_g = Rows(G)

    for p in range(4):
        for low in range(2):
            dst = pl.ds(p * 2 * R + low * R, R)
            src = pl.ds(abs_block(p, low), R)
            VEC[0:1, dst] = gain[:, src]
            VEC[1:2, dst] = shift[:, src]
            VEC[2:3, dst] = out_bias[:, src]
    for ld in tok_loads:
        ld.wait()

    def normalise(k, sub):
        activ = RING[k, sub, :].astype(f32)
        average = jnp.mean(activ, axis=1, keepdims=True)
        centered = activ - average
        variance = jnp.mean(centered * centered, axis=1, keepdims=True)
        inv_std = lax.rsqrt(variance + epsilon)
        return centered * inv_std, inv_std

    LN_ROWS = min(T, 64)

    def ln_body(i, carry):
        x_hat, _ = normalise(0, pl.ds(mult(i * LN_ROWS, LN_ROWS), LN_ROWS))
        XN[pl.ds(mult(own_row + i * LN_ROWS, LN_ROWS), LN_ROWS), :] = (
            x_hat * VEC[0:1, :] + VEC[1:2, :]
        ).astype(bf16)

    lax.fori_loop(0, T // LN_ROWS, ln_body, None)
    rows_n.open()
    for ld in cot_loads:
        ld.wait()
    rows_g.open()

    SV[...] = jnp.zeros_like(SV)
    for p in range(4):
        for low in range(2):
            SV[2:3, pl.ds(abs_block(p, low), R)] = jnp.sum(
                G[own_rows, p * 2 * R + low * R : p * 2 * R + (low + 1) * R].astype(f32),
                axis=0,
                keepdims=True,
            )

    w_up.relay_near()
    rows_n.relay_lo()
    rows_n.relay_x()
    w_up.relay_far()
    w_q.far()
    w_o.far()
    w_q.open()
    w_o.open()
    rows_n.relay_xlo()
    rows_g.relay_lo()
    rows_g.relay_x()
    w_up.ready()
    rows_n.ready()

    TILE = T

    def hidden(rows):
        return dot(XN[rows, :], WU[...], NN) + bu_in[lo]

    def act_body(i, _):
        rows = pl.ds(mult(i * TILE, TILE), TILE)
        ACT[rows, :] = gelu(hidden(rows)).astype(bf16)

    lax.fori_loop(0, ROWS // TILE, act_body, None)

    w_q.relay_near()
    w_o.relay_near()
    rows_g.relay_xlo()
    w_q.relay_far()
    w_o.relay_far()
    w_dn.far()
    w_dn.open()
    rows_g.ready()

    def cols_of(p, q):
        low = lo if q == 0 else 1 - lo
        return pl.ds(col(p, low), R)

    def block_dn(p, q):
        gg = G[:, cols_of(p, q)]
        parts = [dot(ACT[:, m * R : (m + 1) * R], gg, TN) for m in range(F // R)]
        return [(m * R, v) for m, v in enumerate(parts)]

    def block_up(p, q):
        xx = XN[:, cols_of(p, q)]
        return [(0, dot(xx, DH[...], TN))]

    def block_at(p, q):
        cc = cols_of(p, q)
        return [(0, dot(XN[:, cc], DP[...], TN)), (3 * H, dot(ATT[...], G[:, cc], TN))]

    class Grads:
        def __init__(self, index, block, finals):
            self.i = index
            self.block = block
            self.finals = finals
            self.ysend = {}
            self.msend = {}
            for k, (p, q) in enumerate(((3, 1), (3, 0), (1, 1), (1, 0))):
                self.ysend[p, q] = Send(YS.at[index, k], ry.at[index, k], to_y)
            for q in (1, 0):
                self.msend[q] = Send(YS.at[index, 1 - q], rm.at[index, 1 - q], to_hi)

        def slot(self, p, q):
            return (0 if p >= 2 else 2) + (1 - q)

        def near(self, p):
            for q in (1, 0):
                k = self.slot(p, q)
                for off, v in self.block(p, q):
                    YS[self.i, k, :, off : off + v.shape[1]] = v.astype(bf16)
                self.ysend[p, q].start()

        def far(self, q):
            k = self.slot(2, q)
            self.ysend[3, q].got()
            load = Local(ry.at[self.i, k], LD.at[0, :, 0:F])
            vals = self.block(2, q)
            self.ysend[3, q].sent()
            load.wait()
            for off, v in vals:
                n = v.shape[1]
                YS[self.i, k, :, off : off + n] = (
                    v + LD[0, :, off : off + n].astype(f32)
                ).astype(bf16)
            self.msend[q].start()

        def last(self, q):
            k = self.slot(0, q)
            settle((q,))
            self.ysend[1, q].got()
            load = Local(ry.at[self.i, k], LD.at[0, :, 0:F])
            vals = self.block(0, q)
            load.wait()
            for off, v in vals:
                n = v.shape[1]
                FF[q, :, off : off + n] = v + LD[0, :, off : off + n].astype(f32)
            self.msend[q].got()
            load = Local(rm.at[self.i, 1 - q], LD.at[1, :, 0:F])
            load.wait()
            FF[q, :, :] += LD[1, :, 0:F].astype(f32)
            for src, dst in self.finals(FF.at[q], lo):
                if q == 1:
                    final_out[q].append(Send(src, dst, to_lo).start())
                    final_in.append(final_out[q][-1])
                else:
                    final_out[q].append(Local(src, dst))

    final_out = {0: [], 1: []}
    final_in = []

    def settle(which=(0, 1)):
        for q in which:
            for s in final_out[q]:
                if isinstance(s, Send):
                    s.sent()
                else:
                    s.wait()
            final_out[q] = []

    gr_dn = Grads(
        0, block_dn,
        lambda src, h: [
            (src.at[:, pl.ds(m * R, R)], o_gd.at[pl.ds(mult(h * F + m * R, R), R), :])
            for m in range(F // R)
        ],
    )
    gr_at = Grads(
        1, block_at,
        lambda src, h: [
            (src.at[:, pl.ds(0, 3 * H)], o_gq.at[h]),
            (src.at[:, pl.ds(3 * H, R)], o_go.at[pl.ds(mult(h * H, H), H), :]),
        ],
    )
    gr_up = Grads(2, block_up, lambda src, h: [(src, o_gu.at[:, pl.ds(mult(h * F, F), F)])])

    gr_dn.near(3)
    gr_dn.near(1)
    for w in (w_q, w_o):
        w.ready()

    Q, K, V, DA = (0, 0), (0, 4 * H), (1, 0), (1, 4 * H)

    def head_rows(which, start, size, cc):
        slot, base = which
        got = []
        at = start
        while at < start + size:
            stop = min((at // T + 1) * T, start + size)
            cols = pl.ds(mult(base + at // T * H + cc, LANES), LANES)
            got.append(RING[slot, at % T : at % T + stop - at, cols])
            at = stop
        return got[0] if len(got) == 1 else jnp.concatenate(got, axis=0)

    def project(s):
        def body(i, _):
            pos = pl.ds(mult(i * T, T), T)
            rows = pl.ds(mult((s * 4 + i) * T, T), T)
            pr = dot(XN[rows, :], WQ[...], NN) + bq_in[lo]
            cs, sn = cos_t[pos, :], sin_t[pos, :]

            def put(which, a, v):
                RING[which[0], :, pl.ds(mult(which[1] + i * H + a, LANES), LANES)] = v.astype(bf16)

            d_att = dot(G[rows, :], WO[...], NT)
            for h in range(H // LANES):
                a = h * LANES
                put(Q, a, rotate(pr[:, a : a + LANES], cs, sn))
                put(K, a, rotate(pr[:, H + a : H + a + LANES], cs, sn))
                put(V, a, pr[:, 2 * H + a : 2 * H + a + LANES])
                put(DA, a, d_att[:, a : a + LANES])

        lax.fori_loop(0, 4, body, None)

    def attend(s):
        first = lax.broadcasted_iota(jnp.int32, (Q_BLOCK, LANES), 1) < HEAD_DIM
        scaling = HEAD_DIM**-0.5

        def split(v):
            zero = jnp.zeros_like(v)
            return jnp.concatenate([jnp.where(first, v, zero), jnp.where(first, zero, v)], axis=0)

        def join(v):
            return jnp.where(first, v[:Q_BLOCK], v[Q_BLOCK:])

        def piece(j):
            at = j * Q_BLOCK
            return pl.ds(at % T, Q_BLOCK), pl.ds(at // T * LANES, LANES)

        def pair(hp, _):
            cc = hp * LANES
            out_cols = pl.ds(mult(cc, LANES), LANES)
            for i in range(LEN // Q_BLOCK):
                rr = pl.ds(i * Q_BLOCK, Q_BLOCK)
                out_rows = pl.ds(s * LEN + i * Q_BLOCK, Q_BLOCK)
                n = (i + 1) * Q_BLOCK
                old = n - Q_BLOCK
                qm = split(head_rows(Q, old, Q_BLOCK, cc))
                dm = split(head_rows(DA, old, Q_BLOCK, cc))
                kk = head_rows(K, 0, n, cc)
                vv = head_rows(V, 0, n, cc)
                st = dot(kk, qm * jnp.asarray(scaling, bf16), NT)
                kpos = lax.broadcasted_iota(jnp.int32, (Q_BLOCK, 2 * Q_BLOCK), 0)
                qpos = lax.broadcasted_iota(jnp.int32, (Q_BLOCK, 2 * Q_BLOCK), 1)
                qpos = jnp.where(qpos < Q_BLOCK, qpos, qpos - Q_BLOCK)
                diagonal = jnp.where(kpos <= qpos, st[old:], big_negative)
                st = diagonal if i == 0 else jnp.concatenate([st[:old], diagonal], axis=0)
                ex = jnp.exp(st - jnp.max(st, axis=0, keepdims=True))
                prob = ex * (1.0 / jnp.sum(ex, axis=0, keepdims=True))
                pb = prob.astype(bf16)
                ATT[out_rows, out_cols] = join(dot(pb, vv, TN)).astype(bf16)
                dv = dot(pb, dm, NN)
                dprob = dot(vv, dm, NT)
                centre = jnp.sum(dprob * prob, axis=0, keepdims=True)
                ds = (prob * (dprob - centre) * scaling).astype(bf16)
                dq = join(dot(ds, kk, TN))
                DP[out_rows, out_cols] = rotate(dq, cos_t[rr, :], -sin_t[rr, :]).astype(bf16)
                dk = dot(ds, qm, NN)
                for j in range(i + 1):
                    pr, pc = piece(j)
                    part = slice(j * Q_BLOCK, (j + 1) * Q_BLOCK)
                    if j < i:
                        FF[0, pr, pc] += dk[part]
                        FF[1, pr, pc] += dv[part]
                    else:
                        FF[0, pr, pc] = dk[part]
                        FF[1, pr, pc] = dv[part]
            for j in range(LEN // Q_BLOCK):
                pr, pc = piece(j)
                rr = pl.ds(j * Q_BLOCK, Q_BLOCK)
                out_rows = pl.ds(s * LEN + j * Q_BLOCK, Q_BLOCK)
                DP[out_rows, pl.ds(mult(H + cc, LANES), LANES)] = rotate(
                    FF[0, pr, pc], cos_t[rr, :], -sin_t[rr, :]
                ).astype(bf16)
                DP[out_rows, pl.ds(mult(2 * H + cc, LANES), LANES)] = FF[1, pr, pc].astype(bf16)

        lax.fori_loop(0, H // LANES, pair, None)

    project(0)
    attend(0)
    w_dn.relay_near()
    project(1)
    w_dn.relay_far()
    gr_dn.far(1)
    gr_dn.far(0)
    attend(1)

    gr_at.near(3)
    gr_at.near(1)

    def rows_out(rr, cc):
        return dot(ACT[rr, :], WD[:, cc], NN) + dot(ATT[rr, :], WO[:, cc], NN)

    def rows_dn(rr, cc):
        return dot(DH[rr, :], WU[cc, :], NT) + dot(DP[rr, :], WQ[cc, :], NT)

    ring_use = {0: None, 1: None, 2: None}
    ring_next = [0]

    def ring_slot():
        i = ring_next[0]
        ring_next[0] = (i + 1) % 3
        if ring_use[i] is not None:
            ring_use[i].sent()
            ring_use[i] = None
        return i

    class Owner:
        def __init__(self, index, partial):
            self.i = index
            self.partial = partial
            self.cs, self.xs = {}, {}

        def chunks(self, low, xx, cc, loads, store):
            rr = pl.ds(row(low, xx, cc), T)
            for ld in loads:
                ld.wait()

            def body(j, _):
                cols = pl.ds(mult(j * CHUNK, CHUNK), CHUNK)
                v = self.partial(rr, cols)
                for k in range(len(loads)):
                    v = v + LD[k, :, cols].astype(f32)
                store(j, cols, v)

            lax.fori_loop(0, D // CHUNK, body, None)

        def put(self, low, xx, cc, srcs, dst, dev):
            loads = [Local(src, LD.at[k]) for k, src in enumerate(srcs)]
            k = ring_slot()

            def store(j, cols, v):
                RING[k, :, cols] = v.astype(bf16)

            self.chunks(low, xx, cc, loads, store)
            s = Send(RING.at[k], dst, dev).start()
            ring_use[k] = s
            return s

        def core(self):
            for dlo, dx in ((1, 1), (0, 1), (1, 0), (0, 0)):
                low = lo if dlo == 0 else 1 - lo
                xx = x if dx == 0 else 1 - x
                self.cs[dlo, dx] = self.put(
                    low, xx, 1 - c, [], rc.at[self.i, 2 * dlo + dx], to_c
                )

        def cross(self):
            for dlo in (1, 0):
                low = lo if dlo == 0 else 1 - lo
                self.cs[dlo, 1].got()
                self.xs[dlo] = self.put(
                    low, 1 - x, c, [rc.at[self.i, 2 * dlo + 1]], rx.at[self.i, dlo], to_x
                )

        def level(self):
            self.cs[1, 0].got()
            self.xs[1].got()
            self.ls = self.put(
                1 - lo, x, c, [rc.at[self.i, 2], rx.at[self.i, 1]], rl.at[self.i], to_lo
            )

        def own(self):
            self.cs[0, 0].got()
            self.xs[0].got()
            loads = [Local(rc.at[self.i, 0], LD.at[0]), Local(rx.at[self.i, 0], LD.at[1])]

            def store(j, cols, v):
                FF[lax.div(j, D // CHUNK // 2), :, pl.ds(mult(lax.rem(j, D // CHUNK // 2) * CHUNK, CHUNK), CHUNK)] = v

            self.chunks(lo, x, c, loads, store)
            self.ls.got()
            Local(rl.at[self.i], LD.at[0]).wait()

    def own_sub(sub):
        return jnp.concatenate([FF[0, sub, :], FF[1, sub, :]], axis=1) + LD[0, sub, :].astype(f32)

    own_out = Owner(0, rows_out)
    own_dn = Owner(1, rows_dn)

    w_dn.ready()
    own_out.core()

    VEC[3:4, 0:F] = jnp.zeros((1, F), f32)

    def dh_body(i, _):
        rows = pl.ds(mult(i * TILE, TILE), TILE)
        d_act = dot(G[rows, :], WD[...], NT)
        dh = (d_act * gelu_slope(hidden(rows))).astype(bf16)
        DH[rows, :] = dh
        VEC[3:4, 0:F] += jnp.sum(dh.astype(f32), axis=0, keepdims=True)

    lax.fori_loop(0, ROWS // TILE // 2, dh_body, None)
    own_out.cross()
    lax.fori_loop(ROWS // TILE // 2, ROWS // TILE, dh_body, None)

    own_dn.core()
    gr_up.near(3)
    gr_up.near(1)
    gr_at.far(1)
    gr_at.far(0)
    own_dn.cross()
    gr_dn.last(1)
    gr_dn.last(0)
    gr_up.far(1)
    gr_up.far(0)

    SV[3:4, pl.ds(mult(lo * F, F), F)] = VEC[3:4, 0:F]
    VEC[4:5, 0 : 3 * H] = jnp.zeros((1, 3 * H), f32)

    def dp_body(i, _):
        VEC[4:5, 0 : 3 * H] += jnp.sum(
            DP[pl.ds(mult(i * T, T), T), :].astype(f32), axis=0, keepdims=True
        )

    lax.fori_loop(0, ROWS // T, dp_body, None)
    SV[4:5, pl.ds(mult(lo * 3 * H, LANES), 3 * H)] = VEC[4:5, 0 : 3 * H]

    own_out.level()
    settle()

    def load_tokens():
        k = ring_slot()
        return k, [
            Local(
                tokens.at[:, pl.ds(abs_block(p, low), R)],
                RING.at[k, :, pl.ds(p * 2 * R + low * R, R)],
            )
            for p in range(4)
            for low in range(2)
        ]

    k_tok, tok_ld = load_tokens()
    own_out.own()
    for ld in tok_ld:
        ld.wait()
    k_out = ring_slot()

    def out_body(i, _):
        sub = pl.ds(mult(i * LN_ROWS, LN_ROWS), LN_ROWS)
        RING[k_out, sub, :] = (
            RING[k_tok, sub, :].astype(f32) + own_sub(sub) + VEC[2:3, :]
        ).astype(bf16)

    lax.fori_loop(0, T // LN_ROWS, out_body, None)
    out_st = [
        Local(
            RING.at[k_out, :, pl.ds(p * 2 * R + low * R, R)],
            o_out.at[:, pl.ds(abs_block(p, low), R)],
        )
        for p in range(4)
        for low in range(2)
    ]
    for st in out_st:
        st.wait()

    gr_at.last(1)
    own_dn.level()
    gr_at.last(0)
    settle()

    k_x, tok_ld = load_tokens()
    own_dn.own()
    for ld in tok_ld:
        ld.wait()
    VEC[4:6, :] = jnp.zeros((2, D), f32)

    def gt_body(i, _):
        sub = pl.ds(mult(i * LN_ROWS, LN_ROWS), LN_ROWS)
        x_hat, inv_std = normalise(k_x, sub)
        dn = own_sub(sub)
        VEC[4:5, :] += jnp.sum(dn * x_hat, axis=0, keepdims=True)
        VEC[5:6, :] += jnp.sum(dn, axis=0, keepdims=True)
        scaled = dn * VEC[0:1, :]
        gt = (
            inv_std
            * (
                scaled
                - jnp.mean(scaled, axis=1, keepdims=True)
                - x_hat * jnp.mean(scaled * x_hat, axis=1, keepdims=True)
            )
            + G[pl.ds(mult(own_row + i * LN_ROWS, LN_ROWS), LN_ROWS), :].astype(f32)
        )
        FF[0, sub, :] = gt[:, :half_d]
        FF[1, sub, :] = gt[:, half_d:]

    lax.fori_loop(0, T // LN_ROWS, gt_body, None)
    gt_st = []
    for p in range(4):
        for low in range(2):
            off = (p % 2) * 2 * R + low * R
            dst = pl.ds(abs_block(p, low), R)
            src = slice(p * 2 * R + low * R, p * 2 * R + (low + 1) * R)
            gt_st.append(Local(FF.at[p // 2, :, pl.ds(off, R)], o_gt.at[:, dst]))
            SV[0:2, dst] = VEC[4:6, src]

    for k, dev in enumerate((to_y, to_hi, to_lo, to_x, to_c)):
        SS[k, :, :] = SV[...]
        s = Send(SS.at[k], SR.at[k], dev).start()
        s.got()
        if k < 3:
            SV[...] += SR[k]
        else:
            SV[0:3, :] += SR[k, 0:3, :]
    o_vec[...] = SV[...]

    for st in gt_st:
        st.wait()
    gr_up.last(1)
    gr_up.last(0)
    settle()
    for s in final_in:
        s.got()
    for s in pending:
        s.sent()
    assert n_copies[0] <= ssem.shape[0], n_copies
    assert n_local[0] <= lsem.shape[0], n_local


def fast_shards(tokens, ln_gain, ln_bias, w_qkv, b_qkv, w_out, w_up, b_up, w_down, out_bias, cot):
    T, D = tokens.shape
    R, F = w_up.shape[0], w_up.shape[1] // 2
    H = w_out.shape[0] // 2
    cos_t, sin_t = rotary_tables(4 * T)
    wq = w_qkv.reshape(R, 3, 2, H).transpose(2, 0, 1, 3).reshape(2, R, 3 * H)
    bq = b_qkv.reshape(3, 2, H).transpose(1, 0, 2).reshape(2, 1, 3 * H)
    bu = b_up.reshape(2, 1, F)
    S = jax.ShapeDtypeStruct
    hbm = pl.BlockSpec(memory_space=pl.ANY)
    vm = pl.BlockSpec(memory_space=pltpu.VMEM)
    outs = pl.pallas_call(
        block_kernel,
        out_shape=(
            S((T, D), bf16), S((T, D), f32), S((8, D), f32),
            S((2, R, 3 * H), f32), S((2 * H, R), f32), S((R, 2 * F), f32), S((2 * F, R), f32),
            S((3, 4, R, F), bf16), S((3, 2, R, F), bf16),
            S((2, 4, T, D), bf16), S((2, 2, T, D), bf16), S((2, T, D), bf16),
        ),
        in_specs=[hbm, hbm, vm, vm, vm, hbm, hbm, hbm, hbm, vm, vm, vm, vm],
        out_specs=(hbm, hbm, vm) + (hbm,) * 9,
        scratch_shapes=[
            pltpu.VMEM((8 * T, D), bf16),
            pltpu.VMEM((8 * T, D), bf16),
            pltpu.VMEM((D, F), bf16),
            pltpu.VMEM((F, D), bf16),
            pltpu.VMEM((D, 3 * H), bf16),
            pltpu.VMEM((H, D), bf16),
            pltpu.VMEM((8 * T, F), bf16),
            pltpu.VMEM((8 * T, F), bf16),
            pltpu.VMEM((8 * T, H), bf16),
            pltpu.VMEM((8 * T, 3 * H), bf16),
            pltpu.VMEM((3, 4, R, F), bf16),
            pltpu.VMEM((2, R, F), f32),
            pltpu.VMEM((3, T, D), bf16),
            pltpu.VMEM((2, T, D), bf16),
            pltpu.VMEM((8, D), f32),
            pltpu.VMEM((8, D), f32),
            pltpu.VMEM((5, 8, D), f32),
            pltpu.VMEM((5, 8, D), f32),
            pltpu.SemaphoreType.DMA((90,)),
            pltpu.SemaphoreType.DMA((90,)),
            pltpu.SemaphoreType.DMA((110,)),
        ],
        compiler_params=pltpu.CompilerParams(
            collective_id=0, has_side_effects=True, vmem_limit_bytes=VMEM_LIMIT
        ),
        name="parallel_block",
    )(
        tokens, cot, ln_gain.reshape(1, D), ln_bias.reshape(1, D), out_bias.reshape(1, D),
        wq, w_out, w_up, w_down, bq, bu, cos_t, sin_t,
    )
    o_out, o_gt, o_vec, o_gq, o_go, o_gu, o_gd = outs[:7]
    g_qkv = o_gq.reshape(2, R, 3, H).transpose(1, 2, 0, 3).reshape(R, 3, 2 * H)
    g_bq = o_vec[4, : 6 * H].reshape(2, 3, H).transpose(1, 0, 2).reshape(3, 2 * H)
    return (
        o_out, o_gt, o_vec[0], o_vec[1], g_qkv, g_bq, o_go, o_gu, o_vec[3, : 2 * F], o_gd, o_vec[2],
    )


VMEM_LIMIT = 64 << 20


def plain_tables(row_count):
    half_rot = ROT // 2
    positions = jnp.arange(row_count).astype(jnp.float32)
    freqs = 10000.0 ** (-(2.0 * jnp.arange(half_rot).astype(jnp.float32)) / ROT)
    angles = positions[:, None] * freqs[None, :]
    return (jnp.cos(angles)[:, None, :], jnp.sin(angles)[:, None, :])


def plain_rotate(field, cosines, sines):
    half_rot = ROT // 2
    first = field[..., :half_rot]
    second = field[..., half_rot:ROT]
    return jnp.concatenate(
        [first * cosines - second * sines, second * cosines + first * sines, field[..., ROT:]],
        axis=-1,
    )


def gelu_tanh(values):
    return jax.nn.gelu(values, approximate=True)


def causal_scores(query_block, key_rows, block_index):
    block_len = query_block.shape[0]
    query_pos = block_index * block_len + jnp.arange(block_len)
    key_pos = jnp.arange(key_rows.shape[0])
    raw = jnp.einsum("qhd,khd->hqk", query_block, key_rows, preferred_element_type=jnp.float32)
    scaled = raw * HEAD_DIM ** (-0.5)
    return jnp.where(key_pos[None, None, :] <= query_pos[None, :, None], scaled, big_negative)


def attend_forward(queries, key_rows, value_rows, block_len):
    row_count, heads_here, head_size = queries.shape
    n_blocks = row_count // block_len
    query_blocks = queries.reshape(n_blocks, block_len, heads_here, head_size)

    def one_block(item):
        query_block, block_index = item
        scores = causal_scores(query_block, key_rows, block_index)
        top_score = jnp.max(scores, axis=2, keepdims=True)
        exponent = jnp.exp(scores - top_score)
        totals = jnp.sum(exponent, axis=2, keepdims=True)
        probability = (exponent / totals).astype(jnp.bfloat16)
        attended = jnp.einsum(
            "hqk,khd->qhd", probability, value_rows, preferred_element_type=jnp.float32
        )
        return (attended, (top_score + jnp.log(totals))[:, :, 0])

    attended, logsum = lax.map(one_block, (query_blocks, jnp.arange(n_blocks)))
    return (attended.reshape(row_count, heads_here * head_size), logsum)


def attend_backward(queries, key_rows, value_rows, grad_att, logsum, block_len):
    row_count, heads_here, head_size = queries.shape
    n_blocks = row_count // block_len
    query_blocks = queries.reshape(n_blocks, block_len, heads_here, head_size)
    grad_blocks = grad_att.reshape(n_blocks, block_len, heads_here, head_size)
    scaling = HEAD_DIM ** (-0.5)

    def one_block(carry, item):
        grad_keys, grad_values = carry
        query_block, grad_block, lse_block, block_index = item
        scores = causal_scores(query_block, key_rows, block_index)
        probability = jnp.exp(scores - lse_block[:, :, None])
        grad_probs = jnp.einsum(
            "qhd,khd->hqk", grad_block, value_rows, preferred_element_type=jnp.float32
        )
        centre = jnp.sum(grad_probs * probability, axis=2, keepdims=True)
        grad_scores = (probability * (grad_probs - centre) * scaling).astype(jnp.bfloat16)
        grad_query = jnp.einsum(
            "hqk,khd->qhd", grad_scores, key_rows, preferred_element_type=jnp.float32
        )
        grad_keys = grad_keys + jnp.einsum(
            "hqk,qhd->khd", grad_scores, query_block, preferred_element_type=jnp.float32
        )
        grad_values = grad_values + jnp.einsum(
            "hqk,qhd->khd",
            probability.astype(jnp.bfloat16),
            grad_block,
            preferred_element_type=jnp.float32,
        )
        return ((grad_keys, grad_values), grad_query)

    zero_rows = jnp.zeros(key_rows.shape, jnp.float32)
    (grad_keys, grad_values), grad_queries = lax.scan(
        one_block, (zero_rows, zero_rows), (query_blocks, grad_blocks, logsum, jnp.arange(n_blocks))
    )
    return (grad_queries.reshape(row_count, heads_here, head_size), grad_keys, grad_values)


def plain_shards(tokens, ln_gain, ln_bias, w_qkv, b_qkv, w_out, w_up, b_up, w_down, out_bias, cotangent):
    activ = tokens.astype(jnp.float32)
    average = jnp.mean(activ, axis=1, keepdims=True)
    centered = activ - average
    variance = jnp.mean(centered * centered, axis=1, keepdims=True)
    inv_std = lax.rsqrt(variance + epsilon)
    x_hat = centered * inv_std
    normed = lax.all_gather(
        (x_hat * ln_gain + ln_bias).astype(jnp.bfloat16), "tensor", axis=0, tiled=True
    )
    row_count = normed.shape[0]
    block_len = min(row_count, 512)
    qkv_full, out_full, up_full, down_full = (
        lax.all_gather(w_qkv, "dp", axis=0, tiled=True),
        lax.all_gather(w_out, "dp", axis=1, tiled=True),
        lax.all_gather(w_up, "dp", axis=0, tiled=True),
        lax.all_gather(w_down, "dp", axis=1, tiled=True),
    )
    heads_here = w_qkv.shape[2] // HEAD_DIM
    local_width = heads_here * HEAD_DIM
    head_shape = (row_count, heads_here, HEAD_DIM)
    project = (
        jnp.einsum("td,dcf->tcf", normed, qkv_full, preferred_element_type=jnp.float32) + b_qkv
    )
    cosines, sines = plain_tables(row_count)
    queries = plain_rotate(project[:, 0].reshape(head_shape), cosines, sines).astype(jnp.bfloat16)
    key_rows = plain_rotate(project[:, 1].reshape(head_shape), cosines, sines).astype(jnp.bfloat16)
    value_rows = project[:, 2].reshape(head_shape).astype(jnp.bfloat16)
    attended, logsum = attend_forward(queries, key_rows, value_rows, block_len)
    attended = attended.astype(jnp.bfloat16)
    hidden = jnp.dot(normed, up_full, preferred_element_type=jnp.float32) + b_up
    activated = gelu_tanh(hidden).astype(jnp.bfloat16)
    partial_rows = jnp.dot(attended, out_full, preferred_element_type=jnp.float32) + jnp.dot(
        activated, down_full, preferred_element_type=jnp.float32
    )
    summed = lax.psum_scatter(partial_rows, "tensor", scatter_dimension=0, tiled=True)
    output = (activ + summed + out_bias).astype(jnp.bfloat16)
    grad_local = cotangent.astype(jnp.float32)
    grad_rows = lax.all_gather(cotangent, "tensor", axis=0, tiled=True)
    grad_down = jnp.einsum("tf,td->fd", activated, grad_rows, preferred_element_type=jnp.float32)
    grad_act = jnp.einsum("td,fd->tf", grad_rows, down_full, preferred_element_type=jnp.float32)
    gelu_pull = jax.vjp(gelu_tanh, hidden)[1]
    grad_hidden = gelu_pull(grad_act)[0].astype(jnp.bfloat16)
    grad_up = jnp.einsum("td,tf->df", normed, grad_hidden, preferred_element_type=jnp.float32)
    grad_b_up = jnp.sum(grad_hidden.astype(jnp.float32), axis=0)
    grad_normed = jnp.einsum("tf,df->td", grad_hidden, up_full, preferred_element_type=jnp.float32)
    grad_out = jnp.einsum("tf,td->fd", attended, grad_rows, preferred_element_type=jnp.float32)
    grad_att = jnp.einsum(
        "td,fd->tf", grad_rows, out_full, preferred_element_type=jnp.float32
    ).astype(jnp.bfloat16)
    grad_queries, grad_keys, grad_values = attend_backward(
        queries, key_rows, value_rows, grad_att.reshape(head_shape), logsum, block_len
    )
    grad_q_pre = plain_rotate(grad_queries, cosines, -sines).reshape(row_count, local_width)
    grad_k_pre = plain_rotate(grad_keys, cosines, -sines).reshape(row_count, local_width)
    grad_project = jnp.stack(
        [grad_q_pre, grad_k_pre, grad_values.reshape(row_count, local_width)], axis=1
    ).astype(jnp.bfloat16)
    grad_qkv = jnp.einsum("td,tcf->dcf", normed, grad_project, preferred_element_type=jnp.float32)
    grad_b_qkv = jnp.sum(grad_project.astype(jnp.float32), axis=0)
    grad_normed = grad_normed + jnp.einsum(
        "tcf,dcf->td", grad_project, qkv_full, preferred_element_type=jnp.float32
    )
    grad_ln_out = lax.psum_scatter(grad_normed, "tensor", scatter_dimension=0, tiled=True)
    qkv_summed, out_summed, up_summed, down_summed = (
        lax.psum_scatter(grad_qkv, "dp", scatter_dimension=0, tiled=True),
        lax.psum_scatter(grad_out, "dp", scatter_dimension=1, tiled=True),
        lax.psum_scatter(grad_up, "dp", scatter_dimension=0, tiled=True),
        lax.psum_scatter(grad_down, "dp", scatter_dimension=1, tiled=True),
    )
    scaled_grad = grad_ln_out * ln_gain
    grad_tokens = (
        inv_std
        * (
            scaled_grad
            - jnp.mean(scaled_grad, axis=1, keepdims=True)
            - x_hat * jnp.mean(scaled_grad * x_hat, axis=1, keepdims=True)
        )
        + grad_local
    )
    gain_grad, shift_grad, bias_grad = lax.psum(
        (
            jnp.sum(grad_ln_out * x_hat, axis=0),
            jnp.sum(grad_ln_out, axis=0),
            jnp.sum(grad_local, axis=0),
        ),
        ("dp", "tensor"),
    )
    qkv_bias_grad, up_bias_grad = lax.psum((grad_b_qkv, grad_b_up), "dp")
    return (
        output,
        grad_tokens,
        gain_grad,
        shift_grad,
        qkv_summed,
        qkv_bias_grad,
        out_summed,
        up_summed,
        up_bias_grad,
        down_summed,
        bias_grad,
    )


def solution(mesh):
    placed = (
        P(("dp", "tensor"), None),
        P(),
        P(),
        P("dp", None, "tensor"),
        P(None, "tensor"),
        P("tensor", "dp"),
        P("dp", "tensor"),
        P("tensor"),
        P("tensor", "dp"),
        P(),
        P(("dp", "tensor"), None),
    )
    results = (
        P(("dp", "tensor"), None),
        P(("dp", "tensor"), None),
        P(),
        P(),
        P("dp", None, "tensor"),
        P(None, "tensor"),
        P("tensor", "dp"),
        P("dp", "tensor"),
        P("tensor"),
        P("tensor", "dp"),
        P(),
    )
    one_kernel = mesh.shape["dp"] == 8 and mesh.shape["tensor"] == 4
    return jax.shard_map(
        fast_shards if one_kernel else plain_shards,
        mesh=mesh,
        in_specs=placed,
        out_specs=results,
        check_vma=False,
    )
```

```python
import functools
import math

import jax
import jax.numpy as jnp
import numpy as np
from jax import lax
from jax.experimental import pallas as pl
from jax.experimental.pallas import tpu as pltpu
from jax.sharding import PartitionSpec as P

HEAD_DIM = 64
ROT = 32
epsilon = 1e-05
big_negative = -1e30

f32 = jnp.float32
bf16 = jnp.bfloat16
NN = (((1,), (0,)), ((), ()))
NT = (((1,), (1,)), ((), ()))
TN = (((0,), (0,)), ((), ()))
dot = functools.partial(lax.dot_general, preferred_element_type=f32)

GELU_A = math.sqrt(2.0 / math.pi)
GELU_B = 0.044715
CHUNK = 512
Q_BLOCK = 128
LANES = 128


def gelu_both(h):
    square = h * h
    t = jnp.tanh(h * (GELU_A + (GELU_A * GELU_B) * square))
    half = 0.5 * (1.0 + t)
    slope = half + (0.5 * h) * (1.0 - t * t) * (GELU_A + (3.0 * GELU_A * GELU_B) * square)
    return h * half, slope


def rotary_tables(row_count):
    half_rot = ROT // 2
    positions = np.arange(row_count, dtype=np.float32)
    freqs = np.float32(10000.0) ** (-(2.0 * np.arange(half_rot, dtype=np.float32)) / np.float32(ROT))
    angles = positions[:, None] * freqs.astype(np.float32)[None, :]
    cosines, sines = np.cos(angles), np.sin(angles)
    rest = np.zeros((row_count, HEAD_DIM - ROT), np.float32)
    c_head = np.concatenate([cosines, cosines, rest + 1.0], axis=1)
    s_head = np.concatenate([-sines, sines, rest], axis=1)
    pair = lambda t: np.concatenate([t, t], axis=1).astype(np.float32)
    return pair(c_head), pair(s_head)


def rotate(field, cosines, sines):
    half = ROT // 2
    lane = lax.broadcasted_iota(jnp.int32, field.shape, 1)
    first = lax.rem(lane, HEAD_DIM) < half
    partner = jnp.where(
        first, pltpu.roll(field, LANES - half, 1), pltpu.roll(field, half, 1)
    )
    return field * cosines + partner * sines


ORDER = (
    "s:Glo", "s:Oa", "s:Gc", "s:Qc", "s:Od", "s:Oe", "ln", "s:Qd", "s:U0d", "s:Gx", "r:Of",
    "r:Gcx", "s:U0e", "s:Nx", "s:Nc", "s:Nlo", "r:Qg", "r:Oh", "r:Gxlo", "s:D0d", "s:U0c",
    "r:U0h", "r:U0g", "s:U0a", "r:Gcxlo", "r:Nxlo", "s:Oc", "r:Og", "s:Qe", "r:U0f", "r:Ncx",
    "s:Qa", "r:Ncxlo", "r:Qh", "s:D0c", "hid00", "r:Qf", "hid01", "near:D031", "near:D030",
    "s:D0a", "proj0", "s:D0e", "att00", "r:D0g", "att01", "proj1", "r:D0h", "far:D00", "r:D0f",
    "att10", "att11", "far:D01", "near:A11", "core:o11", "dh00", "near:A31", "cross:o1", "swap:A",
    "dh01", "near:U011", "far:A1", "core:n10", "core:n11", "near:A30", "core:n00", "swap:U0",
    "core:o10", "core:o01", "near:U010", "far:A0", "core:o00", "cross:n1", "core:n01", "level:o",
    "near:A10", "near:U030", "cross:o0", "near:U031", "level:n", "fin:U0", "cross:n0",
    "near:D010", "far:U00", "near:D011", "far:U01", "own:o", "fin:A", "swap:D0", "fin:D0",
    "own:n", "small",
)


def block_kernel(
    tokens, cot, gain, shift, out_bias, wq_in, wo_in, wu_in, wd_in, bq_in, bu_in, cos_t, sin_t,
    o_out, o_gt, o_vec, o_part, ry, rm, rl, rc, rx, rr_lo,
    XN, G, WU, WD, WQ, WO, ACT, DH, ATT, DP, YS, FF, RING, LD, VEC, SV, SS, SR,
    ssem, rsem, lsem,
):
    T, D = tokens.shape
    R = wu_in.shape[0]
    F = wu_in.shape[1] // 2
    H = wo_in.shape[0] // 2
    ROWS = 8 * T
    LEN = 4 * T
    half_d = D // 2
    LN_ROWS = min(T, 64)

    dp = lax.axis_index("dp")
    tp = lax.axis_index("tensor")
    hi = lax.div(dp, 4)
    lo = lax.rem(lax.div(dp, 2), 2)
    y = lax.rem(dp, 2)
    x = lax.div(tp, 2)
    c = lax.rem(tp, 2)

    def device(hi_=hi, lo_=lo, y_=y, x_=x, c_=c):
        return {"dp": (hi_ * 2 + lo_) * 2 + y_, "tensor": x_ * 2 + c_}

    to_x = device(x_=1 - x)
    to_c = device(c_=1 - c)
    to_lo = device(lo_=1 - lo)
    to_y = device(y_=1 - y)
    to_hi = device(hi_=1 - hi)
    to_hilo = device(hi_=1 - hi, lo_=1 - lo)
    partners = [to_x, to_c, to_lo, to_y, to_hi, to_hilo]

    mult = pl.multiple_of

    n_copies = [0]
    n_local = [0]
    pending = []

    class Send:
        def __init__(self, src, dst, dev):
            i = n_copies[0]
            n_copies[0] += 1
            self.d = pltpu.make_async_remote_copy(
                src_ref=src, dst_ref=dst, send_sem=ssem.at[i], recv_sem=rsem.at[i],
                device_id=dev, device_id_type=pl.DeviceIdType.MESH,
            )
            self.open = False
            self.arrived = False

        def start(self):
            self.d.start()
            self.open = True
            pending.append(self)

        def got(self):
            if not self.arrived:
                self.d.wait_recv()
            self.arrived = True

        def done(self):
            if self.open:
                self.d.wait_send()
            self.open = False

    class Local:
        def __init__(self, src, dst):
            i = n_local[0]
            n_local[0] += 1
            self.d = pltpu.make_async_copy(src, dst, lsem.at[i])
            self.d.start()
            self.open = True

        def done(self):
            if self.open:
                self.d.wait()
            self.open = False

    sends = {}

    def got(*names):
        for n in names:
            sends[n].got()

    def start(*names):
        for n in names:
            sends[n].start()

    steps = {}

    def col(p, low):
        return mult(p * 2 * R + low * R, R)

    def abs_block(p, low):
        hi_ = hi if p < 2 else 1 - hi
        y_ = y if p % 2 == 0 else 1 - y
        return mult(((hi_ * 2 + low) * 2 + y_) * R, R)

    pieces = [(p, low) for p in range(4) for low in range(2)]

    def piece_cols(p, low):
        return slice(p * 2 * R + low * R, p * 2 * R + (low + 1) * R)

    def piece_ds(p, low):
        return pl.ds(p * 2 * R + low * R, R)

    def row(low, xx, cc):
        return mult((low * 4 + xx * 2 + cc) * T, T)

    own_row = row(lo, x, c)
    own_rows = pl.ds(own_row, T)

    tok_loads, cot_loads = [], []
    for p, low in pieces:
        src = pl.ds(abs_block(p, low), R)
        tok_loads.append(Local(tokens.at[:, src], RING.at[0, :, piece_ds(p, low)]))
    for p, low in pieces:
        src = pl.ds(abs_block(p, low), R)
        cot_loads.append(Local(cot.at[:, src], G.at[own_rows, piece_ds(p, low)]))

    own_weights = {}

    def weight(w, src, land):
        own_weights[w] = Local(src(lo), land(0, lo))
        sends[w + "a"] = Send(src(1 - lo), land(0, lo), to_lo)
        sends[w + "c"] = Send(src(lo), land(2, lo), to_hi)
        sends[w + "e"] = Send(src(1 - lo), land(2, lo), to_hilo)
        sends[w + "d"] = Send(src(lo), land(1, lo), to_y)
        sends[w + "f"] = Send(land(0, 1 - lo), land(1, 1 - lo), to_y)
        sends[w + "g"] = Send(land(2, lo), land(3, lo), to_y)
        sends[w + "h"] = Send(land(2, 1 - lo), land(3, 1 - lo), to_y)
        for n in "aced":
            steps["s:" + w + n] = functools.partial(start, w + n)
        for n, before in (("f", "a"), ("g", "c"), ("h", "e")):
            steps["r:" + w + n] = functools.partial(relay, w + before, w + n)

    def relay(before, *after):
        got(before)
        start(*after)

    def weight_ready(*ws):
        for w in ws:
            own_weights[w].done()
            got(w + "d", w + "f", w + "g", w + "h")

    weight(
        "U0",
        lambda h: wu_in.at[:, pl.ds(mult(h * F, F), F)],
        lambda p, low: WU.at[pl.ds(col(p, low), R), :],
    )
    weight(
        "Q",
        lambda h: wq_in.at[:, :, pl.ds(mult(h * H, H), H)],
        lambda p, low: WQ.at[:, pl.ds(col(p, low), R), :],
    )
    weight(
        "O",
        lambda h: wo_in.at[pl.ds(mult(h * H, H), H), :],
        lambda p, low: WO.at[:, pl.ds(col(p, low), R)],
    )
    weight(
        "D0",
        lambda h: wd_in.at[pl.ds(mult(h * F, F), F), :],
        lambda p, low: WD.at[:, pl.ds(col(p, low), R)],
    )

    def rows_over(r, buf):
        def at(low, xx):
            return buf.at[pl.ds(row(low, xx, c), T), :]

        sends[r + "lo"] = Send(at(lo, x), at(lo, x), to_lo)
        sends[r + "x"] = Send(at(lo, x), at(lo, x), to_x)
        sends[r + "xlo"] = Send(at(1 - lo, x), at(1 - lo, x), to_x)
        sends[r + "c"] = Send(at(lo, x), at(lo, x), to_c)
        sends[r + "clo"] = Send(at(1 - lo, x), at(1 - lo, x), to_c)
        sends[r + "cx"] = Send(at(lo, 1 - x), at(lo, 1 - x), to_c)
        sends[r + "cxlo"] = Send(at(1 - lo, 1 - x), at(1 - lo, 1 - x), to_c)
        steps["r:" + r + "xlo"] = functools.partial(relay, r + "lo", r + "xlo", r + "clo")
        steps["r:" + r + "cx"] = functools.partial(relay, r + "x", r + "cx")
        steps["r:" + r + "cxlo"] = functools.partial(relay, r + "xlo", r + "cxlo")

    rows_over("N", XN)
    rows_over("G", G)

    def rows_ready(*rs):
        for r in rs:
            got(r + "c", r + "clo", r + "cx", r + "cxlo")

    def start_g(n):
        for ld in cot_loads:
            ld.done()
        start("G" + n)

    for n in ("lo", "x", "c"):
        steps["s:N" + n] = functools.partial(start, "N" + n)
        steps["s:G" + n] = functools.partial(start_g, n)

    def normalise(k, sub):
        activ = RING[k, sub, :].astype(f32)
        average = jnp.mean(activ, axis=1, keepdims=True)
        centered = activ - average
        variance = jnp.mean(centered * centered, axis=1, keepdims=True)
        inv_std = lax.rsqrt(variance + epsilon)
        return centered * inv_std, inv_std

    def sub_rows(i):
        return pl.ds(mult(i * LN_ROWS, LN_ROWS), LN_ROWS)

    def step_ln():
        for p, low in pieces:
            src = pl.ds(abs_block(p, low), R)
            VEC[0:1, piece_ds(p, low)] = gain[:, src]
            VEC[1:2, piece_ds(p, low)] = shift[:, src]
            VEC[2:3, piece_ds(p, low)] = out_bias[:, src]
        for ld in tok_loads:
            ld.done()

        def body(i, _):
            x_hat, _unused = normalise(0, sub_rows(i))
            XN[pl.ds(mult(own_row + i * LN_ROWS, LN_ROWS), LN_ROWS), :] = (
                x_hat * VEC[0:1, :] + VEC[1:2, :]
            ).astype(bf16)

        lax.fori_loop(0, T // LN_ROWS, body, None)

    steps["ln"] = step_ln

    def tiles(first, stop, body):
        lax.fori_loop(first, stop, lambda i, _: body(pl.ds(mult(i * T, T), T)), None)

    def step_hid(first, stop):
        weight_ready("U0")
        rows_ready("N")

        def body(rows):
            xn = XN[rows, :]
            for m in range(0, F, R):
                cols = slice(m, m + R)
                bias = bu_in[:, pl.ds(mult(lo * F + m, R), R)]
                h = dot(xn, WU[:, cols], NN) + bias
                act, slope = gelu_both(h)
                ACT[rows, cols] = act.astype(bf16)
                DH[rows, cols] = slope.astype(bf16)

        tiles(first, stop, body)

    steps["hid00"] = functools.partial(step_hid, 0, 4)
    steps["hid01"] = functools.partial(step_hid, 4, 8)

    def step_dh(first, stop):
        weight_ready("D0")
        rows_ready("G")
        if first == 0:
            VEC[3:4, 0:F] = jnp.zeros((1, F), f32)

        def body(rows):
            gg = G[rows, :]
            for m in range(0, F, R):
                cols = slice(m, m + R)
                dh = (dot(gg, WD[cols, :], NT) * DH[rows, cols].astype(f32)).astype(bf16)
                DH[rows, cols] = dh
                VEC[3:4, cols] += jnp.sum(dh.astype(f32), axis=0, keepdims=True)

        tiles(first, stop, body)

    steps["dh00"] = functools.partial(step_dh, 0, 4)
    steps["dh01"] = functools.partial(step_dh, 4, 8)

    Q, K, V, DA = range(4)

    def seq_row(s, off):
        return mult((1 - lo if s == 0 else lo) * LEN + off, Q_BLOCK)

    def head_rows(which, begin, size, cc):
        parts = []
        at = begin
        while at < begin + size:
            stop = min((at // T + 1) * T, begin + size)
            cols = pl.ds(mult(at // T * H + cc, LANES), LANES)
            parts.append(YS[1, which, at % T : at % T + stop - at, cols])
            at = stop
        return parts[0] if len(parts) == 1 else jnp.concatenate(parts, axis=0)

    def step_proj(s):
        weight_ready("Q", "O")
        rows_ready("N", "G")

        def body(i, _):
            pos = pl.ds(mult(i * T, T), T)
            rows = pl.ds(mult(seq_row(s, 0) + i * T, T), T)
            cs, sn = cos_t[pos, :], sin_t[pos, :]

            def put(which, v, turn):
                for a in range(0, H, LANES):
                    u = v[:, a : a + LANES]
                    if turn:
                        u = rotate(u, cs, sn)
                    cols = pl.ds(mult(i * H + a, LANES), LANES)
                    YS[1, which, :, cols] = u.astype(bf16)

            xn = XN[rows, :]
            for k, which in enumerate((Q, K, V)):
                bias = bq_in[k : k + 1, pl.ds(mult(lo * H, LANES), H)]
                put(which, dot(xn, WQ[k], NN) + bias, k < 2)
            put(DA, dot(G[rows, :], WO[...], NT), False)

        lax.fori_loop(0, 4, body, None)

    def step_att(s, first_pair, n_pairs):
        first = lax.broadcasted_iota(jnp.int32, (Q_BLOCK, LANES), 1) < HEAD_DIM
        scaling = HEAD_DIM**-0.5

        def split(v):
            zero = jnp.zeros_like(v)
            return jnp.concatenate([jnp.where(first, v, zero), jnp.where(first, zero, v)], axis=0)

        def join(v):
            return jnp.where(first, v[:Q_BLOCK], v[Q_BLOCK:])

        def place(j):
            at = j * Q_BLOCK
            return pl.ds(at % T, Q_BLOCK), pl.ds(at // T * LANES, LANES)

        def pair(hp, _):
            cc = hp * LANES
            out_cols = pl.ds(mult(cc, LANES), LANES)
            for i in range(LEN // Q_BLOCK):
                rr = pl.ds(i * Q_BLOCK, Q_BLOCK)
                out_rows = pl.ds(seq_row(s, i * Q_BLOCK), Q_BLOCK)
                n = (i + 1) * Q_BLOCK
                old = n - Q_BLOCK
                qm = split(head_rows(Q, old, Q_BLOCK, cc))
                dm = split(head_rows(DA, old, Q_BLOCK, cc))
                kk = head_rows(K, 0, n, cc)
                vv = head_rows(V, 0, n, cc)
                st = dot(kk, qm * jnp.asarray(scaling, bf16), NT)
                kpos = lax.broadcasted_iota(jnp.int32, (Q_BLOCK, 2 * Q_BLOCK), 0)
                qpos = lax.broadcasted_iota(jnp.int32, (Q_BLOCK, 2 * Q_BLOCK), 1)
                qpos = jnp.where(qpos < Q_BLOCK, qpos, qpos - Q_BLOCK)
                diagonal = jnp.where(kpos <= qpos, st[old:], big_negative)
                st = diagonal if i == 0 else jnp.concatenate([st[:old], diagonal], axis=0)
                ex = jnp.exp(st - jnp.max(st, axis=0, keepdims=True))
                prob = ex * (1.0 / jnp.sum(ex, axis=0, keepdims=True))
                pb = prob.astype(bf16)
                ATT[out_rows, out_cols] = join(dot(pb, vv, TN)).astype(bf16)
                dv = dot(pb, dm, NN)
                dprob = dot(vv, dm, NT)
                centre = jnp.sum(dprob * prob, axis=0, keepdims=True)
                ds = (prob * (dprob - centre) * scaling).astype(bf16)
                dq = join(dot(ds, kk, TN))
                DP[out_rows, out_cols] = rotate(dq, cos_t[rr, :], -sin_t[rr, :]).astype(bf16)
                dk = dot(ds, qm, NN)
                for j in range(i + 1):
                    pr, pc = place(j)
                    part = slice(j * Q_BLOCK, (j + 1) * Q_BLOCK)
                    if j < i:
                        FF[0, pr, pc] += dk[part]
                        FF[1, pr, pc] += dv[part]
                    else:
                        FF[0, pr, pc] = dk[part]
                        FF[1, pr, pc] = dv[part]
            for j in range(LEN // Q_BLOCK):
                pr, pc = place(j)
                rr = pl.ds(j * Q_BLOCK, Q_BLOCK)
                out_rows = pl.ds(seq_row(s, j * Q_BLOCK), Q_BLOCK)
                DP[out_rows, pl.ds(mult(H + cc, LANES), LANES)] = rotate(
                    FF[0, pr, pc], cos_t[rr, :], -sin_t[rr, :]
                ).astype(bf16)
                DP[out_rows, pl.ds(mult(2 * H + cc, LANES), LANES)] = FF[1, pr, pc].astype(bf16)

        lax.fori_loop(first_pair, first_pair + n_pairs, pair, None)

    half_pairs = H // LANES // 2
    for s in range(2):
        steps["proj%d" % s] = functools.partial(step_proj, s)
        if half_pairs:
            steps["att%d0" % s] = functools.partial(step_att, s, 0, half_pairs)
            steps["att%d1" % s] = functools.partial(step_att, s, half_pairs, half_pairs)
            steps["att%d" % s] = functools.partial(step_att, s, 0, 2 * half_pairs)
        else:
            steps["att%d0" % s] = functools.partial(step_att, s, 0, 1)
            steps["att%d1" % s] = lambda: None
            steps["att%d" % s] = steps["att%d0" % s]

    ff_use = {0: [], 1: []}

    def ff_free(*which):
        for k in which:
            for ld in ff_use[k]:
                ld.done()
            ff_use[k] = []

    def cols_of(p, q):
        return pl.ds(col(p, lo if q == 0 else 1 - lo), R)

    def block_dn(p, q):
        gg = G[:, cols_of(p, q)]
        return [(m, dot(ACT[:, m : m + R], gg, TN)) for m in range(0, F, R)]

    def block_up(p, q):
        return [(0, dot(XN[:, cols_of(p, q)], DH[...], TN))]

    def block_at(p, q):
        cc = cols_of(p, q)
        return [(0, dot(XN[:, cc], DP[...], TN)), (3 * H, dot(ATT[...], G[:, cc], TN))]

    def weight_grad(g, i, block, needs):
        def slot(p, q):
            return (0 if p >= 2 else 2) + (1 - q)

        def pq(p, q):
            return "%d%d" % (p, q)

        for p, q in ((3, 1), (3, 0), (1, 1), (1, 0)):
            k = slot(p, q)
            sends["y" + g + pq(p, q)] = Send(YS.at[i, k], ry.at[i, k], to_y)
        sends["m" + g + "0"] = Send(YS.at[i, slot(3, 0)], rm.at[i, 0], to_hi)
        sends["m" + g + "1"] = Send(YS.at[i, slot(3, 1)], rm.at[i, 1], to_hilo)
        sends["l" + g] = Send(YS.at[i, slot(1, 1)], rl.at[i], to_lo)

        def near(p, q):
            needs()
            k = slot(p, q)
            for off, v in block(p, q):
                YS[i, k, :, off : off + v.shape[1]] = v.astype(bf16)
            start("y" + g + pq(p, q))

        def pass_on(p, q, then):
            k = slot(p, q)
            came = "y" + g + pq(p + 1, q)
            got(came)
            load = Local(ry.at[i, k], LD.at[0, 0:R, 0:F])
            vals = block(p, q)
            sends[came].done()
            load.done()
            for off, v in vals:
                cols = slice(off, off + v.shape[1])
                YS[i, k, :, cols] = (v + LD[0, 0:R, cols].astype(f32)).astype(bf16)
            start(then)

        def fin():
            ff_free(0)
            got("y" + g + "10")
            load = Local(ry.at[i, slot(0, 0)], LD.at[0, 0:R, 0:F])
            vals = block(0, 0)
            load.done()
            for off, v in vals:
                cols = slice(off, off + v.shape[1])
                FF[0, :, cols] = v + LD[0, 0:R, cols].astype(f32)
            ff_use[0] = [Local(FF.at[0], o_part.at[i])]

        for p, q in ((3, 1), (3, 0), (1, 1), (1, 0)):
            steps["near:" + g + pq(p, q)] = functools.partial(near, p, q)
        for q in range(2):
            steps["far:" + g + str(q)] = functools.partial(pass_on, 2, q, "m" + g + str(q))
        steps["swap:" + g] = functools.partial(pass_on, 0, 1, "l" + g)
        steps["fin:" + g] = fin

    weight_grad("D0", 0, block_dn, lambda: rows_ready("G"))
    weight_grad("A", 1, block_at, lambda: None)
    weight_grad("U0", 2, block_up, lambda: None)

    def rows_out(rr, cc):
        return dot(ACT[rr, :], WD[:, cc], NN) + dot(ATT[rr, :], WO[:, cc], NN)

    def rows_dn(rr, cc):
        v = dot(DH[rr, :], WU[cc, :], NT)
        for k in range(3):
            v = v + dot(DP[rr, k * H : (k + 1) * H], WQ[k, cc, :], NT)
        return v

    ring_use = {0: None, 1: None, 2: None}
    ring_next = [0]

    def ring_slot():
        k = ring_next[0]
        ring_next[0] = (k + 1) % 3
        if ring_use[k] is not None:
            ring_use[k].done()
            ring_use[k] = None
        return k

    def load_tokens():
        k = ring_slot()
        return k, [
            Local(tokens.at[:, pl.ds(abs_block(p, low), R)], RING.at[k, :, piece_ds(p, low)])
            for p, low in pieces
        ]

    def own_sub(sub):
        return jnp.concatenate([FF[0, sub, :], FF[1, sub, :]], axis=1) + LD[0, sub, :].astype(f32)

    def finish_out(k_tok):
        k = ring_slot()

        def body(i, _):
            sub = sub_rows(i)
            RING[k, sub, :] = (
                RING[k_tok, sub, :].astype(f32) + own_sub(sub) + VEC[2:3, :]
            ).astype(bf16)

        lax.fori_loop(0, T // LN_ROWS, body, None)
        stores = [
            Local(RING.at[k, :, piece_ds(p, low)], o_out.at[:, pl.ds(abs_block(p, low), R)])
            for p, low in pieces
        ]
        for st in stores:
            st.done()

    def finish_dn(k_tok):
        VEC[4:6, :] = jnp.zeros((2, D), f32)

        def body(i, _):
            sub = sub_rows(i)
            x_hat, inv_std = normalise(k_tok, sub)
            dn = own_sub(sub)
            VEC[4:5, :] += jnp.sum(dn * x_hat, axis=0, keepdims=True)
            VEC[5:6, :] += jnp.sum(dn, axis=0, keepdims=True)
            scaled = dn * VEC[0:1, :]
            gt = (
                inv_std
                * (
                    scaled
                    - jnp.mean(scaled, axis=1, keepdims=True)
                    - x_hat * jnp.mean(scaled * x_hat, axis=1, keepdims=True)
                )
                + G[pl.ds(mult(own_row + i * LN_ROWS, LN_ROWS), LN_ROWS), :].astype(f32)
            )
            FF[0, sub, :] = gt[:, :half_d]
            FF[1, sub, :] = gt[:, half_d:]

        lax.fori_loop(0, T // LN_ROWS, body, None)
        for p, low in pieces:
            dst = pl.ds(abs_block(p, low), R)
            src = pl.ds((p % 2) * 2 * R + low * R, R)
            ff_use[p // 2].append(Local(FF.at[p // 2, :, src], o_gt.at[:, dst]))

    def owners(w, i, partial, needs, finish):
        def chunks(low, xx, cc, loads, store):
            rr = pl.ds(row(low, xx, cc), T)
            for ld in loads:
                ld.done()

            def body(j, _):
                cols = pl.ds(mult(j * CHUNK, CHUNK), CHUNK)
                v = partial(rr, cols)
                for k in range(len(loads)):
                    v = v + LD[k, :, cols].astype(f32)
                store(j, cols, v)

            lax.fori_loop(0, D // CHUNK, body, None)

        def put(name, low, xx, cc, srcs, dst, dev):
            needs()
            loads = [Local(src, LD.at[k]) for k, src in enumerate(srcs)]
            k = ring_slot()

            def store(j, cols, v):
                RING[k, :, cols] = v.astype(bf16)

            chunks(low, xx, cc, loads, store)
            sends[name] = Send(RING.at[k], dst, dev)
            start(name)
            ring_use[k] = sends[name]

        def core(dlo, dx):
            low = lo if dlo == 0 else 1 - lo
            xx = x if dx == 0 else 1 - x
            name = "c%s%d%d" % (w, dlo, dx)
            put(name, low, xx, 1 - c, [], rc.at[i, 2 * dlo + dx], to_c)

        def cross(dlo):
            low = lo if dlo == 0 else 1 - lo
            got("c%s%d1" % (w, dlo))
            name = "x%s%d" % (w, dlo)
            put(name, low, 1 - x, c, [rc.at[i, 2 * dlo + 1]], rx.at[i, dlo], to_x)

        def level():
            got("c%s10" % w, "x%s1" % w)
            put("l" + w, 1 - lo, x, c, [rc.at[i, 2], rx.at[i, 1]], rr_lo.at[i], to_lo)

        def own():
            k_tok, tok_ld = load_tokens()
            got("c%s00" % w, "x%s0" % w)
            loads = [Local(rc.at[i, 0], LD.at[0]), Local(rx.at[i, 0], LD.at[1])]
            ff_free(0, 1)
            n = D // CHUNK // 2

            def store(j, cols, v):
                part = pl.ds(mult(lax.rem(j, n) * CHUNK, CHUNK), CHUNK)
                FF[lax.div(j, n), :, part] = v

            chunks(lo, x, c, loads, store)
            got("l" + w)
            Local(rr_lo.at[i], LD.at[0]).done()
            for ld in tok_ld:
                ld.done()
            finish(k_tok)

        for dlo in range(2):
            for dx in range(2):
                steps["core:%s%d%d" % (w, dlo, dx)] = functools.partial(core, dlo, dx)
            steps["cross:%s%d" % (w, dlo)] = functools.partial(cross, dlo)
        steps["level:" + w] = level
        steps["own:" + w] = own

    owners("o", 0, rows_out, lambda: weight_ready("D0"), finish_out)
    owners("n", 1, rows_dn, lambda: None, finish_dn)

    def step_small():
        SV[...] = jnp.zeros_like(SV)
        VEC[6:7, 0 : 3 * H] = jnp.zeros((1, 3 * H), f32)
        VEC[7:8, :] = jnp.zeros((1, D), f32)

        def body(rows):
            VEC[6:7, 0 : 3 * H] += jnp.sum(DP[rows, :].astype(f32), axis=0, keepdims=True)

        tiles(0, ROWS // T, body)

        def g_body(i, _):
            rows = pl.ds(mult(own_row + i * LN_ROWS, LN_ROWS), LN_ROWS)
            VEC[7:8, :] += jnp.sum(G[rows, :].astype(f32), axis=0, keepdims=True)

        lax.fori_loop(0, T // LN_ROWS, g_body, None)
        for p, low in pieces:
            dst = pl.ds(abs_block(p, low), R)
            SV[0:2, dst] = VEC[4:6, piece_cols(p, low)]
            SV[2:3, dst] = VEC[7:8, piece_cols(p, low)]
        SV[3:4, pl.ds(mult(lo * F, F), F)] = VEC[3:4, 0:F]
        for k in range(3):
            SV[4 + k : 5 + k, pl.ds(mult(lo * H, LANES), H)] = VEC[6:7, k * H : (k + 1) * H]
        for k, dev in enumerate((to_y, to_hi, to_lo, to_x, to_c)):
            SS[k, :, :] = SV[...]
            s = Send(SS.at[k], SR.at[k], dev)
            s.start()
            s.got()
            if k < 3:
                SV[...] += SR[k]
            else:
                SV[0:3, :] += SR[k, 0:3, :]
        o_vec[...] = SV[...]

    steps["small"] = step_small

    barrier = pltpu.get_barrier_semaphore()
    for dev in partners:
        pl.semaphore_signal(barrier, inc=1, device_id=dev, device_id_type=pl.DeviceIdType.MESH)
    pl.semaphore_wait(barrier, len(partners))
    for name in ORDER:
        steps[name]()
    ff_free(0, 1)
    for s in pending:
        s.got()
        s.done()
    assert n_copies[0] <= ssem.shape[0] and n_local[0] <= lsem.shape[0], (n_copies, n_local)


def finish_kernel(
    b_out, b_gt, b_vec, b_part, rm, rl,
    o_out, o_gt, o_gain, o_shift, o_bias, o_bu, o_bq, o_gq, o_go, o_gu, o_gd,
    PART, RM, RL, OUT, GT, GU, GD, GQ, GO, lsem,
):
    R, F = PART.shape[1:]
    H = o_go.shape[0] // 2
    lo = lax.rem(lax.div(lax.axis_index("dp"), 2), 2)
    mult = pl.multiple_of
    n = [0]

    def copy(src, dst):
        d = pltpu.make_async_copy(src, dst, lsem.at[n[0]])
        n[0] += 1
        d.start()
        return d

    order = (1, 0, 2)
    loads = {i: [copy(b_part.at[i], PART.at[i]), copy(rm.at[i], RM.at[i]), copy(rl.at[i], RL.at[i])] for i in order}
    load_out = copy(b_out, OUT)
    load_gt = copy(b_gt, GT)
    o_gain[...] = b_vec[0:1, :]
    o_shift[...] = b_vec[1:2, :]
    o_bias[...] = b_vec[2:3, :]
    o_bu[...] = b_vec[3:4, 0 : 2 * F]
    o_bq[...] = b_vec[4:7, 0 : 2 * H]
    stores = []

    def halves(i, put):
        for ld in loads[i]:
            ld.wait()
        for m in range(0, F, R):
            cols = slice(m, m + R)
            put(lo, m, PART[i, :, cols] + RM[i, 0, :, cols].astype(f32))
            put(1 - lo, m, RL[i, :, cols].astype(f32) + RM[i, 1, :, cols].astype(f32))

    def put_at(half, m, v):
        if m < 3 * H:
            GQ[m // H, :, pl.ds(mult(half * H, H), H)] = v
        else:
            GO[pl.ds(mult(half * H, H), H), :] = v

    def put_dn(half, m, v):
        GD[pl.ds(mult(half * F + m, R), R), :] = v

    def put_up(half, m, v):
        GU[:, pl.ds(mult(half * F + m, R), R)] = v

    for i, put, pairs in (
        (1, put_at, ((GQ, o_gq), (GO, o_go))), (0, put_dn, ((GD, o_gd),)), (2, put_up, ((GU, o_gu),)),
    ):
        halves(i, put)
        for src, dst in pairs:
            stores.append(copy(src, dst))
    load_out.wait()
    stores.append(copy(OUT, o_out))
    load_gt.wait()
    stores.append(copy(GT, o_gt))
    for st in stores:
        st.wait()


VMEM_LIMIT = 64 << 20


def fast_shards(tokens, ln_gain, ln_bias, w_qkv, b_qkv, w_out, w_up, b_up, w_down, out_bias, cot):
    T, D = tokens.shape
    R, F = w_up.shape[0], w_up.shape[1] // 2
    H = w_out.shape[0] // 2
    cos_t, sin_t = rotary_tables(4 * T)
    S = jax.ShapeDtypeStruct
    hbm = pl.BlockSpec(memory_space=pl.ANY)
    vm = pl.BlockSpec(memory_space=pltpu.VMEM)
    outs = pl.pallas_call(
        block_kernel,
        out_shape=(
            S((T, D), bf16), S((T, D), f32), S((8, D), f32), S((3, R, F), f32),
            S((3, 4, R, F), bf16), S((3, 2, R, F), bf16), S((3, R, F), bf16),
            S((2, 4, T, D), bf16), S((2, 2, T, D), bf16), S((2, T, D), bf16),
        ),
        in_specs=[hbm, hbm, vm, vm, vm, hbm, hbm, hbm, hbm, vm, vm, vm, vm],
        out_specs=(hbm, hbm, vm) + (hbm,) * 7,
        scratch_shapes=[
            pltpu.VMEM((8 * T, D), bf16),
            pltpu.VMEM((8 * T, D), bf16),
            pltpu.VMEM((D, F), bf16),
            pltpu.VMEM((F, D), bf16),
            pltpu.VMEM((3, D, H), bf16),
            pltpu.VMEM((H, D), bf16),
            pltpu.VMEM((8 * T, F), bf16),
            pltpu.VMEM((8 * T, F), bf16),
            pltpu.VMEM((8 * T, H), bf16),
            pltpu.VMEM((8 * T, 3 * H), bf16),
            pltpu.VMEM((3, 4, R, F), bf16),
            pltpu.VMEM((2, R, F), f32),
            pltpu.VMEM((3, T, D), bf16),
            pltpu.VMEM((2, T, D), bf16),
            pltpu.VMEM((8, D), f32),
            pltpu.VMEM((8, D), f32),
            pltpu.VMEM((5, 8, D), f32),
            pltpu.VMEM((5, 8, D), f32),
            pltpu.SemaphoreType.DMA((90,)),
            pltpu.SemaphoreType.DMA((90,)),
            pltpu.SemaphoreType.DMA((110,)),
        ],
        compiler_params=pltpu.CompilerParams(
            collective_id=0, has_side_effects=True, vmem_limit_bytes=VMEM_LIMIT
        ),
        name="parallel_block",
    )(
        tokens, cot, ln_gain.reshape(1, D), ln_bias.reshape(1, D), out_bias.reshape(1, D),
        w_qkv.transpose(1, 0, 2), w_out, w_up, w_down, b_qkv, b_up.reshape(1, 2 * F), cos_t, sin_t,
    )
    b_out, b_gt, b_vec, b_part, _, rm, rl = outs[:7]
    done = pl.pallas_call(
        finish_kernel,
        out_shape=(
            S((T, D), bf16), S((T, D), f32), S((1, D), f32), S((1, D), f32), S((1, D), f32),
            S((1, 2 * F), f32), S((3, 2 * H), f32),
            S((3, R, 2 * H), f32), S((2 * H, R), f32), S((R, 2 * F), f32), S((2 * F, R), f32),
        ),
        in_specs=[hbm, hbm, vm, hbm, hbm, hbm],
        out_specs=(hbm, hbm) + (vm,) * 5 + (hbm,) * 4,
        scratch_shapes=[
            pltpu.VMEM((3, R, F), f32),
            pltpu.VMEM((3, 2, R, F), bf16),
            pltpu.VMEM((3, R, F), bf16),
            pltpu.VMEM((T, D), bf16),
            pltpu.VMEM((T, D), f32),
            pltpu.VMEM((R, 2 * F), f32),
            pltpu.VMEM((2 * F, R), f32),
            pltpu.VMEM((3, R, 2 * H), f32),
            pltpu.VMEM((2 * H, R), f32),
            pltpu.SemaphoreType.DMA((20,)),
        ],
        compiler_params=pltpu.CompilerParams(vmem_limit_bytes=VMEM_LIMIT),
        name="finish",
    )(b_out, b_gt, b_vec, b_part, rm, rl)
    o_out, o_gt, o_gain, o_shift, o_bias, o_bu, o_bq, o_gq, o_go, o_gu, o_gd = done
    return (
        o_out, o_gt, o_gain.reshape(D), o_shift.reshape(D), o_gq.transpose(1, 0, 2), o_bq, o_go,
        o_gu, o_bu.reshape(2 * F), o_gd, o_bias.reshape(D),
    )


def plain_tables(row_count):
    half_rot = ROT // 2
    positions = jnp.arange(row_count).astype(jnp.float32)
    freqs = 10000.0 ** (-(2.0 * jnp.arange(half_rot).astype(jnp.float32)) / ROT)
    angles = positions[:, None] * freqs[None, :]
    return (jnp.cos(angles)[:, None, :], jnp.sin(angles)[:, None, :])


def plain_rotate(field, cosines, sines):
    half_rot = ROT // 2
    first = field[..., :half_rot]
    second = field[..., half_rot:ROT]
    return jnp.concatenate(
        [first * cosines - second * sines, second * cosines + first * sines, field[..., ROT:]],
        axis=-1,
    )


def gelu_tanh(values):
    return jax.nn.gelu(values, approximate=True)


def causal_scores(query_block, key_rows, block_index):
    block_len = query_block.shape[0]
    query_pos = block_index * block_len + jnp.arange(block_len)
    key_pos = jnp.arange(key_rows.shape[0])
    raw = jnp.einsum("qhd,khd->hqk", query_block, key_rows, preferred_element_type=jnp.float32)
    scaled = raw * HEAD_DIM ** (-0.5)
    return jnp.where(key_pos[None, None, :] <= query_pos[None, :, None], scaled, big_negative)


def attend_forward(queries, key_rows, value_rows, block_len):
    row_count, heads_here, head_size = queries.shape
    n_blocks = row_count // block_len
    query_blocks = queries.reshape(n_blocks, block_len, heads_here, head_size)

    def one_block(item):
        query_block, block_index = item
        scores = causal_scores(query_block, key_rows, block_index)
        top_score = jnp.max(scores, axis=2, keepdims=True)
        exponent = jnp.exp(scores - top_score)
        totals = jnp.sum(exponent, axis=2, keepdims=True)
        probability = (exponent / totals).astype(jnp.bfloat16)
        attended = jnp.einsum(
            "hqk,khd->qhd", probability, value_rows, preferred_element_type=jnp.float32
        )
        return (attended, (top_score + jnp.log(totals))[:, :, 0])

    attended, logsum = lax.map(one_block, (query_blocks, jnp.arange(n_blocks)))
    return (attended.reshape(row_count, heads_here * head_size), logsum)


def attend_backward(queries, key_rows, value_rows, grad_att, logsum, block_len):
    row_count, heads_here, head_size = queries.shape
    n_blocks = row_count // block_len
    query_blocks = queries.reshape(n_blocks, block_len, heads_here, head_size)
    grad_blocks = grad_att.reshape(n_blocks, block_len, heads_here, head_size)
    scaling = HEAD_DIM ** (-0.5)

    def one_block(carry, item):
        grad_keys, grad_values = carry
        query_block, grad_block, lse_block, block_index = item
        scores = causal_scores(query_block, key_rows, block_index)
        probability = jnp.exp(scores - lse_block[:, :, None])
        grad_probs = jnp.einsum(
            "qhd,khd->hqk", grad_block, value_rows, preferred_element_type=jnp.float32
        )
        centre = jnp.sum(grad_probs * probability, axis=2, keepdims=True)
        grad_scores = (probability * (grad_probs - centre) * scaling).astype(jnp.bfloat16)
        grad_query = jnp.einsum(
            "hqk,khd->qhd", grad_scores, key_rows, preferred_element_type=jnp.float32
        )
        grad_keys = grad_keys + jnp.einsum(
            "hqk,qhd->khd", grad_scores, query_block, preferred_element_type=jnp.float32
        )
        grad_values = grad_values + jnp.einsum(
            "hqk,qhd->khd",
            probability.astype(jnp.bfloat16),
            grad_block,
            preferred_element_type=jnp.float32,
        )
        return ((grad_keys, grad_values), grad_query)

    zero_rows = jnp.zeros(key_rows.shape, jnp.float32)
    (grad_keys, grad_values), grad_queries = lax.scan(
        one_block, (zero_rows, zero_rows), (query_blocks, grad_blocks, logsum, jnp.arange(n_blocks))
    )
    return (grad_queries.reshape(row_count, heads_here, head_size), grad_keys, grad_values)


def plain_shards(tokens, ln_gain, ln_bias, w_qkv, b_qkv, w_out, w_up, b_up, w_down, out_bias, cotangent):
    activ = tokens.astype(jnp.float32)
    average = jnp.mean(activ, axis=1, keepdims=True)
    centered = activ - average
    variance = jnp.mean(centered * centered, axis=1, keepdims=True)
    inv_std = lax.rsqrt(variance + epsilon)
    x_hat = centered * inv_std
    normed = lax.all_gather(
        (x_hat * ln_gain + ln_bias).astype(jnp.bfloat16), "tensor", axis=0, tiled=True
    )
    row_count = normed.shape[0]
    block_len = min(row_count, 512)
    qkv_full, out_full, up_full, down_full = (
        lax.all_gather(w_qkv, "dp", axis=0, tiled=True),
        lax.all_gather(w_out, "dp", axis=1, tiled=True),
        lax.all_gather(w_up, "dp", axis=0, tiled=True),
        lax.all_gather(w_down, "dp", axis=1, tiled=True),
    )
    heads_here = w_qkv.shape[2] // HEAD_DIM
    local_width = heads_here * HEAD_DIM
    head_shape = (row_count, heads_here, HEAD_DIM)
    project = (
        jnp.einsum("td,dcf->tcf", normed, qkv_full, preferred_element_type=jnp.float32) + b_qkv
    )
    cosines, sines = plain_tables(row_count)
    queries = plain_rotate(project[:, 0].reshape(head_shape), cosines, sines).astype(jnp.bfloat16)
    key_rows = plain_rotate(project[:, 1].reshape(head_shape), cosines, sines).astype(jnp.bfloat16)
    value_rows = project[:, 2].reshape(head_shape).astype(jnp.bfloat16)
    attended, logsum = attend_forward(queries, key_rows, value_rows, block_len)
    attended = attended.astype(jnp.bfloat16)
    hidden = jnp.dot(normed, up_full, preferred_element_type=jnp.float32) + b_up
    activated = gelu_tanh(hidden).astype(jnp.bfloat16)
    partial_rows = jnp.dot(attended, out_full, preferred_element_type=jnp.float32) + jnp.dot(
        activated, down_full, preferred_element_type=jnp.float32
    )
    summed = lax.psum_scatter(partial_rows, "tensor", scatter_dimension=0, tiled=True)
    output = (activ + summed + out_bias).astype(jnp.bfloat16)
    grad_local = cotangent.astype(jnp.float32)
    grad_rows = lax.all_gather(cotangent, "tensor", axis=0, tiled=True)
    grad_down = jnp.einsum("tf,td->fd", activated, grad_rows, preferred_element_type=jnp.float32)
    grad_act = jnp.einsum("td,fd->tf", grad_rows, down_full, preferred_element_type=jnp.float32)
    gelu_pull = jax.vjp(gelu_tanh, hidden)[1]
    grad_hidden = gelu_pull(grad_act)[0].astype(jnp.bfloat16)
    grad_up = jnp.einsum("td,tf->df", normed, grad_hidden, preferred_element_type=jnp.float32)
    grad_b_up = jnp.sum(grad_hidden.astype(jnp.float32), axis=0)
    grad_normed = jnp.einsum("tf,df->td", grad_hidden, up_full, preferred_element_type=jnp.float32)
    grad_out = jnp.einsum("tf,td->fd", attended, grad_rows, preferred_element_type=jnp.float32)
    grad_att = jnp.einsum(
        "td,fd->tf", grad_rows, out_full, preferred_element_type=jnp.float32
    ).astype(jnp.bfloat16)
    grad_queries, grad_keys, grad_values = attend_backward(
        queries, key_rows, value_rows, grad_att.reshape(head_shape), logsum, block_len
    )
    grad_q_pre = plain_rotate(grad_queries, cosines, -sines).reshape(row_count, local_width)
    grad_k_pre = plain_rotate(grad_keys, cosines, -sines).reshape(row_count, local_width)
    grad_project = jnp.stack(
        [grad_q_pre, grad_k_pre, grad_values.reshape(row_count, local_width)], axis=1
    ).astype(jnp.bfloat16)
    grad_qkv = jnp.einsum("td,tcf->dcf", normed, grad_project, preferred_element_type=jnp.float32)
    grad_b_qkv = jnp.sum(grad_project.astype(jnp.float32), axis=0)
    grad_normed = grad_normed + jnp.einsum(
        "tcf,dcf->td", grad_project, qkv_full, preferred_element_type=jnp.float32
    )
    grad_ln_out = lax.psum_scatter(grad_normed, "tensor", scatter_dimension=0, tiled=True)
    qkv_summed, out_summed, up_summed, down_summed = (
        lax.psum_scatter(grad_qkv, "dp", scatter_dimension=0, tiled=True),
        lax.psum_scatter(grad_out, "dp", scatter_dimension=1, tiled=True),
        lax.psum_scatter(grad_up, "dp", scatter_dimension=0, tiled=True),
        lax.psum_scatter(grad_down, "dp", scatter_dimension=1, tiled=True),
    )
    scaled_grad = grad_ln_out * ln_gain
    grad_tokens = (
        inv_std
        * (
            scaled_grad
            - jnp.mean(scaled_grad, axis=1, keepdims=True)
            - x_hat * jnp.mean(scaled_grad * x_hat, axis=1, keepdims=True)
        )
        + grad_local
    )
    gain_grad, shift_grad, bias_grad = lax.psum(
        (
            jnp.sum(grad_ln_out * x_hat, axis=0),
            jnp.sum(grad_ln_out, axis=0),
            jnp.sum(grad_local, axis=0),
        ),
        ("dp", "tensor"),
    )
    qkv_bias_grad, up_bias_grad = lax.psum((grad_b_qkv, grad_b_up), "dp")
    return (
        output,
        grad_tokens,
        gain_grad,
        shift_grad,
        qkv_summed,
        qkv_bias_grad,
        out_summed,
        up_summed,
        up_bias_grad,
        down_summed,
        bias_grad,
    )


def solution(mesh):
    placed = (
        P(("dp", "tensor"), None),
        P(),
        P(),
        P("dp", None, "tensor"),
        P(None, "tensor"),
        P("tensor", "dp"),
        P("dp", "tensor"),
        P("tensor"),
        P("tensor", "dp"),
        P(),
        P(("dp", "tensor"), None),
    )
    results = (
        P(("dp", "tensor"), None),
        P(("dp", "tensor"), None),
        P(),
        P(),
        P("dp", None, "tensor"),
        P(None, "tensor"),
        P("tensor", "dp"),
        P("dp", "tensor"),
        P("tensor"),
        P("tensor", "dp"),
        P(),
    )
    one_kernel = mesh.shape["dp"] == 8 and mesh.shape["tensor"] == 4
    return jax.shard_map(
        fast_shards if one_kernel else plain_shards,
        mesh=mesh,
        in_specs=placed,
        out_specs=results,
        check_vma=False,
    )
```

```python
import functools
import math

import jax
import jax.numpy as jnp
import numpy as np
from jax import lax
from jax.experimental import pallas as pl
from jax.experimental.pallas import tpu as pltpu
from jax.sharding import PartitionSpec as P

HEAD_DIM = 64
ROT = 32
epsilon = 1e-05
big_negative = -1e30

f32 = jnp.float32
bf16 = jnp.bfloat16
NN = (((1,), (0,)), ((), ()))
NT = (((1,), (1,)), ((), ()))
TN = (((0,), (0,)), ((), ()))
dot = functools.partial(lax.dot_general, preferred_element_type=f32)

GELU_A = math.sqrt(2.0 / math.pi)
GELU_B = 0.044715
CHUNK = 512
Q_BLOCK = 128
LANES = 128


def gelu_both(h):
    square = h * h
    t = jnp.tanh(h * (GELU_A + (GELU_A * GELU_B) * square))
    half = 0.5 * (1.0 + t)
    slope = half + (0.5 * h) * (1.0 - t * t) * (GELU_A + (3.0 * GELU_A * GELU_B) * square)
    return h * half, slope


def rotary_tables(row_count):
    half_rot = ROT // 2
    positions = np.arange(row_count, dtype=np.float32)
    freqs = np.float32(10000.0) ** (-(2.0 * np.arange(half_rot, dtype=np.float32)) / np.float32(ROT))
    angles = positions[:, None] * freqs.astype(np.float32)[None, :]
    cosines, sines = np.cos(angles), np.sin(angles)
    rest = np.zeros((row_count, HEAD_DIM - ROT), np.float32)
    c_head = np.concatenate([cosines, cosines, rest + 1.0], axis=1)
    s_head = np.concatenate([-sines, sines, rest], axis=1)
    pair = lambda t: np.concatenate([t, t], axis=1).astype(np.float32)
    return pair(c_head), pair(s_head)


def rotate(field, cosines, sines):
    half = ROT // 2
    lane = lax.broadcasted_iota(jnp.int32, field.shape, 1)
    first = lax.rem(lane, HEAD_DIM) < half
    partner = jnp.where(
        first, pltpu.roll(field, LANES - half, 1), pltpu.roll(field, half, 1)
    )
    return field * cosines + partner * sines


ORDER = (
    "s:Glo", "ln", "s:Od", "s:Gx", "s:Nc", "s:Qc", "s:Oc", "r:Qg", "r:Og", "s:D0d", "s:U0e",
    "s:Nx", "s:U0d", "s:Nlo", "s:Qd", "r:Ncx", "s:U0c", "r:U0h", "r:Gxlo", "r:U0g", "s:U0a",
    "r:Nxlo", "r:Gcxlo", "s:Oe", "r:Oh", "s:Gc", "r:Gcx", "s:Qe", "r:U0f", "s:Oa", "r:Ncxlo",
    "s:Qa", "r:Of", "r:Qh", "hid00", "s:D0e", "r:Qf", "hid01", "near:D011", "s:D0a", "near:D030",
    "proj0", "s:D0c", "att00", "near:D031", "att01", "far:D00", "r:D0h", "r:D0f", "swap:D0",
    "r:D0g", "far:D01", "proj1", "att10", "att11", "near:A30", "core:o11", "core:o01", "cross:o1",
    "core:o10", "far:A0", "dh00", "near:A10", "dh01", "core:n11", "level:o", "near:U031",
    "cross:n1", "core:n10", "near:U010", "near:A31", "fin:A", "far:U01", "near:U030", "near:U011",
    "core:n01", "core:o00", "level:n", "cross:o0", "fin:U0", "near:A11", "far:A1", "cross:n0",
    "near:D010", "swap:U0", "far:U00", "core:n00", "own:o", "swap:A", "fin:D0", "own:n", "small",
)


def block_kernel(
    tokens, cot, gain, shift, out_bias, wq_in, wo_in, wu_in, wd_in, bq_in, bu_in, cos_t, sin_t,
    o_out, o_gt, o_vec, o_part, ry, rm, rl, rc, rx, rr_lo,
    XN, G, WU, WD, WQ, WO, ACT, DH, ATT, DP, KS, VS, DK, DV, YS, FF, RING, LD, VEC, SV, SR,
    ssem, rsem, lsem,
):
    T, D = tokens.shape
    R = wu_in.shape[0]
    F = wu_in.shape[1] // 2
    H = wo_in.shape[0] // 2
    ROWS = 8 * T
    LEN = 4 * T
    half_d = D // 2
    LN_ROWS = min(T, 64)

    dp = lax.axis_index("dp")
    tp = lax.axis_index("tensor")
    hi = lax.div(dp, 4)
    lo = lax.rem(lax.div(dp, 2), 2)
    y = lax.rem(dp, 2)
    x = lax.div(tp, 2)
    c = lax.rem(tp, 2)

    def device(hi_=hi, lo_=lo, y_=y, x_=x, c_=c):
        return {"dp": (hi_ * 2 + lo_) * 2 + y_, "tensor": x_ * 2 + c_}

    to_x = device(x_=1 - x)
    to_c = device(c_=1 - c)
    to_lo = device(lo_=1 - lo)
    to_y = device(y_=1 - y)
    to_hi = device(hi_=1 - hi)
    to_hilo = device(hi_=1 - hi, lo_=1 - lo)
    partners = [to_x, to_c, to_lo, to_y, to_hi, to_hilo]

    mult = pl.multiple_of

    n_copies = [0]
    n_local = [0]
    pending = []

    class Send:
        def __init__(self, src, dst, dev):
            i = n_copies[0]
            n_copies[0] += 1
            self.d = pltpu.make_async_remote_copy(
                src_ref=src, dst_ref=dst, send_sem=ssem.at[i], recv_sem=rsem.at[i],
                device_id=dev, device_id_type=pl.DeviceIdType.MESH,
            )
            self.open = False
            self.arrived = False

        def start(self):
            self.d.start()
            self.open = True
            pending.append(self)

        def got(self):
            if not self.arrived:
                self.d.wait_recv()
            self.arrived = True

        def done(self):
            if self.open:
                self.d.wait_send()
            self.open = False

    class Local:
        def __init__(self, src, dst):
            i = n_local[0]
            n_local[0] += 1
            self.d = pltpu.make_async_copy(src, dst, lsem.at[i])
            self.d.start()
            self.open = True

        def done(self):
            if self.open:
                self.d.wait()
            self.open = False

    sends = {}

    def got(*names):
        for n in names:
            sends[n].got()

    def start(*names):
        for n in names:
            sends[n].start()

    steps = {}

    def col(p, low):
        return mult(p * 2 * R + low * R, R)

    def abs_block(p, low):
        hi_ = hi if p < 2 else 1 - hi
        y_ = y if p % 2 == 0 else 1 - y
        return mult(((hi_ * 2 + low) * 2 + y_) * R, R)

    pieces = [(p, low) for p in range(4) for low in range(2)]

    def piece_cols(p, low):
        return slice(p * 2 * R + low * R, p * 2 * R + (low + 1) * R)

    def piece_ds(p, low):
        return pl.ds(p * 2 * R + low * R, R)

    def row(low, xx, cc):
        return mult((low * 4 + xx * 2 + cc) * T, T)

    own_row = row(lo, x, c)
    own_rows = pl.ds(own_row, T)

    tok_loads, cot_loads = [], []
    for p, low in pieces:
        src = pl.ds(abs_block(p, low), R)
        tok_loads.append(Local(tokens.at[:, src], RING.at[0, :, piece_ds(p, low)]))
    for p, low in pieces:
        src = pl.ds(abs_block(p, low), R)
        cot_loads.append(Local(cot.at[:, src], G.at[own_rows, piece_ds(p, low)]))

    own_weights = {}

    def weight(w, src, land):
        own_weights[w] = Local(src(lo), land(0, lo))
        sends[w + "a"] = Send(src(1 - lo), land(0, lo), to_lo)
        sends[w + "c"] = Send(src(lo), land(2, lo), to_hi)
        sends[w + "e"] = Send(src(1 - lo), land(2, lo), to_hilo)
        sends[w + "d"] = Send(src(lo), land(1, lo), to_y)
        sends[w + "f"] = Send(land(0, 1 - lo), land(1, 1 - lo), to_y)
        sends[w + "g"] = Send(land(2, lo), land(3, lo), to_y)
        sends[w + "h"] = Send(land(2, 1 - lo), land(3, 1 - lo), to_y)
        for n in "aced":
            steps["s:" + w + n] = functools.partial(start, w + n)
        for n, before in (("f", "a"), ("g", "c"), ("h", "e")):
            steps["r:" + w + n] = functools.partial(relay, w + before, w + n)

    def relay(before, *after):
        got(before)
        start(*after)

    def weight_ready(*ws):
        for w in ws:
            own_weights[w].done()
            got(w + "d", w + "f", w + "g", w + "h")

    weight(
        "U0",
        lambda h: wu_in.at[:, pl.ds(mult(h * F, F), F)],
        lambda p, low: WU.at[pl.ds(col(p, low), R), :],
    )
    weight(
        "Q",
        lambda h: wq_in.at[:, :, pl.ds(mult(h * H, H), H)],
        lambda p, low: WQ.at[:, pl.ds(col(p, low), R), :],
    )
    weight(
        "O",
        lambda h: wo_in.at[pl.ds(mult(h * H, H), H), :],
        lambda p, low: WO.at[:, pl.ds(col(p, low), R)],
    )
    weight(
        "D0",
        lambda h: wd_in.at[pl.ds(mult(h * F, F), F), :],
        lambda p, low: WD.at[:, pl.ds(col(p, low), R)],
    )

    def rows_over(r, buf):
        def at(low, xx):
            return buf.at[pl.ds(row(low, xx, c), T), :]

        sends[r + "lo"] = Send(at(lo, x), at(lo, x), to_lo)
        sends[r + "x"] = Send(at(lo, x), at(lo, x), to_x)
        sends[r + "xlo"] = Send(at(1 - lo, x), at(1 - lo, x), to_x)
        sends[r + "c"] = Send(at(lo, x), at(lo, x), to_c)
        sends[r + "clo"] = Send(at(1 - lo, x), at(1 - lo, x), to_c)
        sends[r + "cx"] = Send(at(lo, 1 - x), at(lo, 1 - x), to_c)
        sends[r + "cxlo"] = Send(at(1 - lo, 1 - x), at(1 - lo, 1 - x), to_c)
        steps["r:" + r + "xlo"] = functools.partial(relay, r + "lo", r + "xlo", r + "clo")
        steps["r:" + r + "cx"] = functools.partial(relay, r + "x", r + "cx")
        steps["r:" + r + "cxlo"] = functools.partial(relay, r + "xlo", r + "cxlo")

    rows_over("N", XN)
    rows_over("G", G)

    def rows_ready(*rs):
        for r in rs:
            got(r + "c", r + "clo", r + "cx", r + "cxlo")

    def start_g(n):
        for ld in cot_loads:
            ld.done()
        start("G" + n)

    for n in ("lo", "x", "c"):
        steps["s:N" + n] = functools.partial(start, "N" + n)
        steps["s:G" + n] = functools.partial(start_g, n)

    def normalise(k, sub):
        activ = RING[k, sub, :].astype(f32)
        average = jnp.mean(activ, axis=1, keepdims=True)
        centered = activ - average
        variance = jnp.mean(centered * centered, axis=1, keepdims=True)
        inv_std = lax.rsqrt(variance + epsilon)
        return centered * inv_std, inv_std

    def sub_rows(i):
        return pl.ds(mult(i * LN_ROWS, LN_ROWS), LN_ROWS)

    def step_ln():
        for p, low in pieces:
            src = pl.ds(abs_block(p, low), R)
            VEC[0:1, piece_ds(p, low)] = gain[:, src]
            VEC[1:2, piece_ds(p, low)] = shift[:, src]
            VEC[2:3, piece_ds(p, low)] = out_bias[:, src]
        for ld in tok_loads:
            ld.done()

        def body(i, _):
            x_hat, _unused = normalise(0, sub_rows(i))
            XN[pl.ds(mult(own_row + i * LN_ROWS, LN_ROWS), LN_ROWS), :] = (
                x_hat * VEC[0:1, :] + VEC[1:2, :]
            ).astype(bf16)

        lax.fori_loop(0, T // LN_ROWS, body, None)

    steps["ln"] = step_ln

    def tiles(first, stop, body):
        lax.fori_loop(first, stop, lambda i, _: body(pl.ds(mult(i * T, T), T)), None)

    def step_hid(first, stop):
        weight_ready("U0")
        rows_ready("N")

        def body(rows):
            xn = XN[rows, :]
            for m in range(0, F, R):
                cols = slice(m, m + R)
                bias = bu_in[:, pl.ds(mult(lo * F + m, R), R)]
                h = dot(xn, WU[:, cols], NN) + bias
                act, slope = gelu_both(h)
                ACT[rows, cols] = act.astype(bf16)
                DH[rows, cols] = slope.astype(bf16)

        tiles(first, stop, body)

    steps["hid00"] = functools.partial(step_hid, 0, 4)
    steps["hid01"] = functools.partial(step_hid, 4, 8)

    def step_dh(first, stop):
        weight_ready("D0")
        rows_ready("G")
        if first == 0:
            VEC[3:4, 0:F] = jnp.zeros((1, F), f32)

        def body(rows):
            gg = G[rows, :]
            for m in range(0, F, R):
                cols = slice(m, m + R)
                dh = (dot(gg, WD[cols, :], NT) * DH[rows, cols].astype(f32)).astype(bf16)
                DH[rows, cols] = dh
                VEC[3:4, cols] += jnp.sum(dh.astype(f32), axis=0, keepdims=True)

        tiles(first, stop, body)

    steps["dh00"] = functools.partial(step_dh, 0, 4)
    steps["dh01"] = functools.partial(step_dh, 4, 8)

    Q, DA = 0, 1

    def seq_row(s, off):
        return mult((1 - lo if s == 0 else lo) * LEN + off, Q_BLOCK)

    def head_rows(which, begin, cc):
        cols = pl.ds(mult(begin // T * H + cc, LANES), LANES)
        return YS[1, which, begin % T : begin % T + Q_BLOCK, cols]

    def step_proj(s):
        weight_ready("Q", "O")
        rows_ready("N", "G")

        def body(i, _):
            pos = pl.ds(mult(i * T, T), T)
            rows = pl.ds(mult(seq_row(s, 0) + i * T, T), T)
            cs, sn = cos_t[pos, :], sin_t[pos, :]

            def turned(v):
                return [
                    rotate(v[:, a : a + LANES], cs, sn).astype(bf16) for a in range(0, H, LANES)
                ]

            def put(which, vs):
                for n, u in enumerate(vs):
                    YS[1, which, :, pl.ds(mult(i * H + n * LANES, LANES), LANES)] = u

            xn = XN[rows, :]

            def part(k):
                return dot(xn, WQ[k], NN) + bq_in[k : k + 1, pl.ds(mult(lo * H, LANES), H)]

            put(Q, turned(part(0)))
            for n, u in enumerate(turned(part(1))):
                KS[pos, n * LANES : (n + 1) * LANES] = u
            VS[pos, :] = part(2).astype(bf16)
            d_att = dot(G[rows, :], WO[...], NT).astype(bf16)
            put(DA, [d_att[:, a : a + LANES] for a in range(0, H, LANES)])

        lax.fori_loop(0, 4, body, None)

    def step_att(s, first_pair, n_pairs):
        first = lax.broadcasted_iota(jnp.int32, (Q_BLOCK, LANES), 1) < HEAD_DIM
        scaling = HEAD_DIM**-0.5

        def split(v):
            zero = jnp.zeros_like(v)
            return jnp.concatenate([jnp.where(first, v, zero), jnp.where(first, zero, v)], axis=0)

        def join(v):
            return jnp.where(first, v[:Q_BLOCK], v[Q_BLOCK:])

        def pair(hp, _):
            cc = hp * LANES
            out_cols = pl.ds(mult(cc, LANES), LANES)
            for i in range(LEN // Q_BLOCK):
                rr = pl.ds(i * Q_BLOCK, Q_BLOCK)
                out_rows = pl.ds(seq_row(s, i * Q_BLOCK), Q_BLOCK)
                n = (i + 1) * Q_BLOCK
                old = n - Q_BLOCK
                qm = split(head_rows(Q, old, cc))
                dm = split(head_rows(DA, old, cc))
                kk = KS[0:n, out_cols]
                vv = VS[0:n, out_cols]
                st = dot(kk, qm * jnp.asarray(scaling, bf16), NT)
                kpos = lax.broadcasted_iota(jnp.int32, (Q_BLOCK, 2 * Q_BLOCK), 0)
                qpos = lax.broadcasted_iota(jnp.int32, (Q_BLOCK, 2 * Q_BLOCK), 1)
                qpos = jnp.where(qpos < Q_BLOCK, qpos, qpos - Q_BLOCK)
                diagonal = jnp.where(kpos <= qpos, st[old:], big_negative)
                st = diagonal if i == 0 else jnp.concatenate([st[:old], diagonal], axis=0)
                ex = jnp.exp(st - jnp.max(st, axis=0, keepdims=True))
                prob = ex * (1.0 / jnp.sum(ex, axis=0, keepdims=True))
                pb = prob.astype(bf16)
                ATT[out_rows, out_cols] = join(dot(pb, vv, TN)).astype(bf16)
                dv = dot(pb, dm, NN)
                dprob = dot(vv, dm * jnp.asarray(scaling, bf16), NT)
                centre = jnp.sum(dprob * prob, axis=0, keepdims=True)
                ds = (prob * (dprob - centre)).astype(bf16)
                dq = join(dot(ds, kk, TN))
                DP[out_rows, out_cols] = rotate(dq, cos_t[rr, :], -sin_t[rr, :]).astype(bf16)
                dk = dot(ds, qm, NN)
                if i > 0:
                    DK[0:old, :] += dk[:old]
                    DV[0:old, :] += dv[:old]
                DK[rr, :] = dk[old:]
                DV[rr, :] = dv[old:]
            seq = pl.ds(seq_row(s, 0), LEN)
            DP[seq, pl.ds(mult(H + cc, LANES), LANES)] = rotate(
                DK[...], cos_t[...], -sin_t[...]
            ).astype(bf16)
            DP[seq, pl.ds(mult(2 * H + cc, LANES), LANES)] = DV[...].astype(bf16)

        lax.fori_loop(first_pair, first_pair + n_pairs, pair, None)

    half_pairs = H // LANES // 2
    for s in range(2):
        steps["proj%d" % s] = functools.partial(step_proj, s)
        if half_pairs:
            steps["att%d0" % s] = functools.partial(step_att, s, 0, half_pairs)
            steps["att%d1" % s] = functools.partial(step_att, s, half_pairs, half_pairs)
            steps["att%d" % s] = functools.partial(step_att, s, 0, 2 * half_pairs)
        else:
            steps["att%d0" % s] = functools.partial(step_att, s, 0, 1)
            steps["att%d1" % s] = lambda: None
            steps["att%d" % s] = steps["att%d0" % s]

    ff_use = {0: [], 1: []}

    def ff_free(*which):
        for k in which:
            for ld in ff_use[k]:
                ld.done()
            ff_use[k] = []

    def cols_of(p, q):
        return pl.ds(col(p, lo if q == 0 else 1 - lo), R)

    def block_dn(p, q):
        gg = G[:, cols_of(p, q)]
        return [(m, dot(ACT[:, m : m + R], gg, TN)) for m in range(0, F, R)]

    def block_up(p, q):
        return [(0, dot(XN[:, cols_of(p, q)], DH[...], TN))]

    def block_at(p, q):
        cc = cols_of(p, q)
        return [(0, dot(XN[:, cc], DP[...], TN)), (3 * H, dot(ATT[...], G[:, cc], TN))]

    def weight_grad(g, i, block, needs):
        def slot(p, q):
            return (0 if p >= 2 else 2) + (1 - q)

        def pq(p, q):
            return "%d%d" % (p, q)

        for p, q in ((3, 1), (3, 0), (1, 1), (1, 0)):
            k = slot(p, q)
            sends["y" + g + pq(p, q)] = Send(YS.at[i, k], ry.at[i, k], to_y)
        sends["m" + g + "0"] = Send(YS.at[i, slot(3, 0)], rm.at[i, 0], to_hi)
        sends["m" + g + "1"] = Send(YS.at[i, slot(3, 1)], rm.at[i, 1], to_hilo)
        sends["l" + g] = Send(YS.at[i, slot(1, 1)], rl.at[i], to_lo)

        def near(p, q):
            needs()
            k = slot(p, q)
            for off, v in block(p, q):
                YS[i, k, :, off : off + v.shape[1]] = v.astype(bf16)
            start("y" + g + pq(p, q))

        def pass_on(p, q, then):
            k = slot(p, q)
            came = "y" + g + pq(p + 1, q)
            got(came)
            load = Local(ry.at[i, k], LD.at[0, 0:R, 0:F])
            vals = block(p, q)
            sends[came].done()
            load.done()
            for off, v in vals:
                cols = slice(off, off + v.shape[1])
                YS[i, k, :, cols] = (v + LD[0, 0:R, cols].astype(f32)).astype(bf16)
            start(then)

        def fin():
            ff_free(0)
            got("y" + g + "10")
            load = Local(ry.at[i, slot(0, 0)], LD.at[0, 0:R, 0:F])
            vals = block(0, 0)
            load.done()
            for off, v in vals:
                cols = slice(off, off + v.shape[1])
                FF[0, :, cols] = v + LD[0, 0:R, cols].astype(f32)
            ff_use[0] = [Local(FF.at[0], o_part.at[i])]

        for p, q in ((3, 1), (3, 0), (1, 1), (1, 0)):
            steps["near:" + g + pq(p, q)] = functools.partial(near, p, q)
        for q in range(2):
            steps["far:" + g + str(q)] = functools.partial(pass_on, 2, q, "m" + g + str(q))
        steps["swap:" + g] = functools.partial(pass_on, 0, 1, "l" + g)
        steps["fin:" + g] = fin

    weight_grad("D0", 0, block_dn, lambda: rows_ready("G"))
    weight_grad("A", 1, block_at, lambda: None)
    weight_grad("U0", 2, block_up, lambda: None)

    def rows_out(rr, cc):
        return dot(ACT[rr, :], WD[:, cc], NN) + dot(ATT[rr, :], WO[:, cc], NN)

    def rows_dn(rr, cc):
        v = dot(DH[rr, :], WU[cc, :], NT)
        for k in range(3):
            v = v + dot(DP[rr, k * H : (k + 1) * H], WQ[k, cc, :], NT)
        return v

    ring_use = {0: None, 1: None, 2: None}
    ring_next = [0]

    def ring_slot():
        k = ring_next[0]
        ring_next[0] = (k + 1) % 3
        if ring_use[k] is not None:
            ring_use[k].done()
            ring_use[k] = None
        return k

    def load_tokens():
        k = ring_slot()
        return k, [
            Local(tokens.at[:, pl.ds(abs_block(p, low), R)], RING.at[k, :, piece_ds(p, low)])
            for p, low in pieces
        ]

    def own_sub(sub):
        return jnp.concatenate([FF[0, sub, :], FF[1, sub, :]], axis=1) + LD[0, sub, :].astype(f32)

    def finish_out(k_tok):
        k = ring_slot()

        def body(i, _):
            sub = sub_rows(i)
            RING[k, sub, :] = (
                RING[k_tok, sub, :].astype(f32) + own_sub(sub) + VEC[2:3, :]
            ).astype(bf16)

        lax.fori_loop(0, T // LN_ROWS, body, None)
        stores = [
            Local(RING.at[k, :, piece_ds(p, low)], o_out.at[:, pl.ds(abs_block(p, low), R)])
            for p, low in pieces
        ]
        for st in stores:
            st.done()

    def finish_dn(k_tok):
        VEC[4:6, :] = jnp.zeros((2, D), f32)

        def body(i, _):
            sub = sub_rows(i)
            x_hat, inv_std = normalise(k_tok, sub)
            dn = own_sub(sub)
            VEC[4:5, :] += jnp.sum(dn * x_hat, axis=0, keepdims=True)
            VEC[5:6, :] += jnp.sum(dn, axis=0, keepdims=True)
            scaled = dn * VEC[0:1, :]
            gt = (
                inv_std
                * (
                    scaled
                    - jnp.mean(scaled, axis=1, keepdims=True)
                    - x_hat * jnp.mean(scaled * x_hat, axis=1, keepdims=True)
                )
                + G[pl.ds(mult(own_row + i * LN_ROWS, LN_ROWS), LN_ROWS), :].astype(f32)
            )
            FF[0, sub, :] = gt[:, :half_d]
            FF[1, sub, :] = gt[:, half_d:]

        lax.fori_loop(0, T // LN_ROWS, body, None)
        for p, low in pieces:
            dst = pl.ds(abs_block(p, low), R)
            src = pl.ds((p % 2) * 2 * R + low * R, R)
            ff_use[p // 2].append(Local(FF.at[p // 2, :, src], o_gt.at[:, dst]))

    def owners(w, i, partial, needs, finish):
        def chunks(low, xx, cc, loads, store):
            rr = pl.ds(row(low, xx, cc), T)
            for ld in loads:
                ld.done()

            def body(j, _):
                cols = pl.ds(mult(j * CHUNK, CHUNK), CHUNK)
                v = partial(rr, cols)
                for k in range(len(loads)):
                    v = v + LD[k, :, cols].astype(f32)
                store(j, cols, v)

            lax.fori_loop(0, D // CHUNK, body, None)

        def put(name, low, xx, cc, srcs, dst, dev):
            needs()
            loads = [Local(src, LD.at[k]) for k, src in enumerate(srcs)]
            k = ring_slot()

            def store(j, cols, v):
                RING[k, :, cols] = v.astype(bf16)

            chunks(low, xx, cc, loads, store)
            sends[name] = Send(RING.at[k], dst, dev)
            start(name)
            ring_use[k] = sends[name]

        def core(dlo, dx):
            low = lo if dlo == 0 else 1 - lo
            xx = x if dx == 0 else 1 - x
            name = "c%s%d%d" % (w, dlo, dx)
            put(name, low, xx, 1 - c, [], rc.at[i, 2 * dlo + dx], to_c)

        def cross(dlo):
            low = lo if dlo == 0 else 1 - lo
            got("c%s%d1" % (w, dlo))
            name = "x%s%d" % (w, dlo)
            put(name, low, 1 - x, c, [rc.at[i, 2 * dlo + 1]], rx.at[i, dlo], to_x)

        def level():
            got("c%s10" % w, "x%s1" % w)
            put("l" + w, 1 - lo, x, c, [rc.at[i, 2], rx.at[i, 1]], rr_lo.at[i], to_lo)

        def own():
            k_tok, tok_ld = load_tokens()
            got("c%s00" % w, "x%s0" % w)
            loads = [Local(rc.at[i, 0], LD.at[0]), Local(rx.at[i, 0], LD.at[1])]
            ff_free(0, 1)
            n = D // CHUNK // 2

            def store(j, cols, v):
                part = pl.ds(mult(lax.rem(j, n) * CHUNK, CHUNK), CHUNK)
                FF[lax.div(j, n), :, part] = v

            chunks(lo, x, c, loads, store)
            got("l" + w)
            Local(rr_lo.at[i], LD.at[0]).done()
            for ld in tok_ld:
                ld.done()
            finish(k_tok)

        for dlo in range(2):
            for dx in range(2):
                steps["core:%s%d%d" % (w, dlo, dx)] = functools.partial(core, dlo, dx)
            steps["cross:%s%d" % (w, dlo)] = functools.partial(cross, dlo)
        steps["level:" + w] = level
        steps["own:" + w] = own

    owners("o", 0, rows_out, lambda: weight_ready("D0"), finish_out)
    owners("n", 1, rows_dn, lambda: None, finish_dn)

    def step_small():
        SV[...] = jnp.zeros_like(SV)
        VEC[6:7, 0 : 3 * H] = jnp.zeros((1, 3 * H), f32)
        VEC[7:8, :] = jnp.zeros((1, D), f32)

        def body(rows):
            VEC[6:7, 0 : 3 * H] += jnp.sum(DP[rows, :].astype(f32), axis=0, keepdims=True)

        tiles(0, ROWS // T, body)

        def g_body(i, _):
            rows = pl.ds(mult(own_row + i * LN_ROWS, LN_ROWS), LN_ROWS)
            VEC[7:8, :] += jnp.sum(G[rows, :].astype(f32), axis=0, keepdims=True)

        lax.fori_loop(0, T // LN_ROWS, g_body, None)
        for p, low in pieces:
            dst = pl.ds(abs_block(p, low), R)
            SV[0:2, dst] = VEC[4:6, piece_cols(p, low)]
            SV[2:3, dst] = VEC[7:8, piece_cols(p, low)]
        SV[3:4, pl.ds(mult(lo * F, F), F)] = VEC[3:4, 0:F]
        for k in range(3):
            SV[4 + k : 5 + k, pl.ds(mult(lo * H, LANES), H)] = VEC[6:7, k * H : (k + 1) * H]
        for k, dev in enumerate((to_y, to_hi, to_lo, to_x, to_c)):
            s = Send(SV, SR.at[k], dev)
            s.start()
            s.got()
            s.done()
            if k < 3:
                SV[...] += SR[k]
            else:
                SV[0:3, :] += SR[k, 0:3, :]
        o_vec[...] = SV[...]

    steps["small"] = step_small

    barrier = pltpu.get_barrier_semaphore()
    for dev in partners:
        pl.semaphore_signal(barrier, inc=1, device_id=dev, device_id_type=pl.DeviceIdType.MESH)
    pl.semaphore_wait(barrier, len(partners))
    for name in ORDER:
        steps[name]()
    ff_free(0, 1)
    for s in pending:
        s.got()
        s.done()
    assert n_copies[0] <= ssem.shape[0] and n_local[0] <= lsem.shape[0], (n_copies, n_local)


def finish_kernel(
    b_out, b_gt, b_vec, b_part, rm, rl,
    o_out, o_gt, o_gain, o_shift, o_bias, o_bu, o_bq, o_gq, o_go, o_gu, o_gd,
    PART, RM, RL, OUT, GT, GU, GD, GQ, GO, lsem,
):
    R, F = PART.shape[1:]
    H = o_go.shape[0] // 2
    lo = lax.rem(lax.div(lax.axis_index("dp"), 2), 2)
    mult = pl.multiple_of
    n = [0]

    def copy(src, dst):
        d = pltpu.make_async_copy(src, dst, lsem.at[n[0]])
        n[0] += 1
        d.start()
        return d

    order = (1, 0, 2)
    loads = {i: [copy(b_part.at[i], PART.at[i]), copy(rm.at[i], RM.at[i]), copy(rl.at[i], RL.at[i])] for i in order}
    load_out = copy(b_out, OUT)
    load_gt = copy(b_gt, GT)
    o_gain[...] = b_vec[0:1, :]
    o_shift[...] = b_vec[1:2, :]
    o_bias[...] = b_vec[2:3, :]
    o_bu[...] = b_vec[3:4, 0 : 2 * F]
    o_bq[...] = b_vec[4:7, 0 : 2 * H]
    stores = []

    def halves(i, put):
        for ld in loads[i]:
            ld.wait()
        for m in range(0, F, R):
            cols = slice(m, m + R)
            put(lo, m, PART[i, :, cols] + RM[i, 0, :, cols].astype(f32))
            put(1 - lo, m, RL[i, :, cols].astype(f32) + RM[i, 1, :, cols].astype(f32))

    def put_at(half, m, v):
        if m < 3 * H:
            GQ[m // H, :, pl.ds(mult(half * H, H), H)] = v
        else:
            GO[pl.ds(mult(half * H, H), H), :] = v

    def put_dn(half, m, v):
        GD[pl.ds(mult(half * F + m, R), R), :] = v

    def put_up(half, m, v):
        GU[:, pl.ds(mult(half * F + m, R), R)] = v

    for i, put, pairs in (
        (1, put_at, ((GQ, o_gq), (GO, o_go))), (0, put_dn, ((GD, o_gd),)), (2, put_up, ((GU, o_gu),)),
    ):
        halves(i, put)
        for src, dst in pairs:
            stores.append(copy(src, dst))
    load_out.wait()
    stores.append(copy(OUT, o_out))
    load_gt.wait()
    stores.append(copy(GT, o_gt))
    for st in stores:
        st.wait()


VMEM_LIMIT = 64 << 20


def fast_shards(tokens, ln_gain, ln_bias, w_qkv, b_qkv, w_out, w_up, b_up, w_down, out_bias, cot):
    T, D = tokens.shape
    R, F = w_up.shape[0], w_up.shape[1] // 2
    H = w_out.shape[0] // 2
    cos_t, sin_t = rotary_tables(4 * T)
    S = jax.ShapeDtypeStruct
    hbm = pl.BlockSpec(memory_space=pl.ANY)
    vm = pl.BlockSpec(memory_space=pltpu.VMEM)
    outs = pl.pallas_call(
        block_kernel,
        out_shape=(
            S((T, D), bf16), S((T, D), f32), S((8, D), f32), S((3, R, F), f32),
            S((3, 4, R, F), bf16), S((3, 2, R, F), bf16), S((3, R, F), bf16),
            S((2, 4, T, D), bf16), S((2, 2, T, D), bf16), S((2, T, D), bf16),
        ),
        in_specs=[hbm, hbm, vm, vm, vm, hbm, hbm, hbm, hbm, vm, vm, vm, vm],
        out_specs=(hbm, hbm, vm) + (hbm,) * 7,
        scratch_shapes=[
            pltpu.VMEM((8 * T, D), bf16),
            pltpu.VMEM((8 * T, D), bf16),
            pltpu.VMEM((D, F), bf16),
            pltpu.VMEM((F, D), bf16),
            pltpu.VMEM((3, D, H), bf16),
            pltpu.VMEM((H, D), bf16),
            pltpu.VMEM((8 * T, F), bf16),
            pltpu.VMEM((8 * T, F), bf16),
            pltpu.VMEM((8 * T, H), bf16),
            pltpu.VMEM((8 * T, 3 * H), bf16),
            pltpu.VMEM((4 * T, H), bf16),
            pltpu.VMEM((4 * T, H), bf16),
            pltpu.VMEM((4 * T, LANES), f32),
            pltpu.VMEM((4 * T, LANES), f32),
            pltpu.VMEM((3, 4, R, F), bf16),
            pltpu.VMEM((2, R, F), f32),
            pltpu.VMEM((3, T, D), bf16),
            pltpu.VMEM((2, T, D), bf16),
            pltpu.VMEM((8, D), f32),
            pltpu.VMEM((8, D), f32),
            pltpu.VMEM((5, 8, D), f32),
            pltpu.SemaphoreType.DMA((90,)),
            pltpu.SemaphoreType.DMA((90,)),
            pltpu.SemaphoreType.DMA((110,)),
        ],
        compiler_params=pltpu.CompilerParams(
            collective_id=0, has_side_effects=True, vmem_limit_bytes=VMEM_LIMIT
        ),
        name="parallel_block",
    )(
        tokens, cot, ln_gain.reshape(1, D), ln_bias.reshape(1, D), out_bias.reshape(1, D),
        w_qkv.transpose(1, 0, 2), w_out, w_up, w_down, b_qkv, b_up.reshape(1, 2 * F), cos_t, sin_t,
    )
    b_out, b_gt, b_vec, b_part, _, rm, rl = outs[:7]
    done = pl.pallas_call(
        finish_kernel,
        out_shape=(
            S((T, D), bf16), S((T, D), f32), S((1, D), f32), S((1, D), f32), S((1, D), f32),
            S((1, 2 * F), f32), S((3, 2 * H), f32),
            S((3, R, 2 * H), f32), S((2 * H, R), f32), S((R, 2 * F), f32), S((2 * F, R), f32),
        ),
        in_specs=[hbm, hbm, vm, hbm, hbm, hbm],
        out_specs=(hbm, hbm) + (vm,) * 5 + (hbm,) * 4,
        scratch_shapes=[
            pltpu.VMEM((3, R, F), f32),
            pltpu.VMEM((3, 2, R, F), bf16),
            pltpu.VMEM((3, R, F), bf16),
            pltpu.VMEM((T, D), bf16),
            pltpu.VMEM((T, D), f32),
            pltpu.VMEM((R, 2 * F), f32),
            pltpu.VMEM((2 * F, R), f32),
            pltpu.VMEM((3, R, 2 * H), f32),
            pltpu.VMEM((2 * H, R), f32),
            pltpu.SemaphoreType.DMA((20,)),
        ],
        compiler_params=pltpu.CompilerParams(vmem_limit_bytes=VMEM_LIMIT),
        name="finish",
    )(b_out, b_gt, b_vec, b_part, rm, rl)
    o_out, o_gt, o_gain, o_shift, o_bias, o_bu, o_bq, o_gq, o_go, o_gu, o_gd = done
    return (
        o_out, o_gt, o_gain.reshape(D), o_shift.reshape(D), o_gq.transpose(1, 0, 2), o_bq, o_go,
        o_gu, o_bu.reshape(2 * F), o_gd, o_bias.reshape(D),
    )


def plain_tables(row_count):
    half_rot = ROT // 2
    positions = jnp.arange(row_count).astype(jnp.float32)
    freqs = 10000.0 ** (-(2.0 * jnp.arange(half_rot).astype(jnp.float32)) / ROT)
    angles = positions[:, None] * freqs[None, :]
    return (jnp.cos(angles)[:, None, :], jnp.sin(angles)[:, None, :])


def plain_rotate(field, cosines, sines):
    half_rot = ROT // 2
    first = field[..., :half_rot]
    second = field[..., half_rot:ROT]
    return jnp.concatenate(
        [first * cosines - second * sines, second * cosines + first * sines, field[..., ROT:]],
        axis=-1,
    )


def gelu_tanh(values):
    return jax.nn.gelu(values, approximate=True)


def causal_scores(query_block, key_rows, block_index):
    block_len = query_block.shape[0]
    query_pos = block_index * block_len + jnp.arange(block_len)
    key_pos = jnp.arange(key_rows.shape[0])
    raw = jnp.einsum("qhd,khd->hqk", query_block, key_rows, preferred_element_type=jnp.float32)
    scaled = raw * HEAD_DIM ** (-0.5)
    return jnp.where(key_pos[None, None, :] <= query_pos[None, :, None], scaled, big_negative)


def attend_forward(queries, key_rows, value_rows, block_len):
    row_count, heads_here, head_size = queries.shape
    n_blocks = row_count // block_len
    query_blocks = queries.reshape(n_blocks, block_len, heads_here, head_size)

    def one_block(item):
        query_block, block_index = item
        scores = causal_scores(query_block, key_rows, block_index)
        top_score = jnp.max(scores, axis=2, keepdims=True)
        exponent = jnp.exp(scores - top_score)
        totals = jnp.sum(exponent, axis=2, keepdims=True)
        probability = (exponent / totals).astype(jnp.bfloat16)
        attended = jnp.einsum(
            "hqk,khd->qhd", probability, value_rows, preferred_element_type=jnp.float32
        )
        return (attended, (top_score + jnp.log(totals))[:, :, 0])

    attended, logsum = lax.map(one_block, (query_blocks, jnp.arange(n_blocks)))
    return (attended.reshape(row_count, heads_here * head_size), logsum)


def attend_backward(queries, key_rows, value_rows, grad_att, logsum, block_len):
    row_count, heads_here, head_size = queries.shape
    n_blocks = row_count // block_len
    query_blocks = queries.reshape(n_blocks, block_len, heads_here, head_size)
    grad_blocks = grad_att.reshape(n_blocks, block_len, heads_here, head_size)
    scaling = HEAD_DIM ** (-0.5)

    def one_block(carry, item):
        grad_keys, grad_values = carry
        query_block, grad_block, lse_block, block_index = item
        scores = causal_scores(query_block, key_rows, block_index)
        probability = jnp.exp(scores - lse_block[:, :, None])
        grad_probs = jnp.einsum(
            "qhd,khd->hqk", grad_block, value_rows, preferred_element_type=jnp.float32
        )
        centre = jnp.sum(grad_probs * probability, axis=2, keepdims=True)
        grad_scores = (probability * (grad_probs - centre) * scaling).astype(jnp.bfloat16)
        grad_query = jnp.einsum(
            "hqk,khd->qhd", grad_scores, key_rows, preferred_element_type=jnp.float32
        )
        grad_keys = grad_keys + jnp.einsum(
            "hqk,qhd->khd", grad_scores, query_block, preferred_element_type=jnp.float32
        )
        grad_values = grad_values + jnp.einsum(
            "hqk,qhd->khd",
            probability.astype(jnp.bfloat16),
            grad_block,
            preferred_element_type=jnp.float32,
        )
        return ((grad_keys, grad_values), grad_query)

    zero_rows = jnp.zeros(key_rows.shape, jnp.float32)
    (grad_keys, grad_values), grad_queries = lax.scan(
        one_block, (zero_rows, zero_rows), (query_blocks, grad_blocks, logsum, jnp.arange(n_blocks))
    )
    return (grad_queries.reshape(row_count, heads_here, head_size), grad_keys, grad_values)


def plain_shards(tokens, ln_gain, ln_bias, w_qkv, b_qkv, w_out, w_up, b_up, w_down, out_bias, cotangent):
    activ = tokens.astype(jnp.float32)
    average = jnp.mean(activ, axis=1, keepdims=True)
    centered = activ - average
    variance = jnp.mean(centered * centered, axis=1, keepdims=True)
    inv_std = lax.rsqrt(variance + epsilon)
    x_hat = centered * inv_std
    normed = lax.all_gather(
        (x_hat * ln_gain + ln_bias).astype(jnp.bfloat16), "tensor", axis=0, tiled=True
    )
    row_count = normed.shape[0]
    block_len = min(row_count, 512)
    qkv_full, out_full, up_full, down_full = (
        lax.all_gather(w_qkv, "dp", axis=0, tiled=True),
        lax.all_gather(w_out, "dp", axis=1, tiled=True),
        lax.all_gather(w_up, "dp", axis=0, tiled=True),
        lax.all_gather(w_down, "dp", axis=1, tiled=True),
    )
    heads_here = w_qkv.shape[2] // HEAD_DIM
    local_width = heads_here * HEAD_DIM
    head_shape = (row_count, heads_here, HEAD_DIM)
    project = (
        jnp.einsum("td,dcf->tcf", normed, qkv_full, preferred_element_type=jnp.float32) + b_qkv
    )
    cosines, sines = plain_tables(row_count)
    queries = plain_rotate(project[:, 0].reshape(head_shape), cosines, sines).astype(jnp.bfloat16)
    key_rows = plain_rotate(project[:, 1].reshape(head_shape), cosines, sines).astype(jnp.bfloat16)
    value_rows = project[:, 2].reshape(head_shape).astype(jnp.bfloat16)
    attended, logsum = attend_forward(queries, key_rows, value_rows, block_len)
    attended = attended.astype(jnp.bfloat16)
    hidden = jnp.dot(normed, up_full, preferred_element_type=jnp.float32) + b_up
    activated = gelu_tanh(hidden).astype(jnp.bfloat16)
    partial_rows = jnp.dot(attended, out_full, preferred_element_type=jnp.float32) + jnp.dot(
        activated, down_full, preferred_element_type=jnp.float32
    )
    summed = lax.psum_scatter(partial_rows, "tensor", scatter_dimension=0, tiled=True)
    output = (activ + summed + out_bias).astype(jnp.bfloat16)
    grad_local = cotangent.astype(jnp.float32)
    grad_rows = lax.all_gather(cotangent, "tensor", axis=0, tiled=True)
    grad_down = jnp.einsum("tf,td->fd", activated, grad_rows, preferred_element_type=jnp.float32)
    grad_act = jnp.einsum("td,fd->tf", grad_rows, down_full, preferred_element_type=jnp.float32)
    gelu_pull = jax.vjp(gelu_tanh, hidden)[1]
    grad_hidden = gelu_pull(grad_act)[0].astype(jnp.bfloat16)
    grad_up = jnp.einsum("td,tf->df", normed, grad_hidden, preferred_element_type=jnp.float32)
    grad_b_up = jnp.sum(grad_hidden.astype(jnp.float32), axis=0)
    grad_normed = jnp.einsum("tf,df->td", grad_hidden, up_full, preferred_element_type=jnp.float32)
    grad_out = jnp.einsum("tf,td->fd", attended, grad_rows, preferred_element_type=jnp.float32)
    grad_att = jnp.einsum(
        "td,fd->tf", grad_rows, out_full, preferred_element_type=jnp.float32
    ).astype(jnp.bfloat16)
    grad_queries, grad_keys, grad_values = attend_backward(
        queries, key_rows, value_rows, grad_att.reshape(head_shape), logsum, block_len
    )
    grad_q_pre = plain_rotate(grad_queries, cosines, -sines).reshape(row_count, local_width)
    grad_k_pre = plain_rotate(grad_keys, cosines, -sines).reshape(row_count, local_width)
    grad_project = jnp.stack(
        [grad_q_pre, grad_k_pre, grad_values.reshape(row_count, local_width)], axis=1
    ).astype(jnp.bfloat16)
    grad_qkv = jnp.einsum("td,tcf->dcf", normed, grad_project, preferred_element_type=jnp.float32)
    grad_b_qkv = jnp.sum(grad_project.astype(jnp.float32), axis=0)
    grad_normed = grad_normed + jnp.einsum(
        "tcf,dcf->td", grad_project, qkv_full, preferred_element_type=jnp.float32
    )
    grad_ln_out = lax.psum_scatter(grad_normed, "tensor", scatter_dimension=0, tiled=True)
    qkv_summed, out_summed, up_summed, down_summed = (
        lax.psum_scatter(grad_qkv, "dp", scatter_dimension=0, tiled=True),
        lax.psum_scatter(grad_out, "dp", scatter_dimension=1, tiled=True),
        lax.psum_scatter(grad_up, "dp", scatter_dimension=0, tiled=True),
        lax.psum_scatter(grad_down, "dp", scatter_dimension=1, tiled=True),
    )
    scaled_grad = grad_ln_out * ln_gain
    grad_tokens = (
        inv_std
        * (
            scaled_grad
            - jnp.mean(scaled_grad, axis=1, keepdims=True)
            - x_hat * jnp.mean(scaled_grad * x_hat, axis=1, keepdims=True)
        )
        + grad_local
    )
    gain_grad, shift_grad, bias_grad = lax.psum(
        (
            jnp.sum(grad_ln_out * x_hat, axis=0),
            jnp.sum(grad_ln_out, axis=0),
            jnp.sum(grad_local, axis=0),
        ),
        ("dp", "tensor"),
    )
    qkv_bias_grad, up_bias_grad = lax.psum((grad_b_qkv, grad_b_up), "dp")
    return (
        output,
        grad_tokens,
        gain_grad,
        shift_grad,
        qkv_summed,
        qkv_bias_grad,
        out_summed,
        up_summed,
        up_bias_grad,
        down_summed,
        bias_grad,
    )


def solution(mesh):
    placed = (
        P(("dp", "tensor"), None),
        P(),
        P(),
        P("dp", None, "tensor"),
        P(None, "tensor"),
        P("tensor", "dp"),
        P("dp", "tensor"),
        P("tensor"),
        P("tensor", "dp"),
        P(),
        P(("dp", "tensor"), None),
    )
    results = (
        P(("dp", "tensor"), None),
        P(("dp", "tensor"), None),
        P(),
        P(),
        P("dp", None, "tensor"),
        P(None, "tensor"),
        P("tensor", "dp"),
        P("dp", "tensor"),
        P("tensor"),
        P("tensor", "dp"),
        P(),
    )
    one_kernel = mesh.shape["dp"] == 8 and mesh.shape["tensor"] == 4
    return jax.shard_map(
        fast_shards if one_kernel else plain_shards,
        mesh=mesh,
        in_specs=placed,
        out_specs=results,
        check_vma=False,
    )
```

```python
import functools
import math

import jax
import jax.numpy as jnp
import numpy as np
from jax import lax
from jax.experimental import pallas as pl
from jax.experimental.pallas import tpu as pltpu
from jax.sharding import PartitionSpec as P

HEAD_DIM = 64
ROT = 32
epsilon = 1e-05
big_negative = -1e30

f32 = jnp.float32
bf16 = jnp.bfloat16
NN = (((1,), (0,)), ((), ()))
NT = (((1,), (1,)), ((), ()))
TN = (((0,), (0,)), ((), ()))
dot = functools.partial(lax.dot_general, preferred_element_type=f32)

GELU_A = math.sqrt(2.0 / math.pi)
GELU_B = 0.044715
CHUNK = 512
Q_BLOCK = 128
LANES = 128


def gelu_both(h):
    square = h * h
    t = jnp.tanh(h * (GELU_A + (GELU_A * GELU_B) * square))
    half = 0.5 * (1.0 + t)
    slope = half + (0.5 * h) * (1.0 - t * t) * (GELU_A + (3.0 * GELU_A * GELU_B) * square)
    return h * half, slope


def rotary_tables(row_count):
    half_rot = ROT // 2
    positions = np.arange(row_count, dtype=np.float32)
    freqs = np.float32(10000.0) ** (-(2.0 * np.arange(half_rot, dtype=np.float32)) / np.float32(ROT))
    angles = positions[:, None] * freqs.astype(np.float32)[None, :]
    cosines, sines = np.cos(angles), np.sin(angles)
    rest = np.zeros((row_count, HEAD_DIM - ROT), np.float32)
    c_head = np.concatenate([cosines, cosines, rest + 1.0], axis=1)
    s_head = np.concatenate([-sines, sines, rest], axis=1)
    pair = lambda t: np.concatenate([t, t], axis=1).astype(np.float32)
    return pair(c_head), pair(s_head)


def rotate(field, cosines, sines):
    half = ROT // 2
    lane = lax.broadcasted_iota(jnp.int32, field.shape, 1)
    first = lax.rem(lane, HEAD_DIM) < half
    partner = jnp.where(
        first, pltpu.roll(field, LANES - half, 1), pltpu.roll(field, half, 1)
    )
    return field * cosines + partner * sines


ORDER = (
    "s:Glo", "ln", "s:Od", "s:Gx", "s:Nc", "s:Qc", "s:Oc", "r:Qg", "r:Og", "s:D0d", "s:U0e",
    "s:Nx", "s:U0d", "s:Nlo", "s:Qd", "r:Ncx", "s:U0c", "r:U0h", "r:Gxlo", "r:U0g", "s:U0a",
    "r:Nxlo", "r:Gcxlo", "s:Oe", "r:Oh", "s:Gc", "r:Gcx", "s:Qe", "r:U0f", "s:Oa", "r:Ncxlo",
    "s:Qa", "r:Of", "r:Qh", "hid00", "s:D0e", "r:Qf", "hid01", "near:D011", "s:D0a", "near:D030",
    "proj0", "s:D0c", "att00", "near:D031", "att01", "far:D00", "r:D0h", "r:D0f", "swap:D0",
    "r:D0g", "far:D01", "proj1", "att10", "att11", "near:A30", "core:o11", "core:o01", "cross:o1",
    "core:o10", "far:A0", "dh00", "near:A10", "dh01", "core:n11", "level:o", "near:U031", "vec",
    "cross:n1", "core:n10", "near:U010", "near:A31", "v1", "fin:A", "far:U01", "near:U030",
    "near:U011", "v2", "core:n01", "core:o00", "level:n", "cross:o0", "v3", "fin:U0", "near:A11",
    "far:A1", "cross:n0", "v4", "near:D010", "swap:U0", "far:U00", "core:n00", "v5", "own:o",
    "swap:A", "fin:D0", "own:n", "small",
)


def block_kernel(
    tokens, cot, gain, shift, out_bias, wq_in, wo_in, wu_in, wd_in, bq_in, bu_in, cos_t, sin_t,
    o_out, o_gt, o_vec, o_part, ry, rm, rl, rc, rx, rr_lo,
    XN, G, WU, WD, WQ, WO, ACT, DH, ATT, DP, KS, VS, DK, DV, YS, FF, RING, LD, VEC, SV, SR, SA, SRA,
    ssem, rsem, lsem,
):
    T, D = tokens.shape
    R = wu_in.shape[0]
    F = wu_in.shape[1] // 2
    H = wo_in.shape[0] // 2
    ROWS = 8 * T
    LEN = 4 * T
    half_d = D // 2
    LN_ROWS = min(T, 64)

    dp = lax.axis_index("dp")
    tp = lax.axis_index("tensor")
    hi = lax.div(dp, 4)
    lo = lax.rem(lax.div(dp, 2), 2)
    y = lax.rem(dp, 2)
    x = lax.div(tp, 2)
    c = lax.rem(tp, 2)

    def device(hi_=hi, lo_=lo, y_=y, x_=x, c_=c):
        return {"dp": (hi_ * 2 + lo_) * 2 + y_, "tensor": x_ * 2 + c_}

    to_x = device(x_=1 - x)
    to_c = device(c_=1 - c)
    to_lo = device(lo_=1 - lo)
    to_y = device(y_=1 - y)
    to_hi = device(hi_=1 - hi)
    to_hilo = device(hi_=1 - hi, lo_=1 - lo)
    partners = [to_x, to_c, to_lo, to_y, to_hi, to_hilo]

    mult = pl.multiple_of

    n_copies = [0]
    n_local = [0]
    pending = []

    class Send:
        def __init__(self, src, dst, dev):
            i = n_copies[0]
            n_copies[0] += 1
            self.d = pltpu.make_async_remote_copy(
                src_ref=src, dst_ref=dst, send_sem=ssem.at[i], recv_sem=rsem.at[i],
                device_id=dev, device_id_type=pl.DeviceIdType.MESH,
            )
            self.open = False
            self.arrived = False

        def start(self):
            self.d.start()
            self.open = True
            pending.append(self)

        def got(self):
            if not self.arrived:
                self.d.wait_recv()
            self.arrived = True

        def done(self):
            if self.open:
                self.d.wait_send()
            self.open = False

    class Local:
        def __init__(self, src, dst):
            i = n_local[0]
            n_local[0] += 1
            self.d = pltpu.make_async_copy(src, dst, lsem.at[i])
            self.d.start()
            self.open = True

        def done(self):
            if self.open:
                self.d.wait()
            self.open = False

    sends = {}

    def got(*names):
        for n in names:
            sends[n].got()

    def start(*names):
        for n in names:
            sends[n].start()

    steps = {}

    def col(p, low):
        return mult(p * 2 * R + low * R, R)

    def abs_block(p, low):
        hi_ = hi if p < 2 else 1 - hi
        y_ = y if p % 2 == 0 else 1 - y
        return mult(((hi_ * 2 + low) * 2 + y_) * R, R)

    pieces = [(p, low) for p in range(4) for low in range(2)]

    def piece_cols(p, low):
        return slice(p * 2 * R + low * R, p * 2 * R + (low + 1) * R)

    def piece_ds(p, low):
        return pl.ds(p * 2 * R + low * R, R)

    def row(low, xx, cc):
        return mult((low * 4 + xx * 2 + cc) * T, T)

    own_row = row(lo, x, c)
    own_rows = pl.ds(own_row, T)

    tok_loads, cot_loads = [], []
    for p, low in pieces:
        src = pl.ds(abs_block(p, low), R)
        tok_loads.append(Local(tokens.at[:, src], RING.at[0, :, piece_ds(p, low)]))
    for p, low in pieces:
        src = pl.ds(abs_block(p, low), R)
        cot_loads.append(Local(cot.at[:, src], G.at[own_rows, piece_ds(p, low)]))

    own_weights = {}

    def weight(w, src, land):
        own_weights[w] = Local(src(lo), land(0, lo))
        sends[w + "a"] = Send(src(1 - lo), land(0, lo), to_lo)
        sends[w + "c"] = Send(src(lo), land(2, lo), to_hi)
        sends[w + "e"] = Send(src(1 - lo), land(2, lo), to_hilo)
        sends[w + "d"] = Send(src(lo), land(1, lo), to_y)
        sends[w + "f"] = Send(land(0, 1 - lo), land(1, 1 - lo), to_y)
        sends[w + "g"] = Send(land(2, lo), land(3, lo), to_y)
        sends[w + "h"] = Send(land(2, 1 - lo), land(3, 1 - lo), to_y)
        for n in "aced":
            steps["s:" + w + n] = functools.partial(start, w + n)
        for n, before in (("f", "a"), ("g", "c"), ("h", "e")):
            steps["r:" + w + n] = functools.partial(relay, w + before, w + n)

    def relay(before, *after):
        got(before)
        start(*after)

    def weight_ready(*ws):
        for w in ws:
            own_weights[w].done()
            got(w + "d", w + "f", w + "g", w + "h")

    weight(
        "U0",
        lambda h: wu_in.at[:, pl.ds(mult(h * F, F), F)],
        lambda p, low: WU.at[pl.ds(col(p, low), R), :],
    )
    weight(
        "Q",
        lambda h: wq_in.at[:, :, pl.ds(mult(h * H, H), H)],
        lambda p, low: WQ.at[:, pl.ds(col(p, low), R), :],
    )
    weight(
        "O",
        lambda h: wo_in.at[pl.ds(mult(h * H, H), H), :],
        lambda p, low: WO.at[:, pl.ds(col(p, low), R)],
    )
    weight(
        "D0",
        lambda h: wd_in.at[pl.ds(mult(h * F, F), F), :],
        lambda p, low: WD.at[:, pl.ds(col(p, low), R)],
    )

    def rows_over(r, buf):
        def at(low, xx):
            return buf.at[pl.ds(row(low, xx, c), T), :]

        sends[r + "lo"] = Send(at(lo, x), at(lo, x), to_lo)
        sends[r + "x"] = Send(at(lo, x), at(lo, x), to_x)
        sends[r + "xlo"] = Send(at(1 - lo, x), at(1 - lo, x), to_x)
        sends[r + "c"] = Send(at(lo, x), at(lo, x), to_c)
        sends[r + "clo"] = Send(at(1 - lo, x), at(1 - lo, x), to_c)
        sends[r + "cx"] = Send(at(lo, 1 - x), at(lo, 1 - x), to_c)
        sends[r + "cxlo"] = Send(at(1 - lo, 1 - x), at(1 - lo, 1 - x), to_c)
        steps["r:" + r + "xlo"] = functools.partial(relay, r + "lo", r + "xlo", r + "clo")
        steps["r:" + r + "cx"] = functools.partial(relay, r + "x", r + "cx")
        steps["r:" + r + "cxlo"] = functools.partial(relay, r + "xlo", r + "cxlo")

    rows_over("N", XN)
    rows_over("G", G)

    def rows_ready(*rs):
        for r in rs:
            got(r + "c", r + "clo", r + "cx", r + "cxlo")

    def start_g(n):
        for ld in cot_loads:
            ld.done()
        start("G" + n)

    for n in ("lo", "x", "c"):
        steps["s:N" + n] = functools.partial(start, "N" + n)
        steps["s:G" + n] = functools.partial(start_g, n)

    def normalise(k, sub):
        activ = RING[k, sub, :].astype(f32)
        average = jnp.mean(activ, axis=1, keepdims=True)
        centered = activ - average
        variance = jnp.mean(centered * centered, axis=1, keepdims=True)
        inv_std = lax.rsqrt(variance + epsilon)
        return centered * inv_std, inv_std

    def sub_rows(i):
        return pl.ds(mult(i * LN_ROWS, LN_ROWS), LN_ROWS)

    def step_ln():
        for p, low in pieces:
            src = pl.ds(abs_block(p, low), R)
            VEC[0:1, piece_ds(p, low)] = gain[:, src]
            VEC[1:2, piece_ds(p, low)] = shift[:, src]
            VEC[2:3, piece_ds(p, low)] = out_bias[:, src]
        for ld in tok_loads:
            ld.done()

        def body(i, _):
            x_hat, _unused = normalise(0, sub_rows(i))
            XN[pl.ds(mult(own_row + i * LN_ROWS, LN_ROWS), LN_ROWS), :] = (
                x_hat * VEC[0:1, :] + VEC[1:2, :]
            ).astype(bf16)

        lax.fori_loop(0, T // LN_ROWS, body, None)

    steps["ln"] = step_ln

    def tiles(first, stop, body):
        lax.fori_loop(first, stop, lambda i, _: body(pl.ds(mult(i * T, T), T)), None)

    def step_hid(first, stop):
        weight_ready("U0")
        rows_ready("N")

        def body(rows):
            xn = XN[rows, :]
            for m in range(0, F, R):
                cols = slice(m, m + R)
                bias = bu_in[:, pl.ds(mult(lo * F + m, R), R)]
                h = dot(xn, WU[:, cols], NN) + bias
                act, slope = gelu_both(h)
                ACT[rows, cols] = act.astype(bf16)
                DH[rows, cols] = slope.astype(bf16)

        tiles(first, stop, body)

    steps["hid00"] = functools.partial(step_hid, 0, 4)
    steps["hid01"] = functools.partial(step_hid, 4, 8)

    def step_dh(first, stop):
        weight_ready("D0")
        rows_ready("G")
        if first == 0:
            VEC[3:4, 0:F] = jnp.zeros((1, F), f32)

        def body(rows):
            gg = G[rows, :]
            for m in range(0, F, R):
                cols = slice(m, m + R)
                dh = (dot(gg, WD[cols, :], NT) * DH[rows, cols].astype(f32)).astype(bf16)
                DH[rows, cols] = dh
                VEC[3:4, cols] += jnp.sum(dh.astype(f32), axis=0, keepdims=True)

        tiles(first, stop, body)

    steps["dh00"] = functools.partial(step_dh, 0, 4)
    steps["dh01"] = functools.partial(step_dh, 4, 8)

    Q, DA = 0, 1

    def seq_row(s, off):
        return mult((1 - lo if s == 0 else lo) * LEN + off, Q_BLOCK)

    def head_rows(which, begin, cc):
        cols = pl.ds(mult(begin // T * H + cc, LANES), LANES)
        return YS[1, which, begin % T : begin % T + Q_BLOCK, cols]

    def step_proj(s):
        weight_ready("Q", "O")
        rows_ready("N", "G")

        def body(i, _):
            pos = pl.ds(mult(i * T, T), T)
            rows = pl.ds(mult(seq_row(s, 0) + i * T, T), T)
            cs, sn = cos_t[pos, :], sin_t[pos, :]

            def turned(v):
                return [
                    rotate(v[:, a : a + LANES], cs, sn).astype(bf16) for a in range(0, H, LANES)
                ]

            def put(which, vs):
                for n, u in enumerate(vs):
                    YS[1, which, :, pl.ds(mult(i * H + n * LANES, LANES), LANES)] = u

            xn = XN[rows, :]

            def part(k):
                return dot(xn, WQ[k], NN) + bq_in[k : k + 1, pl.ds(mult(lo * H, LANES), H)]

            put(Q, turned(part(0)))
            for n, u in enumerate(turned(part(1))):
                KS[pos, n * LANES : (n + 1) * LANES] = u
            VS[pos, :] = part(2).astype(bf16)
            d_att = dot(G[rows, :], WO[...], NT).astype(bf16)
            put(DA, [d_att[:, a : a + LANES] for a in range(0, H, LANES)])

        lax.fori_loop(0, 4, body, None)

    def step_att(s, first_pair, n_pairs):
        first = lax.broadcasted_iota(jnp.int32, (Q_BLOCK, LANES), 1) < HEAD_DIM
        scaling = HEAD_DIM**-0.5

        def split(v):
            zero = jnp.zeros_like(v)
            return jnp.concatenate([jnp.where(first, v, zero), jnp.where(first, zero, v)], axis=0)

        def join(v):
            return jnp.where(first, v[:Q_BLOCK], v[Q_BLOCK:])

        def pair(hp, _):
            cc = hp * LANES
            out_cols = pl.ds(mult(cc, LANES), LANES)
            for i in range(LEN // Q_BLOCK):
                rr = pl.ds(i * Q_BLOCK, Q_BLOCK)
                out_rows = pl.ds(seq_row(s, i * Q_BLOCK), Q_BLOCK)
                n = (i + 1) * Q_BLOCK
                old = n - Q_BLOCK
                qm = split(head_rows(Q, old, cc))
                dm = split(head_rows(DA, old, cc))
                kk = KS[0:n, out_cols]
                vv = VS[0:n, out_cols]
                st = dot(kk, qm * jnp.asarray(scaling, bf16), NT)
                kpos = lax.broadcasted_iota(jnp.int32, (Q_BLOCK, 2 * Q_BLOCK), 0)
                qpos = lax.broadcasted_iota(jnp.int32, (Q_BLOCK, 2 * Q_BLOCK), 1)
                qpos = jnp.where(qpos < Q_BLOCK, qpos, qpos - Q_BLOCK)
                diagonal = jnp.where(kpos <= qpos, st[old:], big_negative)
                st = diagonal if i == 0 else jnp.concatenate([st[:old], diagonal], axis=0)
                ex = jnp.exp(st - jnp.max(st, axis=0, keepdims=True))
                prob = ex * (1.0 / jnp.sum(ex, axis=0, keepdims=True))
                pb = prob.astype(bf16)
                ATT[out_rows, out_cols] = join(dot(pb, vv, TN)).astype(bf16)
                dv = dot(pb, dm, NN)
                dprob = dot(vv, dm * jnp.asarray(scaling, bf16), NT)
                centre = jnp.sum(dprob * prob, axis=0, keepdims=True)
                ds = (prob * (dprob - centre)).astype(bf16)
                dq = join(dot(ds, kk, TN))
                DP[out_rows, out_cols] = rotate(dq, cos_t[rr, :], -sin_t[rr, :]).astype(bf16)
                dk = dot(ds, qm, NN)
                if i > 0:
                    DK[0:old, :] += dk[:old]
                    DV[0:old, :] += dv[:old]
                DK[rr, :] = dk[old:]
                DV[rr, :] = dv[old:]
            seq = pl.ds(seq_row(s, 0), LEN)
            DP[seq, pl.ds(mult(H + cc, LANES), LANES)] = rotate(
                DK[...], cos_t[...], -sin_t[...]
            ).astype(bf16)
            DP[seq, pl.ds(mult(2 * H + cc, LANES), LANES)] = DV[...].astype(bf16)

        lax.fori_loop(first_pair, first_pair + n_pairs, pair, None)

    half_pairs = H // LANES // 2
    for s in range(2):
        steps["proj%d" % s] = functools.partial(step_proj, s)
        if half_pairs:
            steps["att%d0" % s] = functools.partial(step_att, s, 0, half_pairs)
            steps["att%d1" % s] = functools.partial(step_att, s, half_pairs, half_pairs)
            steps["att%d" % s] = functools.partial(step_att, s, 0, 2 * half_pairs)
        else:
            steps["att%d0" % s] = functools.partial(step_att, s, 0, 1)
            steps["att%d1" % s] = lambda: None
            steps["att%d" % s] = steps["att%d0" % s]

    ff_use = {0: [], 1: []}

    def ff_free(*which):
        for k in which:
            for ld in ff_use[k]:
                ld.done()
            ff_use[k] = []

    def cols_of(p, q):
        return pl.ds(col(p, lo if q == 0 else 1 - lo), R)

    def block_dn(p, q):
        gg = G[:, cols_of(p, q)]
        return [(m, dot(ACT[:, m : m + R], gg, TN)) for m in range(0, F, R)]

    def block_up(p, q):
        return [(0, dot(XN[:, cols_of(p, q)], DH[...], TN))]

    def block_at(p, q):
        cc = cols_of(p, q)
        return [(0, dot(XN[:, cc], DP[...], TN)), (3 * H, dot(ATT[...], G[:, cc], TN))]

    def weight_grad(g, i, block, needs):
        def slot(p, q):
            return (0 if p >= 2 else 2) + (1 - q)

        def pq(p, q):
            return "%d%d" % (p, q)

        for p, q in ((3, 1), (3, 0), (1, 1), (1, 0)):
            k = slot(p, q)
            sends["y" + g + pq(p, q)] = Send(YS.at[i, k], ry.at[i, k], to_y)
        sends["m" + g + "0"] = Send(YS.at[i, slot(3, 0)], rm.at[i, 0], to_hi)
        sends["m" + g + "1"] = Send(YS.at[i, slot(3, 1)], rm.at[i, 1], to_hilo)
        sends["l" + g] = Send(YS.at[i, slot(1, 1)], rl.at[i], to_lo)

        def near(p, q):
            needs()
            k = slot(p, q)
            for off, v in block(p, q):
                YS[i, k, :, off : off + v.shape[1]] = v.astype(bf16)
            start("y" + g + pq(p, q))

        def pass_on(p, q, then):
            k = slot(p, q)
            came = "y" + g + pq(p + 1, q)
            got(came)
            load = Local(ry.at[i, k], LD.at[0, 0:R, 0:F])
            vals = block(p, q)
            sends[came].done()
            load.done()
            for off, v in vals:
                cols = slice(off, off + v.shape[1])
                YS[i, k, :, cols] = (v + LD[0, 0:R, cols].astype(f32)).astype(bf16)
            start(then)

        def fin():
            ff_free(0)
            got("y" + g + "10")
            load = Local(ry.at[i, slot(0, 0)], LD.at[0, 0:R, 0:F])
            vals = block(0, 0)
            load.done()
            for off, v in vals:
                cols = slice(off, off + v.shape[1])
                FF[0, :, cols] = v + LD[0, 0:R, cols].astype(f32)
            ff_use[0] = [Local(FF.at[0], o_part.at[i])]

        for p, q in ((3, 1), (3, 0), (1, 1), (1, 0)):
            steps["near:" + g + pq(p, q)] = functools.partial(near, p, q)
        for q in range(2):
            steps["far:" + g + str(q)] = functools.partial(pass_on, 2, q, "m" + g + str(q))
        steps["swap:" + g] = functools.partial(pass_on, 0, 1, "l" + g)
        steps["fin:" + g] = fin

    weight_grad("D0", 0, block_dn, lambda: rows_ready("G"))
    weight_grad("A", 1, block_at, lambda: None)
    weight_grad("U0", 2, block_up, lambda: None)

    def rows_out(rr, cc):
        return dot(ACT[rr, :], WD[:, cc], NN) + dot(ATT[rr, :], WO[:, cc], NN)

    def rows_dn(rr, cc):
        v = dot(DH[rr, :], WU[cc, :], NT)
        for k in range(3):
            v = v + dot(DP[rr, k * H : (k + 1) * H], WQ[k, cc, :], NT)
        return v

    ring_use = {0: None, 1: None, 2: None}
    ring_next = [0]

    def ring_slot():
        k = ring_next[0]
        ring_next[0] = (k + 1) % 3
        if ring_use[k] is not None:
            ring_use[k].done()
            ring_use[k] = None
        return k

    def load_tokens():
        k = ring_slot()
        return k, [
            Local(tokens.at[:, pl.ds(abs_block(p, low), R)], RING.at[k, :, piece_ds(p, low)])
            for p, low in pieces
        ]

    def own_sub(sub):
        return jnp.concatenate([FF[0, sub, :], FF[1, sub, :]], axis=1) + LD[0, sub, :].astype(f32)

    def finish_out(k_tok):
        k = ring_slot()

        def body(i, _):
            sub = sub_rows(i)
            RING[k, sub, :] = (
                RING[k_tok, sub, :].astype(f32) + own_sub(sub) + VEC[2:3, :]
            ).astype(bf16)

        lax.fori_loop(0, T // LN_ROWS, body, None)
        stores = [
            Local(RING.at[k, :, piece_ds(p, low)], o_out.at[:, pl.ds(abs_block(p, low), R)])
            for p, low in pieces
        ]
        for st in stores:
            st.done()

    def finish_dn(k_tok):
        VEC[4:6, :] = jnp.zeros((2, D), f32)

        def body(i, _):
            sub = sub_rows(i)
            x_hat, inv_std = normalise(k_tok, sub)
            dn = own_sub(sub)
            VEC[4:5, :] += jnp.sum(dn * x_hat, axis=0, keepdims=True)
            VEC[5:6, :] += jnp.sum(dn, axis=0, keepdims=True)
            scaled = dn * VEC[0:1, :]
            gt = (
                inv_std
                * (
                    scaled
                    - jnp.mean(scaled, axis=1, keepdims=True)
                    - x_hat * jnp.mean(scaled * x_hat, axis=1, keepdims=True)
                )
                + G[pl.ds(mult(own_row + i * LN_ROWS, LN_ROWS), LN_ROWS), :].astype(f32)
            )
            FF[0, sub, :] = gt[:, :half_d]
            FF[1, sub, :] = gt[:, half_d:]

        lax.fori_loop(0, T // LN_ROWS, body, None)
        for p, low in pieces:
            dst = pl.ds(abs_block(p, low), R)
            src = pl.ds((p % 2) * 2 * R + low * R, R)
            ff_use[p // 2].append(Local(FF.at[p // 2, :, src], o_gt.at[:, dst]))

    def owners(w, i, partial, needs, finish):
        def chunks(low, xx, cc, loads, store):
            rr = pl.ds(row(low, xx, cc), T)
            for ld in loads:
                ld.done()

            def body(j, _):
                cols = pl.ds(mult(j * CHUNK, CHUNK), CHUNK)
                v = partial(rr, cols)
                for k in range(len(loads)):
                    v = v + LD[k, :, cols].astype(f32)
                store(j, cols, v)

            lax.fori_loop(0, D // CHUNK, body, None)

        def put(name, low, xx, cc, srcs, dst, dev):
            needs()
            loads = [Local(src, LD.at[k]) for k, src in enumerate(srcs)]
            k = ring_slot()

            def store(j, cols, v):
                RING[k, :, cols] = v.astype(bf16)

            chunks(low, xx, cc, loads, store)
            sends[name] = Send(RING.at[k], dst, dev)
            start(name)
            ring_use[k] = sends[name]

        def core(dlo, dx):
            low = lo if dlo == 0 else 1 - lo
            xx = x if dx == 0 else 1 - x
            name = "c%s%d%d" % (w, dlo, dx)
            put(name, low, xx, 1 - c, [], rc.at[i, 2 * dlo + dx], to_c)

        def cross(dlo):
            low = lo if dlo == 0 else 1 - lo
            got("c%s%d1" % (w, dlo))
            name = "x%s%d" % (w, dlo)
            put(name, low, 1 - x, c, [rc.at[i, 2 * dlo + 1]], rx.at[i, dlo], to_x)

        def level():
            got("c%s10" % w, "x%s1" % w)
            put("l" + w, 1 - lo, x, c, [rc.at[i, 2], rx.at[i, 1]], rr_lo.at[i], to_lo)

        def own():
            k_tok, tok_ld = load_tokens()
            got("c%s00" % w, "x%s0" % w)
            loads = [Local(rc.at[i, 0], LD.at[0]), Local(rx.at[i, 0], LD.at[1])]
            ff_free(0, 1)
            n = D // CHUNK // 2

            def store(j, cols, v):
                part = pl.ds(mult(lax.rem(j, n) * CHUNK, CHUNK), CHUNK)
                FF[lax.div(j, n), :, part] = v

            chunks(lo, x, c, loads, store)
            got("l" + w)
            Local(rr_lo.at[i], LD.at[0]).done()
            for ld in tok_ld:
                ld.done()
            finish(k_tok)

        for dlo in range(2):
            for dx in range(2):
                steps["core:%s%d%d" % (w, dlo, dx)] = functools.partial(core, dlo, dx)
            steps["cross:%s%d" % (w, dlo)] = functools.partial(cross, dlo)
        steps["level:" + w] = level
        steps["own:" + w] = own

    owners("o", 0, rows_out, lambda: weight_ready("D0"), finish_out)
    owners("n", 1, rows_dn, lambda: None, finish_dn)

    stage_dev = (to_y, to_hi, to_lo, to_x, to_c)
    for k in range(5):
        sends["v%d" % k] = Send(SV, SR.at[k], stage_dev[k])
        sends["w%d" % k] = Send(SA, SRA.at[k], stage_dev[k])
    abs_d = {pc: lax.div(abs_block(*pc), R) for pc in pieces}

    def step_vec():
        SV[...] = jnp.zeros_like(SV)
        VEC[6:7, 0 : 3 * H] = jnp.zeros((1, 3 * H), f32)
        VEC[7:8, :] = jnp.zeros((1, D), f32)

        def body(rows):
            VEC[6:7, 0 : 3 * H] += jnp.sum(DP[rows, :].astype(f32), axis=0, keepdims=True)

        tiles(0, ROWS // T, body)

        def g_body(i, _):
            rows = pl.ds(mult(own_row + i * LN_ROWS, LN_ROWS), LN_ROWS)
            VEC[7:8, :] += jnp.sum(G[rows, :].astype(f32), axis=0, keepdims=True)

        lax.fori_loop(0, T // LN_ROWS, g_body, None)
        for pc in pieces:
            at = pl.ds(mult(lax.rem(abs_d[pc], 4) * R, R), R)
            SV[pl.ds(lax.div(abs_d[pc], 4), 1), at] = VEC[7:8, piece_cols(*pc)]
        SV[pl.ds(2 + lo, 1), :] = VEC[3:4, 0:F]
        for k in range(3):
            SV[4 + k : 5 + k, pl.ds(mult(lo * H, LANES), H)] = VEC[6:7, k * H : (k + 1) * H]
        start("v0")

    def step_v(k):
        got("v%d" % (k - 1))
        sends["v%d" % (k - 1)].done()
        if k <= 3:
            SV[...] += SR[k - 1]
        else:
            SV[0:2, :] += SR[k - 1, 0:2, :]
        if k < 5:
            start("v%d" % k)
        else:
            o_vec[2:3, 0:half_d] = SV[0:1, :]
            o_vec[2:3, half_d:] = SV[1:2, :]
            o_vec[3:4, 0:half_d] = SV[2:3, :]
            o_vec[3:4, half_d:] = SV[3:4, :]
            o_vec[4:7, 0:half_d] = SV[4:7, :]

    steps["vec"] = step_vec
    for k in range(1, 6):
        steps["v%d" % k] = functools.partial(step_v, k)

    def step_small():
        quarter = D // 4
        for row_, base in ((4, 0), (5, 4)):
            for pc in pieces:
                at = pl.ds(mult(lax.rem(abs_d[pc], 2) * R, R), R)
                SA[pl.ds(base + lax.div(abs_d[pc], 2), 1), at] = VEC[row_ : row_ + 1, piece_cols(*pc)]
        for k in range(5):
            start("w%d" % k)
            got("w%d" % k)
            sends["w%d" % k].done()
            SA[...] += SRA[k]
        for i in range(4):
            o_vec[0:1, i * quarter : (i + 1) * quarter] = SA[i : i + 1, :]
            o_vec[1:2, i * quarter : (i + 1) * quarter] = SA[4 + i : 5 + i, :]

    steps["small"] = step_small

    barrier = pltpu.get_barrier_semaphore()
    for dev in partners:
        pl.semaphore_signal(barrier, inc=1, device_id=dev, device_id_type=pl.DeviceIdType.MESH)
    pl.semaphore_wait(barrier, len(partners))
    o_vec[...] = jnp.zeros_like(o_vec)
    for name in ORDER:
        steps[name]()
    ff_free(0, 1)
    for s in pending:
        s.got()
        s.done()
    assert n_copies[0] <= ssem.shape[0] and n_local[0] <= lsem.shape[0], (n_copies, n_local)


def finish_kernel(
    b_out, b_gt, b_vec, b_part, rm, rl,
    o_out, o_gt, o_gain, o_shift, o_bias, o_bu, o_bq, o_gq, o_go, o_gu, o_gd,
    PART, RM, RL, OUT, GT, GU, GD, GQ, GO, lsem,
):
    R, F = PART.shape[1:]
    H = o_go.shape[0] // 2
    lo = lax.rem(lax.div(lax.axis_index("dp"), 2), 2)
    mult = pl.multiple_of
    n = [0]

    def copy(src, dst):
        d = pltpu.make_async_copy(src, dst, lsem.at[n[0]])
        n[0] += 1
        d.start()
        return d

    order = (1, 0, 2)
    loads = {i: [copy(b_part.at[i], PART.at[i]), copy(rm.at[i], RM.at[i]), copy(rl.at[i], RL.at[i])] for i in order}
    load_out = copy(b_out, OUT)
    load_gt = copy(b_gt, GT)
    o_gain[...] = b_vec[0:1, :]
    o_shift[...] = b_vec[1:2, :]
    o_bias[...] = b_vec[2:3, :]
    o_bu[...] = b_vec[3:4, 0 : 2 * F]
    o_bq[...] = b_vec[4:7, 0 : 2 * H]
    stores = []

    def halves(i, put):
        for ld in loads[i]:
            ld.wait()
        for m in range(0, F, R):
            cols = slice(m, m + R)
            put(lo, m, PART[i, :, cols] + RM[i, 0, :, cols].astype(f32))
            put(1 - lo, m, RL[i, :, cols].astype(f32) + RM[i, 1, :, cols].astype(f32))

    def put_at(half, m, v):
        if m < 3 * H:
            GQ[m // H, :, pl.ds(mult(half * H, H), H)] = v
        else:
            GO[pl.ds(mult(half * H, H), H), :] = v

    def put_dn(half, m, v):
        GD[pl.ds(mult(half * F + m, R), R), :] = v

    def put_up(half, m, v):
        GU[:, pl.ds(mult(half * F + m, R), R)] = v

    for i, put, pairs in (
        (1, put_at, ((GQ, o_gq), (GO, o_go))), (0, put_dn, ((GD, o_gd),)), (2, put_up, ((GU, o_gu),)),
    ):
        halves(i, put)
        for src, dst in pairs:
            stores.append(copy(src, dst))
    load_out.wait()
    stores.append(copy(OUT, o_out))
    load_gt.wait()
    stores.append(copy(GT, o_gt))
    for st in stores:
        st.wait()


VMEM_LIMIT = 64 << 20


def fast_shards(tokens, ln_gain, ln_bias, w_qkv, b_qkv, w_out, w_up, b_up, w_down, out_bias, cot):
    T, D = tokens.shape
    R, F = w_up.shape[0], w_up.shape[1] // 2
    H = w_out.shape[0] // 2
    cos_t, sin_t = rotary_tables(4 * T)
    S = jax.ShapeDtypeStruct
    hbm = pl.BlockSpec(memory_space=pl.ANY)
    vm = pl.BlockSpec(memory_space=pltpu.VMEM)
    outs = pl.pallas_call(
        block_kernel,
        out_shape=(
            S((T, D), bf16), S((T, D), f32), S((8, D), f32), S((3, R, F), f32),
            S((3, 4, R, F), bf16), S((3, 2, R, F), bf16), S((3, R, F), bf16),
            S((2, 4, T, D), bf16), S((2, 2, T, D), bf16), S((2, T, D), bf16),
        ),
        in_specs=[hbm, hbm, vm, vm, vm, hbm, hbm, hbm, hbm, vm, vm, vm, vm],
        out_specs=(hbm, hbm, vm) + (hbm,) * 7,
        scratch_shapes=[
            pltpu.VMEM((8 * T, D), bf16),
            pltpu.VMEM((8 * T, D), bf16),
            pltpu.VMEM((D, F), bf16),
            pltpu.VMEM((F, D), bf16),
            pltpu.VMEM((3, D, H), bf16),
            pltpu.VMEM((H, D), bf16),
            pltpu.VMEM((8 * T, F), bf16),
            pltpu.VMEM((8 * T, F), bf16),
            pltpu.VMEM((8 * T, H), bf16),
            pltpu.VMEM((8 * T, 3 * H), bf16),
            pltpu.VMEM((4 * T, H), bf16),
            pltpu.VMEM((4 * T, H), bf16),
            pltpu.VMEM((4 * T, LANES), f32),
            pltpu.VMEM((4 * T, LANES), f32),
            pltpu.VMEM((3, 4, R, F), bf16),
            pltpu.VMEM((2, R, F), f32),
            pltpu.VMEM((3, T, D), bf16),
            pltpu.VMEM((2, T, D), bf16),
            pltpu.VMEM((8, D), f32),
            pltpu.VMEM((8, D // 2), f32),
            pltpu.VMEM((5, 8, D // 2), f32),
            pltpu.VMEM((8, D // 4), f32),
            pltpu.VMEM((5, 8, D // 4), f32),
            pltpu.SemaphoreType.DMA((96,)),
            pltpu.SemaphoreType.DMA((96,)),
            pltpu.SemaphoreType.DMA((110,)),
        ],
        compiler_params=pltpu.CompilerParams(
            collective_id=0, has_side_effects=True, vmem_limit_bytes=VMEM_LIMIT
        ),
        name="parallel_block",
    )(
        tokens, cot, ln_gain.reshape(1, D), ln_bias.reshape(1, D), out_bias.reshape(1, D),
        w_qkv.transpose(1, 0, 2), w_out, w_up, w_down, b_qkv, b_up.reshape(1, 2 * F), cos_t, sin_t,
    )
    b_out, b_gt, b_vec, b_part, _, rm, rl = outs[:7]
    done = pl.pallas_call(
        finish_kernel,
        out_shape=(
            S((T, D), bf16), S((T, D), f32), S((1, D), f32), S((1, D), f32), S((1, D), f32),
            S((1, 2 * F), f32), S((3, 2 * H), f32),
            S((3, R, 2 * H), f32), S((2 * H, R), f32), S((R, 2 * F), f32), S((2 * F, R), f32),
        ),
        in_specs=[hbm, hbm, vm, hbm, hbm, hbm],
        out_specs=(hbm, hbm) + (vm,) * 5 + (hbm,) * 4,
        scratch_shapes=[
            pltpu.VMEM((3, R, F), f32),
            pltpu.VMEM((3, 2, R, F), bf16),
            pltpu.VMEM((3, R, F), bf16),
            pltpu.VMEM((T, D), bf16),
            pltpu.VMEM((T, D), f32),
            pltpu.VMEM((R, 2 * F), f32),
            pltpu.VMEM((2 * F, R), f32),
            pltpu.VMEM((3, R, 2 * H), f32),
            pltpu.VMEM((2 * H, R), f32),
            pltpu.SemaphoreType.DMA((20,)),
        ],
        compiler_params=pltpu.CompilerParams(vmem_limit_bytes=VMEM_LIMIT),
        name="finish",
    )(b_out, b_gt, b_vec, b_part, rm, rl)
    o_out, o_gt, o_gain, o_shift, o_bias, o_bu, o_bq, o_gq, o_go, o_gu, o_gd = done
    return (
        o_out, o_gt, o_gain.reshape(D), o_shift.reshape(D), o_gq.transpose(1, 0, 2), o_bq, o_go,
        o_gu, o_bu.reshape(2 * F), o_gd, o_bias.reshape(D),
    )


def plain_tables(row_count):
    half_rot = ROT // 2
    positions = jnp.arange(row_count).astype(jnp.float32)
    freqs = 10000.0 ** (-(2.0 * jnp.arange(half_rot).astype(jnp.float32)) / ROT)
    angles = positions[:, None] * freqs[None, :]
    return (jnp.cos(angles)[:, None, :], jnp.sin(angles)[:, None, :])


def plain_rotate(field, cosines, sines):
    half_rot = ROT // 2
    first = field[..., :half_rot]
    second = field[..., half_rot:ROT]
    return jnp.concatenate(
        [first * cosines - second * sines, second * cosines + first * sines, field[..., ROT:]],
        axis=-1,
    )


def gelu_tanh(values):
    return jax.nn.gelu(values, approximate=True)


def causal_scores(query_block, key_rows, block_index):
    block_len = query_block.shape[0]
    query_pos = block_index * block_len + jnp.arange(block_len)
    key_pos = jnp.arange(key_rows.shape[0])
    raw = jnp.einsum("qhd,khd->hqk", query_block, key_rows, preferred_element_type=jnp.float32)
    scaled = raw * HEAD_DIM ** (-0.5)
    return jnp.where(key_pos[None, None, :] <= query_pos[None, :, None], scaled, big_negative)


def attend_forward(queries, key_rows, value_rows, block_len):
    row_count, heads_here, head_size = queries.shape
    n_blocks = row_count // block_len
    query_blocks = queries.reshape(n_blocks, block_len, heads_here, head_size)

    def one_block(item):
        query_block, block_index = item
        scores = causal_scores(query_block, key_rows, block_index)
        top_score = jnp.max(scores, axis=2, keepdims=True)
        exponent = jnp.exp(scores - top_score)
        totals = jnp.sum(exponent, axis=2, keepdims=True)
        probability = (exponent / totals).astype(jnp.bfloat16)
        attended = jnp.einsum(
            "hqk,khd->qhd", probability, value_rows, preferred_element_type=jnp.float32
        )
        return (attended, (top_score + jnp.log(totals))[:, :, 0])

    attended, logsum = lax.map(one_block, (query_blocks, jnp.arange(n_blocks)))
    return (attended.reshape(row_count, heads_here * head_size), logsum)


def attend_backward(queries, key_rows, value_rows, grad_att, logsum, block_len):
    row_count, heads_here, head_size = queries.shape
    n_blocks = row_count // block_len
    query_blocks = queries.reshape(n_blocks, block_len, heads_here, head_size)
    grad_blocks = grad_att.reshape(n_blocks, block_len, heads_here, head_size)
    scaling = HEAD_DIM ** (-0.5)

    def one_block(carry, item):
        grad_keys, grad_values = carry
        query_block, grad_block, lse_block, block_index = item
        scores = causal_scores(query_block, key_rows, block_index)
        probability = jnp.exp(scores - lse_block[:, :, None])
        grad_probs = jnp.einsum(
            "qhd,khd->hqk", grad_block, value_rows, preferred_element_type=jnp.float32
        )
        centre = jnp.sum(grad_probs * probability, axis=2, keepdims=True)
        grad_scores = (probability * (grad_probs - centre) * scaling).astype(jnp.bfloat16)
        grad_query = jnp.einsum(
            "hqk,khd->qhd", grad_scores, key_rows, preferred_element_type=jnp.float32
        )
        grad_keys = grad_keys + jnp.einsum(
            "hqk,qhd->khd", grad_scores, query_block, preferred_element_type=jnp.float32
        )
        grad_values = grad_values + jnp.einsum(
            "hqk,qhd->khd",
            probability.astype(jnp.bfloat16),
            grad_block,
            preferred_element_type=jnp.float32,
        )
        return ((grad_keys, grad_values), grad_query)

    zero_rows = jnp.zeros(key_rows.shape, jnp.float32)
    (grad_keys, grad_values), grad_queries = lax.scan(
        one_block, (zero_rows, zero_rows), (query_blocks, grad_blocks, logsum, jnp.arange(n_blocks))
    )
    return (grad_queries.reshape(row_count, heads_here, head_size), grad_keys, grad_values)


def plain_shards(tokens, ln_gain, ln_bias, w_qkv, b_qkv, w_out, w_up, b_up, w_down, out_bias, cotangent):
    activ = tokens.astype(jnp.float32)
    average = jnp.mean(activ, axis=1, keepdims=True)
    centered = activ - average
    variance = jnp.mean(centered * centered, axis=1, keepdims=True)
    inv_std = lax.rsqrt(variance + epsilon)
    x_hat = centered * inv_std
    normed = lax.all_gather(
        (x_hat * ln_gain + ln_bias).astype(jnp.bfloat16), "tensor", axis=0, tiled=True
    )
    row_count = normed.shape[0]
    block_len = min(row_count, 512)
    qkv_full, out_full, up_full, down_full = (
        lax.all_gather(w_qkv, "dp", axis=0, tiled=True),
        lax.all_gather(w_out, "dp", axis=1, tiled=True),
        lax.all_gather(w_up, "dp", axis=0, tiled=True),
        lax.all_gather(w_down, "dp", axis=1, tiled=True),
    )
    heads_here = w_qkv.shape[2] // HEAD_DIM
    local_width = heads_here * HEAD_DIM
    head_shape = (row_count, heads_here, HEAD_DIM)
    project = (
        jnp.einsum("td,dcf->tcf", normed, qkv_full, preferred_element_type=jnp.float32) + b_qkv
    )
    cosines, sines = plain_tables(row_count)
    queries = plain_rotate(project[:, 0].reshape(head_shape), cosines, sines).astype(jnp.bfloat16)
    key_rows = plain_rotate(project[:, 1].reshape(head_shape), cosines, sines).astype(jnp.bfloat16)
    value_rows = project[:, 2].reshape(head_shape).astype(jnp.bfloat16)
    attended, logsum = attend_forward(queries, key_rows, value_rows, block_len)
    attended = attended.astype(jnp.bfloat16)
    hidden = jnp.dot(normed, up_full, preferred_element_type=jnp.float32) + b_up
    activated = gelu_tanh(hidden).astype(jnp.bfloat16)
    partial_rows = jnp.dot(attended, out_full, preferred_element_type=jnp.float32) + jnp.dot(
        activated, down_full, preferred_element_type=jnp.float32
    )
    summed = lax.psum_scatter(partial_rows, "tensor", scatter_dimension=0, tiled=True)
    output = (activ + summed + out_bias).astype(jnp.bfloat16)
    grad_local = cotangent.astype(jnp.float32)
    grad_rows = lax.all_gather(cotangent, "tensor", axis=0, tiled=True)
    grad_down = jnp.einsum("tf,td->fd", activated, grad_rows, preferred_element_type=jnp.float32)
    grad_act = jnp.einsum("td,fd->tf", grad_rows, down_full, preferred_element_type=jnp.float32)
    gelu_pull = jax.vjp(gelu_tanh, hidden)[1]
    grad_hidden = gelu_pull(grad_act)[0].astype(jnp.bfloat16)
    grad_up = jnp.einsum("td,tf->df", normed, grad_hidden, preferred_element_type=jnp.float32)
    grad_b_up = jnp.sum(grad_hidden.astype(jnp.float32), axis=0)
    grad_normed = jnp.einsum("tf,df->td", grad_hidden, up_full, preferred_element_type=jnp.float32)
    grad_out = jnp.einsum("tf,td->fd", attended, grad_rows, preferred_element_type=jnp.float32)
    grad_att = jnp.einsum(
        "td,fd->tf", grad_rows, out_full, preferred_element_type=jnp.float32
    ).astype(jnp.bfloat16)
    grad_queries, grad_keys, grad_values = attend_backward(
        queries, key_rows, value_rows, grad_att.reshape(head_shape), logsum, block_len
    )
    grad_q_pre = plain_rotate(grad_queries, cosines, -sines).reshape(row_count, local_width)
    grad_k_pre = plain_rotate(grad_keys, cosines, -sines).reshape(row_count, local_width)
    grad_project = jnp.stack(
        [grad_q_pre, grad_k_pre, grad_values.reshape(row_count, local_width)], axis=1
    ).astype(jnp.bfloat16)
    grad_qkv = jnp.einsum("td,tcf->dcf", normed, grad_project, preferred_element_type=jnp.float32)
    grad_b_qkv = jnp.sum(grad_project.astype(jnp.float32), axis=0)
    grad_normed = grad_normed + jnp.einsum(
        "tcf,dcf->td", grad_project, qkv_full, preferred_element_type=jnp.float32
    )
    grad_ln_out = lax.psum_scatter(grad_normed, "tensor", scatter_dimension=0, tiled=True)
    qkv_summed, out_summed, up_summed, down_summed = (
        lax.psum_scatter(grad_qkv, "dp", scatter_dimension=0, tiled=True),
        lax.psum_scatter(grad_out, "dp", scatter_dimension=1, tiled=True),
        lax.psum_scatter(grad_up, "dp", scatter_dimension=0, tiled=True),
        lax.psum_scatter(grad_down, "dp", scatter_dimension=1, tiled=True),
    )
    scaled_grad = grad_ln_out * ln_gain
    grad_tokens = (
        inv_std
        * (
            scaled_grad
            - jnp.mean(scaled_grad, axis=1, keepdims=True)
            - x_hat * jnp.mean(scaled_grad * x_hat, axis=1, keepdims=True)
        )
        + grad_local
    )
    gain_grad, shift_grad, bias_grad = lax.psum(
        (
            jnp.sum(grad_ln_out * x_hat, axis=0),
            jnp.sum(grad_ln_out, axis=0),
            jnp.sum(grad_local, axis=0),
        ),
        ("dp", "tensor"),
    )
    qkv_bias_grad, up_bias_grad = lax.psum((grad_b_qkv, grad_b_up), "dp")
    return (
        output,
        grad_tokens,
        gain_grad,
        shift_grad,
        qkv_summed,
        qkv_bias_grad,
        out_summed,
        up_summed,
        up_bias_grad,
        down_summed,
        bias_grad,
    )


def solution(mesh):
    placed = (
        P(("dp", "tensor"), None),
        P(),
        P(),
        P("dp", None, "tensor"),
        P(None, "tensor"),
        P("tensor", "dp"),
        P("dp", "tensor"),
        P("tensor"),
        P("tensor", "dp"),
        P(),
        P(("dp", "tensor"), None),
    )
    results = (
        P(("dp", "tensor"), None),
        P(("dp", "tensor"), None),
        P(),
        P(),
        P("dp", None, "tensor"),
        P(None, "tensor"),
        P("tensor", "dp"),
        P("dp", "tensor"),
        P("tensor"),
        P("tensor", "dp"),
        P(),
    )
    one_kernel = mesh.shape["dp"] == 8 and mesh.shape["tensor"] == 4
    return jax.shard_map(
        fast_shards if one_kernel else plain_shards,
        mesh=mesh,
        in_specs=placed,
        out_specs=results,
        check_vma=False,
    )
```

```python
import functools
import math

import jax
import jax.numpy as jnp
import numpy as np
from jax import lax
from jax.experimental import pallas as pl
from jax.experimental.pallas import tpu as pltpu
from jax.sharding import PartitionSpec as P

HEAD_DIM = 64
ROT = 32
epsilon = 1e-05
big_negative = -1e30

f32 = jnp.float32
bf16 = jnp.bfloat16
NN = (((1,), (0,)), ((), ()))
NT = (((1,), (1,)), ((), ()))
TN = (((0,), (0,)), ((), ()))
dot = functools.partial(lax.dot_general, preferred_element_type=f32)

GELU_A = math.sqrt(2.0 / math.pi)
GELU_B = 0.044715
CHUNK = 1024
Q_BLOCK = 128
LANES = 128


def gelu_both(h):
    square = h * h
    t = jnp.tanh(h * (GELU_A + (GELU_A * GELU_B) * square))
    half = 0.5 * (1.0 + t)
    slope = half + (0.5 * h) * (1.0 - t * t) * (GELU_A + (3.0 * GELU_A * GELU_B) * square)
    return h * half, slope


def rotary_tables(row_count):
    half_rot = ROT // 2
    positions = np.arange(row_count, dtype=np.float32)
    freqs = np.float32(10000.0) ** (-(2.0 * np.arange(half_rot, dtype=np.float32)) / np.float32(ROT))
    angles = positions[:, None] * freqs.astype(np.float32)[None, :]
    cosines, sines = np.cos(angles), np.sin(angles)
    rest = np.zeros((row_count, HEAD_DIM - ROT), np.float32)
    c_head = np.concatenate([cosines, cosines, rest + 1.0], axis=1)
    s_head = np.concatenate([-sines, sines, rest], axis=1)
    pair = lambda t: np.concatenate([t, t], axis=1).astype(np.float32)
    return pair(c_head), pair(s_head)


def rotate(field, cosines, sines):
    half = ROT // 2
    lane = lax.broadcasted_iota(jnp.int32, field.shape, 1)
    first = lax.rem(lane, HEAD_DIM) < half
    partner = jnp.where(
        first, pltpu.roll(field, LANES - half, 1), pltpu.roll(field, half, 1)
    )
    return field * cosines + partner * sines


ORDER = (
    "s:Glo", "ln", "s:Od", "s:Gx", "s:Nc", "s:Qc", "s:Oc", "r:Qg", "r:Og", "s:D0d", "s:U0e",
    "s:Nx", "s:U0d", "s:Nlo", "s:Qd", "r:Ncx", "s:U0c", "r:U0h", "r:Gxlo", "r:U0g", "s:U0a",
    "r:Nxlo", "r:Gcxlo", "s:Oe", "r:Oh", "s:Gc", "r:Gcx", "s:Qe", "r:U0f", "s:Oa", "r:Ncxlo",
    "s:Qa", "r:Of", "r:Qh", "hid00", "s:D0e", "r:Qf", "hid01", "near:D011", "s:D0a", "near:D030",
    "proj0", "s:D0c", "att00", "near:D031", "att01", "far:D00", "r:D0h", "r:D0f", "swap:D0",
    "r:D0g", "far:D01", "proj1", "att10", "att11", "near:A30", "core:o11", "core:o01", "cross:o1",
    "core:o10", "far:A0", "dh00", "near:A10", "dh01", "core:n11", "level:o", "near:U031", "vec",
    "cross:n1", "core:n10", "near:U010", "near:A31", "v1", "fin:A", "far:U01", "near:U030",
    "near:U011", "v2", "core:n01", "core:o00", "level:n", "cross:o0", "v3", "fin:U0", "near:A11",
    "far:A1", "cross:n0", "v4", "near:D010", "swap:U0", "far:U00", "core:n00", "v5", "own:o",
    "swap:A", "fin:D0", "own:n", "small",
)


def block_kernel(
    tokens, cot, gain, shift, out_bias, wq_in, wo_in, wu_in, wd_in, bq_in, bu_in, cos_t, sin_t,
    o_out, o_gt, o_vec, o_part, ry, rm, rl, rc, rx, rr_lo,
    XN, G, WU, WD, WQ, WO, ACT, DH, ATT, DP, KS, VS, DK, DV, YS, FF, RING, LD, VEC, SV, SR, SA, SRA,
    ssem, rsem, lsem,
):
    T, D = tokens.shape
    R = wu_in.shape[0]
    F = wu_in.shape[1] // 2
    H = wo_in.shape[0] // 2
    ROWS = 8 * T
    LEN = 4 * T
    half_d = D // 2
    LN_ROWS = min(T, 64)

    dp = lax.axis_index("dp")
    tp = lax.axis_index("tensor")
    hi = lax.div(dp, 4)
    lo = lax.rem(lax.div(dp, 2), 2)
    y = lax.rem(dp, 2)
    x = lax.div(tp, 2)
    c = lax.rem(tp, 2)

    def device(hi_=hi, lo_=lo, y_=y, x_=x, c_=c):
        return {"dp": (hi_ * 2 + lo_) * 2 + y_, "tensor": x_ * 2 + c_}

    to_x = device(x_=1 - x)
    to_c = device(c_=1 - c)
    to_lo = device(lo_=1 - lo)
    to_y = device(y_=1 - y)
    to_hi = device(hi_=1 - hi)
    to_hilo = device(hi_=1 - hi, lo_=1 - lo)
    partners = [to_x, to_c, to_lo, to_y, to_hi, to_hilo]

    mult = pl.multiple_of

    n_copies = [0]
    n_local = [0]
    pending = []

    class Send:
        def __init__(self, src, dst, dev):
            i = n_copies[0]
            n_copies[0] += 1
            self.d = pltpu.make_async_remote_copy(
                src_ref=src, dst_ref=dst, send_sem=ssem.at[i], recv_sem=rsem.at[i],
                device_id=dev, device_id_type=pl.DeviceIdType.MESH,
            )
            self.open = False
            self.arrived = False

        def start(self):
            self.d.start()
            self.open = True
            pending.append(self)

        def got(self):
            if not self.arrived:
                self.d.wait_recv()
            self.arrived = True

        def done(self):
            if self.open:
                self.d.wait_send()
            self.open = False

    class Local:
        def __init__(self, src, dst):
            i = n_local[0]
            n_local[0] += 1
            self.d = pltpu.make_async_copy(src, dst, lsem.at[i])
            self.d.start()
            self.open = True

        def done(self):
            if self.open:
                self.d.wait()
            self.open = False

    sends = {}

    def got(*names):
        for n in names:
            sends[n].got()

    def start(*names):
        for n in names:
            sends[n].start()

    steps = {}

    def col(p, low):
        return mult(p * 2 * R + low * R, R)

    def abs_block(p, low):
        hi_ = hi if p < 2 else 1 - hi
        y_ = y if p % 2 == 0 else 1 - y
        return mult(((hi_ * 2 + low) * 2 + y_) * R, R)

    pieces = [(p, low) for p in range(4) for low in range(2)]

    def piece_cols(p, low):
        return slice(p * 2 * R + low * R, p * 2 * R + (low + 1) * R)

    def piece_ds(p, low):
        return pl.ds(p * 2 * R + low * R, R)

    def row(low, xx, cc):
        return mult((low * 4 + xx * 2 + cc) * T, T)

    own_row = row(lo, x, c)
    own_rows = pl.ds(own_row, T)

    tok_loads, cot_loads = [], []
    for p, low in pieces:
        src = pl.ds(abs_block(p, low), R)
        tok_loads.append(Local(tokens.at[:, src], RING.at[0, :, piece_ds(p, low)]))
    for p, low in pieces:
        src = pl.ds(abs_block(p, low), R)
        cot_loads.append(Local(cot.at[:, src], G.at[own_rows, piece_ds(p, low)]))

    own_weights = {}

    def weight(w, src, land):
        own_weights[w] = Local(src(lo), land(0, lo))
        sends[w + "a"] = Send(src(1 - lo), land(0, lo), to_lo)
        sends[w + "c"] = Send(src(lo), land(2, lo), to_hi)
        sends[w + "e"] = Send(src(1 - lo), land(2, lo), to_hilo)
        sends[w + "d"] = Send(src(lo), land(1, lo), to_y)
        sends[w + "f"] = Send(land(0, 1 - lo), land(1, 1 - lo), to_y)
        sends[w + "g"] = Send(land(2, lo), land(3, lo), to_y)
        sends[w + "h"] = Send(land(2, 1 - lo), land(3, 1 - lo), to_y)
        for n in "aced":
            steps["s:" + w + n] = functools.partial(start, w + n)
        for n, before in (("f", "a"), ("g", "c"), ("h", "e")):
            steps["r:" + w + n] = functools.partial(relay, w + before, w + n)

    def relay(before, *after):
        got(before)
        start(*after)

    def weight_ready(*ws):
        for w in ws:
            own_weights[w].done()
            got(w + "d", w + "f", w + "g", w + "h")

    weight(
        "U0",
        lambda h: wu_in.at[:, pl.ds(mult(h * F, F), F)],
        lambda p, low: WU.at[pl.ds(col(p, low), R), :],
    )
    weight(
        "Q",
        lambda h: wq_in.at[:, :, pl.ds(mult(h * H, H), H)],
        lambda p, low: WQ.at[:, pl.ds(col(p, low), R), :],
    )
    weight(
        "O",
        lambda h: wo_in.at[pl.ds(mult(h * H, H), H), :],
        lambda p, low: WO.at[:, pl.ds(col(p, low), R)],
    )
    weight(
        "D0",
        lambda h: wd_in.at[pl.ds(mult(h * F, F), F), :],
        lambda p, low: WD.at[:, pl.ds(col(p, low), R)],
    )

    def rows_over(r, buf):
        def at(low, xx):
            return buf.at[pl.ds(row(low, xx, c), T), :]

        sends[r + "lo"] = Send(at(lo, x), at(lo, x), to_lo)
        sends[r + "x"] = Send(at(lo, x), at(lo, x), to_x)
        sends[r + "xlo"] = Send(at(1 - lo, x), at(1 - lo, x), to_x)
        sends[r + "c"] = Send(at(lo, x), at(lo, x), to_c)
        sends[r + "clo"] = Send(at(1 - lo, x), at(1 - lo, x), to_c)
        sends[r + "cx"] = Send(at(lo, 1 - x), at(lo, 1 - x), to_c)
        sends[r + "cxlo"] = Send(at(1 - lo, 1 - x), at(1 - lo, 1 - x), to_c)
        steps["r:" + r + "xlo"] = functools.partial(relay, r + "lo", r + "xlo", r + "clo")
        steps["r:" + r + "cx"] = functools.partial(relay, r + "x", r + "cx")
        steps["r:" + r + "cxlo"] = functools.partial(relay, r + "xlo", r + "cxlo")

    rows_over("N", XN)
    rows_over("G", G)

    def rows_ready(*rs):
        for r in rs:
            got(r + "c", r + "clo", r + "cx", r + "cxlo")

    def start_g(n):
        for ld in cot_loads:
            ld.done()
        start("G" + n)

    for n in ("lo", "x", "c"):
        steps["s:N" + n] = functools.partial(start, "N" + n)
        steps["s:G" + n] = functools.partial(start_g, n)

    def normalise(k, sub):
        activ = RING[k, sub, :].astype(f32)
        average = jnp.mean(activ, axis=1, keepdims=True)
        centered = activ - average
        variance = jnp.mean(centered * centered, axis=1, keepdims=True)
        inv_std = lax.rsqrt(variance + epsilon)
        return centered * inv_std, inv_std

    def sub_rows(i):
        return pl.ds(mult(i * LN_ROWS, LN_ROWS), LN_ROWS)

    def step_ln():
        for p, low in pieces:
            src = pl.ds(abs_block(p, low), R)
            VEC[0:1, piece_ds(p, low)] = gain[:, src]
            VEC[1:2, piece_ds(p, low)] = shift[:, src]
            VEC[2:3, piece_ds(p, low)] = out_bias[:, src]
        for ld in tok_loads:
            ld.done()

        def body(i, _):
            x_hat, _unused = normalise(0, sub_rows(i))
            XN[pl.ds(mult(own_row + i * LN_ROWS, LN_ROWS), LN_ROWS), :] = (
                x_hat * VEC[0:1, :] + VEC[1:2, :]
            ).astype(bf16)

        lax.fori_loop(0, T // LN_ROWS, body, None)

    steps["ln"] = step_ln

    def tiles(first, stop, body):
        lax.fori_loop(first, stop, lambda i, _: body(pl.ds(mult(i * T, T), T)), None)

    def step_hid(first, stop):
        weight_ready("U0")
        rows_ready("N")

        def body(rows):
            xn = XN[rows, :]
            for m in range(0, F, R):
                cols = slice(m, m + R)
                bias = bu_in[:, pl.ds(mult(lo * F + m, R), R)]
                h = dot(xn, WU[:, cols], NN) + bias
                act, slope = gelu_both(h)
                ACT[rows, cols] = act.astype(bf16)
                DH[rows, cols] = slope.astype(bf16)

        tiles(first, stop, body)

    steps["hid00"] = functools.partial(step_hid, 0, 4)
    steps["hid01"] = functools.partial(step_hid, 4, 8)

    def step_dh(first, stop):
        weight_ready("D0")
        rows_ready("G")
        if first == 0:
            VEC[3:4, 0:F] = jnp.zeros((1, F), f32)

        def body(rows):
            gg = G[rows, :]
            for m in range(0, F, R):
                cols = slice(m, m + R)
                dh = (dot(gg, WD[cols, :], NT) * DH[rows, cols].astype(f32)).astype(bf16)
                DH[rows, cols] = dh
                VEC[3:4, cols] += jnp.sum(dh.astype(f32), axis=0, keepdims=True)

        tiles(first, stop, body)

    steps["dh00"] = functools.partial(step_dh, 0, 4)
    steps["dh01"] = functools.partial(step_dh, 4, 8)

    Q, DA = 0, 1

    def seq_row(s, off):
        return mult((1 - lo if s == 0 else lo) * LEN + off, Q_BLOCK)

    def head_rows(which, begin, cc):
        cols = pl.ds(mult(begin // T * H + cc, LANES), LANES)
        return YS[1, which, begin % T : begin % T + Q_BLOCK, cols]

    def step_proj(s):
        weight_ready("Q", "O")
        rows_ready("N", "G")

        def body(i, _):
            pos = pl.ds(mult(i * T, T), T)
            rows = pl.ds(mult(seq_row(s, 0) + i * T, T), T)
            cs, sn = cos_t[pos, :], sin_t[pos, :]

            def turned(v):
                return [
                    rotate(v[:, a : a + LANES], cs, sn).astype(bf16) for a in range(0, H, LANES)
                ]

            def put(which, vs):
                for n, u in enumerate(vs):
                    YS[1, which, :, pl.ds(mult(i * H + n * LANES, LANES), LANES)] = u

            xn = XN[rows, :]

            def part(k):
                return dot(xn, WQ[k], NN) + bq_in[k : k + 1, pl.ds(mult(lo * H, LANES), H)]

            put(Q, turned(part(0)))
            for n, u in enumerate(turned(part(1))):
                KS[pos, n * LANES : (n + 1) * LANES] = u
            VS[pos, :] = part(2).astype(bf16)
            d_att = dot(G[rows, :], WO[...], NT).astype(bf16)
            put(DA, [d_att[:, a : a + LANES] for a in range(0, H, LANES)])

        lax.fori_loop(0, 4, body, None)

    def step_att(s, first_pair, n_pairs):
        first = lax.broadcasted_iota(jnp.int32, (Q_BLOCK, LANES), 1) < HEAD_DIM
        scaling = HEAD_DIM**-0.5

        def split(v):
            zero = jnp.zeros_like(v)
            return jnp.concatenate([jnp.where(first, v, zero), jnp.where(first, zero, v)], axis=0)

        def join(v):
            return jnp.where(first, v[:Q_BLOCK], v[Q_BLOCK:])

        def pair(hp, _):
            cc = hp * LANES
            out_cols = pl.ds(mult(cc, LANES), LANES)
            for i in range(LEN // Q_BLOCK):
                rr = pl.ds(i * Q_BLOCK, Q_BLOCK)
                out_rows = pl.ds(seq_row(s, i * Q_BLOCK), Q_BLOCK)
                n = (i + 1) * Q_BLOCK
                old = n - Q_BLOCK
                qm = split(head_rows(Q, old, cc))
                dm = split(head_rows(DA, old, cc))
                kk = KS[0:n, out_cols]
                vv = VS[0:n, out_cols]
                st = dot(kk, qm * jnp.asarray(scaling, bf16), NT)
                kpos = lax.broadcasted_iota(jnp.int32, (Q_BLOCK, 2 * Q_BLOCK), 0)
                qpos = lax.broadcasted_iota(jnp.int32, (Q_BLOCK, 2 * Q_BLOCK), 1)
                qpos = jnp.where(qpos < Q_BLOCK, qpos, qpos - Q_BLOCK)
                diagonal = jnp.where(kpos <= qpos, st[old:], big_negative)
                st = diagonal if i == 0 else jnp.concatenate([st[:old], diagonal], axis=0)
                ex = jnp.exp(st - jnp.max(st, axis=0, keepdims=True))
                prob = ex * (1.0 / jnp.sum(ex, axis=0, keepdims=True))
                pb = prob.astype(bf16)
                ATT[out_rows, out_cols] = join(dot(pb, vv, TN)).astype(bf16)
                dv = dot(pb, dm, NN)
                dprob = dot(vv, dm * jnp.asarray(scaling, bf16), NT)
                centre = jnp.sum(dprob * prob, axis=0, keepdims=True)
                ds = (prob * (dprob - centre)).astype(bf16)
                dq = join(dot(ds, kk, TN))
                DP[out_rows, out_cols] = rotate(dq, cos_t[rr, :], -sin_t[rr, :]).astype(bf16)
                dk = dot(ds, qm, NN)
                if i > 0:
                    DK[0:old, :] += dk[:old]
                    DV[0:old, :] += dv[:old]
                DK[rr, :] = dk[old:]
                DV[rr, :] = dv[old:]
            seq = pl.ds(seq_row(s, 0), LEN)
            DP[seq, pl.ds(mult(H + cc, LANES), LANES)] = rotate(
                DK[...], cos_t[...], -sin_t[...]
            ).astype(bf16)
            DP[seq, pl.ds(mult(2 * H + cc, LANES), LANES)] = DV[...].astype(bf16)

        lax.fori_loop(first_pair, first_pair + n_pairs, pair, None)

    half_pairs = H // LANES // 2
    for s in range(2):
        steps["proj%d" % s] = functools.partial(step_proj, s)
        if half_pairs:
            steps["att%d0" % s] = functools.partial(step_att, s, 0, half_pairs)
            steps["att%d1" % s] = functools.partial(step_att, s, half_pairs, half_pairs)
            steps["att%d" % s] = functools.partial(step_att, s, 0, 2 * half_pairs)
        else:
            steps["att%d0" % s] = functools.partial(step_att, s, 0, 1)
            steps["att%d1" % s] = lambda: None
            steps["att%d" % s] = steps["att%d0" % s]

    ff_use = {0: [], 1: []}

    def ff_free(*which):
        for k in which:
            for ld in ff_use[k]:
                ld.done()
            ff_use[k] = []

    def cols_of(p, q):
        return pl.ds(col(p, lo if q == 0 else 1 - lo), R)

    def block_dn(p, q):
        gg = G[:, cols_of(p, q)]
        return [(m, dot(ACT[:, m : m + R], gg, TN)) for m in range(0, F, R)]

    def block_up(p, q):
        return [(0, dot(XN[:, cols_of(p, q)], DH[...], TN))]

    def block_at(p, q):
        cc = cols_of(p, q)
        return [(0, dot(XN[:, cc], DP[...], TN)), (3 * H, dot(ATT[...], G[:, cc], TN))]

    def weight_grad(g, i, block, needs):
        def slot(p, q):
            return (0 if p >= 2 else 2) + (1 - q)

        def pq(p, q):
            return "%d%d" % (p, q)

        for p, q in ((3, 1), (3, 0), (1, 1), (1, 0)):
            k = slot(p, q)
            sends["y" + g + pq(p, q)] = Send(YS.at[i, k], ry.at[i, k], to_y)
        sends["m" + g + "0"] = Send(YS.at[i, slot(3, 0)], rm.at[i, 0], to_hi)
        sends["m" + g + "1"] = Send(YS.at[i, slot(3, 1)], rm.at[i, 1], to_hilo)
        sends["l" + g] = Send(YS.at[i, slot(1, 1)], rl.at[i], to_lo)

        def near(p, q):
            needs()
            k = slot(p, q)
            for off, v in block(p, q):
                YS[i, k, :, off : off + v.shape[1]] = v.astype(bf16)
            start("y" + g + pq(p, q))

        def pass_on(p, q, then):
            k = slot(p, q)
            came = "y" + g + pq(p + 1, q)
            got(came)
            load = Local(ry.at[i, k], LD.at[0, 0:R, 0:F])
            vals = block(p, q)
            sends[came].done()
            load.done()
            for off, v in vals:
                cols = slice(off, off + v.shape[1])
                YS[i, k, :, cols] = (v + LD[0, 0:R, cols].astype(f32)).astype(bf16)
            start(then)

        def fin():
            ff_free(0)
            got("y" + g + "10")
            load = Local(ry.at[i, slot(0, 0)], LD.at[0, 0:R, 0:F])
            vals = block(0, 0)
            load.done()
            for off, v in vals:
                cols = slice(off, off + v.shape[1])
                FF[0, :, cols] = v + LD[0, 0:R, cols].astype(f32)
            ff_use[0] = [Local(FF.at[0], o_part.at[i])]

        for p, q in ((3, 1), (3, 0), (1, 1), (1, 0)):
            steps["near:" + g + pq(p, q)] = functools.partial(near, p, q)
        for q in range(2):
            steps["far:" + g + str(q)] = functools.partial(pass_on, 2, q, "m" + g + str(q))
        steps["swap:" + g] = functools.partial(pass_on, 0, 1, "l" + g)
        steps["fin:" + g] = fin

    weight_grad("D0", 0, block_dn, lambda: rows_ready("G"))
    weight_grad("A", 1, block_at, lambda: None)
    weight_grad("U0", 2, block_up, lambda: None)

    def rows_out(rr, cc):
        return dot(ACT[rr, :], WD[:, cc], NN) + dot(ATT[rr, :], WO[:, cc], NN)

    def rows_dn(rr, cc):
        v = dot(DH[rr, :], WU[cc, :], NT)
        for k in range(3):
            v = v + dot(DP[rr, k * H : (k + 1) * H], WQ[k, cc, :], NT)
        return v

    ring_use = {0: None, 1: None, 2: None}
    ring_next = [0]

    def ring_slot():
        k = ring_next[0]
        ring_next[0] = (k + 1) % 3
        if ring_use[k] is not None:
            ring_use[k].done()
            ring_use[k] = None
        return k

    def load_tokens():
        k = ring_slot()
        return k, [
            Local(tokens.at[:, pl.ds(abs_block(p, low), R)], RING.at[k, :, piece_ds(p, low)])
            for p, low in pieces
        ]

    def own_sub(sub):
        return jnp.concatenate([FF[0, sub, :], FF[1, sub, :]], axis=1) + LD[0, sub, :].astype(f32)

    def finish_out(k_tok):
        k = ring_slot()

        def body(i, _):
            sub = sub_rows(i)
            RING[k, sub, :] = (
                RING[k_tok, sub, :].astype(f32) + own_sub(sub) + VEC[2:3, :]
            ).astype(bf16)

        lax.fori_loop(0, T // LN_ROWS, body, None)
        stores = [
            Local(RING.at[k, :, piece_ds(p, low)], o_out.at[:, pl.ds(abs_block(p, low), R)])
            for p, low in pieces
        ]
        for st in stores:
            st.done()

    def finish_dn(k_tok):
        VEC[4:6, :] = jnp.zeros((2, D), f32)

        def body(i, _):
            sub = sub_rows(i)
            x_hat, inv_std = normalise(k_tok, sub)
            dn = own_sub(sub)
            VEC[4:5, :] += jnp.sum(dn * x_hat, axis=0, keepdims=True)
            VEC[5:6, :] += jnp.sum(dn, axis=0, keepdims=True)
            scaled = dn * VEC[0:1, :]
            gt = (
                inv_std
                * (
                    scaled
                    - jnp.mean(scaled, axis=1, keepdims=True)
                    - x_hat * jnp.mean(scaled * x_hat, axis=1, keepdims=True)
                )
                + G[pl.ds(mult(own_row + i * LN_ROWS, LN_ROWS), LN_ROWS), :].astype(f32)
            )
            FF[0, sub, :] = gt[:, :half_d]
            FF[1, sub, :] = gt[:, half_d:]

        lax.fori_loop(0, T // LN_ROWS, body, None)
        for p, low in pieces:
            dst = pl.ds(abs_block(p, low), R)
            src = pl.ds((p % 2) * 2 * R + low * R, R)
            ff_use[p // 2].append(Local(FF.at[p // 2, :, src], o_gt.at[:, dst]))

    def owners(w, i, partial, needs, finish):
        def chunks(low, xx, cc, loads, store):
            rr = pl.ds(row(low, xx, cc), T)
            for ld in loads:
                ld.done()

            def body(j, _):
                cols = pl.ds(mult(j * CHUNK, CHUNK), CHUNK)
                v = partial(rr, cols)
                for k in range(len(loads)):
                    v = v + LD[k, :, cols].astype(f32)
                store(j, cols, v)

            lax.fori_loop(0, D // CHUNK, body, None)

        def put(name, low, xx, cc, srcs, dst, dev):
            needs()
            loads = [Local(src, LD.at[k]) for k, src in enumerate(srcs)]
            k = ring_slot()

            def store(j, cols, v):
                RING[k, :, cols] = v.astype(bf16)

            chunks(low, xx, cc, loads, store)
            sends[name] = Send(RING.at[k], dst, dev)
            start(name)
            ring_use[k] = sends[name]

        def core(dlo, dx):
            low = lo if dlo == 0 else 1 - lo
            xx = x if dx == 0 else 1 - x
            name = "c%s%d%d" % (w, dlo, dx)
            put(name, low, xx, 1 - c, [], rc.at[i, 2 * dlo + dx], to_c)

        def cross(dlo):
            low = lo if dlo == 0 else 1 - lo
            got("c%s%d1" % (w, dlo))
            name = "x%s%d" % (w, dlo)
            put(name, low, 1 - x, c, [rc.at[i, 2 * dlo + 1]], rx.at[i, dlo], to_x)

        def level():
            got("c%s10" % w, "x%s1" % w)
            put("l" + w, 1 - lo, x, c, [rc.at[i, 2], rx.at[i, 1]], rr_lo.at[i], to_lo)

        def own():
            k_tok, tok_ld = load_tokens()
            got("c%s00" % w, "x%s0" % w)
            loads = [Local(rc.at[i, 0], LD.at[0]), Local(rx.at[i, 0], LD.at[1])]
            ff_free(0, 1)
            n = D // CHUNK // 2

            def store(j, cols, v):
                part = pl.ds(mult(lax.rem(j, n) * CHUNK, CHUNK), CHUNK)
                FF[lax.div(j, n), :, part] = v

            chunks(lo, x, c, loads, store)
            got("l" + w)
            Local(rr_lo.at[i], LD.at[0]).done()
            for ld in tok_ld:
                ld.done()
            finish(k_tok)

        for dlo in range(2):
            for dx in range(2):
                steps["core:%s%d%d" % (w, dlo, dx)] = functools.partial(core, dlo, dx)
            steps["cross:%s%d" % (w, dlo)] = functools.partial(cross, dlo)
        steps["level:" + w] = level
        steps["own:" + w] = own

    owners("o", 0, rows_out, lambda: weight_ready("D0"), finish_out)
    owners("n", 1, rows_dn, lambda: None, finish_dn)

    stage_dev = (to_y, to_hi, to_lo, to_x, to_c)
    for k in range(5):
        sends["v%d" % k] = Send(SV, SR.at[k], stage_dev[k])
        sends["w%d" % k] = Send(SA, SRA.at[k], stage_dev[k])
    abs_d = {pc: lax.div(abs_block(*pc), R) for pc in pieces}

    def step_vec():
        SV[...] = jnp.zeros_like(SV)
        VEC[6:7, 0 : 3 * H] = jnp.zeros((1, 3 * H), f32)
        VEC[7:8, :] = jnp.zeros((1, D), f32)

        def body(rows):
            VEC[6:7, 0 : 3 * H] += jnp.sum(DP[rows, :].astype(f32), axis=0, keepdims=True)

        tiles(0, ROWS // T, body)

        def g_body(i, _):
            rows = pl.ds(mult(own_row + i * LN_ROWS, LN_ROWS), LN_ROWS)
            VEC[7:8, :] += jnp.sum(G[rows, :].astype(f32), axis=0, keepdims=True)

        lax.fori_loop(0, T // LN_ROWS, g_body, None)
        for pc in pieces:
            at = pl.ds(mult(lax.rem(abs_d[pc], 4) * R, R), R)
            SV[pl.ds(lax.div(abs_d[pc], 4), 1), at] = VEC[7:8, piece_cols(*pc)]
        SV[pl.ds(2 + lo, 1), :] = VEC[3:4, 0:F]
        for k in range(3):
            SV[4 + k : 5 + k, pl.ds(mult(lo * H, LANES), H)] = VEC[6:7, k * H : (k + 1) * H]
        start("v0")

    def step_v(k):
        got("v%d" % (k - 1))
        sends["v%d" % (k - 1)].done()
        if k <= 3:
            SV[...] += SR[k - 1]
        else:
            SV[0:2, :] += SR[k - 1, 0:2, :]
        if k < 5:
            start("v%d" % k)
        else:
            o_vec[2:3, 0:half_d] = SV[0:1, :]
            o_vec[2:3, half_d:] = SV[1:2, :]
            o_vec[3:4, 0:half_d] = SV[2:3, :]
            o_vec[3:4, half_d:] = SV[3:4, :]
            o_vec[4:7, 0:half_d] = SV[4:7, :]

    steps["vec"] = step_vec
    for k in range(1, 6):
        steps["v%d" % k] = functools.partial(step_v, k)

    def step_small():
        quarter = D // 4
        for row_, base in ((4, 0), (5, 4)):
            for pc in pieces:
                at = pl.ds(mult(lax.rem(abs_d[pc], 2) * R, R), R)
                SA[pl.ds(base + lax.div(abs_d[pc], 2), 1), at] = VEC[row_ : row_ + 1, piece_cols(*pc)]
        for k in range(5):
            start("w%d" % k)
            got("w%d" % k)
            sends["w%d" % k].done()
            SA[...] += SRA[k]
        for i in range(4):
            o_vec[0:1, i * quarter : (i + 1) * quarter] = SA[i : i + 1, :]
            o_vec[1:2, i * quarter : (i + 1) * quarter] = SA[4 + i : 5 + i, :]

    steps["small"] = step_small

    barrier = pltpu.get_barrier_semaphore()
    for dev in partners:
        pl.semaphore_signal(barrier, inc=1, device_id=dev, device_id_type=pl.DeviceIdType.MESH)
    pl.semaphore_wait(barrier, len(partners))
    o_vec[...] = jnp.zeros_like(o_vec)
    for name in ORDER:
        steps[name]()
    ff_free(0, 1)
    for s in pending:
        s.got()
        s.done()
    assert n_copies[0] <= ssem.shape[0] and n_local[0] <= lsem.shape[0], (n_copies, n_local)


def finish_kernel(
    b_out, b_gt, b_vec, b_part, rm, rl,
    o_out, o_gt, o_gain, o_shift, o_bias, o_bu, o_bq, o_gq, o_go, o_gu, o_gd,
    PART, RM, RL, OUT, GT, GU, GD, GQ, GO, lsem,
):
    R, F = PART.shape[1:]
    H = o_go.shape[0] // 2
    lo = lax.rem(lax.div(lax.axis_index("dp"), 2), 2)
    mult = pl.multiple_of
    n = [0]

    def copy(src, dst):
        d = pltpu.make_async_copy(src, dst, lsem.at[n[0]])
        n[0] += 1
        d.start()
        return d

    order = (1, 0, 2)
    loads = {i: [copy(b_part.at[i], PART.at[i]), copy(rm.at[i], RM.at[i]), copy(rl.at[i], RL.at[i])] for i in order}
    load_out = copy(b_out, OUT)
    load_gt = copy(b_gt, GT)
    o_gain[...] = b_vec[0:1, :]
    o_shift[...] = b_vec[1:2, :]
    o_bias[...] = b_vec[2:3, :]
    o_bu[...] = b_vec[3:4, 0 : 2 * F]
    o_bq[...] = b_vec[4:7, 0 : 2 * H]
    stores = []

    def halves(i, put):
        for ld in loads[i]:
            ld.wait()
        for m in range(0, F, R):
            cols = slice(m, m + R)
            put(lo, m, PART[i, :, cols] + RM[i, 0, :, cols].astype(f32))
            put(1 - lo, m, RL[i, :, cols].astype(f32) + RM[i, 1, :, cols].astype(f32))

    def put_at(half, m, v):
        if m < 3 * H:
            GQ[m // H, :, pl.ds(mult(half * H, H), H)] = v
        else:
            GO[pl.ds(mult(half * H, H), H), :] = v

    def put_dn(half, m, v):
        GD[pl.ds(mult(half * F + m, R), R), :] = v

    def put_up(half, m, v):
        GU[:, pl.ds(mult(half * F + m, R), R)] = v

    for i, put, pairs in (
        (1, put_at, ((GQ, o_gq), (GO, o_go))), (0, put_dn, ((GD, o_gd),)), (2, put_up, ((GU, o_gu),)),
    ):
        halves(i, put)
        for src, dst in pairs:
            stores.append(copy(src, dst))
    load_out.wait()
    stores.append(copy(OUT, o_out))
    load_gt.wait()
    stores.append(copy(GT, o_gt))
    for st in stores:
        st.wait()


VMEM_LIMIT = 64 << 20


def fast_shards(tokens, ln_gain, ln_bias, w_qkv, b_qkv, w_out, w_up, b_up, w_down, out_bias, cot):
    T, D = tokens.shape
    R, F = w_up.shape[0], w_up.shape[1] // 2
    H = w_out.shape[0] // 2
    cos_t, sin_t = rotary_tables(4 * T)
    S = jax.ShapeDtypeStruct
    hbm = pl.BlockSpec(memory_space=pl.ANY)
    vm = pl.BlockSpec(memory_space=pltpu.VMEM)
    outs = pl.pallas_call(
        block_kernel,
        out_shape=(
            S((T, D), bf16), S((T, D), f32), S((8, D), f32), S((3, R, F), f32),
            S((3, 4, R, F), bf16), S((3, 2, R, F), bf16), S((3, R, F), bf16),
            S((2, 4, T, D), bf16), S((2, 2, T, D), bf16), S((2, T, D), bf16),
        ),
        in_specs=[hbm, hbm, vm, vm, vm, hbm, hbm, hbm, hbm, vm, vm, vm, vm],
        out_specs=(hbm, hbm, vm) + (hbm,) * 7,
        scratch_shapes=[
            pltpu.VMEM((8 * T, D), bf16),
            pltpu.VMEM((8 * T, D), bf16),
            pltpu.VMEM((D, F), bf16),
            pltpu.VMEM((F, D), bf16),
            pltpu.VMEM((3, D, H), bf16),
            pltpu.VMEM((H, D), bf16),
            pltpu.VMEM((8 * T, F), bf16),
            pltpu.VMEM((8 * T, F), bf16),
            pltpu.VMEM((8 * T, H), bf16),
            pltpu.VMEM((8 * T, 3 * H), bf16),
            pltpu.VMEM((4 * T, H), bf16),
            pltpu.VMEM((4 * T, H), bf16),
            pltpu.VMEM((4 * T, LANES), f32),
            pltpu.VMEM((4 * T, LANES), f32),
            pltpu.VMEM((3, 4, R, F), bf16),
            pltpu.VMEM((2, R, F), f32),
            pltpu.VMEM((3, T, D), bf16),
            pltpu.VMEM((2, T, D), bf16),
            pltpu.VMEM((8, D), f32),
            pltpu.VMEM((8, D // 2), f32),
            pltpu.VMEM((5, 8, D // 2), f32),
            pltpu.VMEM((8, D // 4), f32),
            pltpu.VMEM((5, 8, D // 4), f32),
            pltpu.SemaphoreType.DMA((96,)),
            pltpu.SemaphoreType.DMA((96,)),
            pltpu.SemaphoreType.DMA((110,)),
        ],
        compiler_params=pltpu.CompilerParams(
            collective_id=0, has_side_effects=True, vmem_limit_bytes=VMEM_LIMIT
        ),
        name="parallel_block",
    )(
        tokens, cot, ln_gain.reshape(1, D), ln_bias.reshape(1, D), out_bias.reshape(1, D),
        w_qkv.transpose(1, 0, 2), w_out, w_up, w_down, b_qkv, b_up.reshape(1, 2 * F), cos_t, sin_t,
    )
    b_out, b_gt, b_vec, b_part, _, rm, rl = outs[:7]
    done = pl.pallas_call(
        finish_kernel,
        out_shape=(
            S((T, D), bf16), S((T, D), f32), S((1, D), f32), S((1, D), f32), S((1, D), f32),
            S((1, 2 * F), f32), S((3, 2 * H), f32),
            S((3, R, 2 * H), f32), S((2 * H, R), f32), S((R, 2 * F), f32), S((2 * F, R), f32),
        ),
        in_specs=[hbm, hbm, vm, hbm, hbm, hbm],
        out_specs=(hbm, hbm) + (vm,) * 5 + (hbm,) * 4,
        scratch_shapes=[
            pltpu.VMEM((3, R, F), f32),
            pltpu.VMEM((3, 2, R, F), bf16),
            pltpu.VMEM((3, R, F), bf16),
            pltpu.VMEM((T, D), bf16),
            pltpu.VMEM((T, D), f32),
            pltpu.VMEM((R, 2 * F), f32),
            pltpu.VMEM((2 * F, R), f32),
            pltpu.VMEM((3, R, 2 * H), f32),
            pltpu.VMEM((2 * H, R), f32),
            pltpu.SemaphoreType.DMA((20,)),
        ],
        compiler_params=pltpu.CompilerParams(vmem_limit_bytes=VMEM_LIMIT),
        name="finish",
    )(b_out, b_gt, b_vec, b_part, rm, rl)
    o_out, o_gt, o_gain, o_shift, o_bias, o_bu, o_bq, o_gq, o_go, o_gu, o_gd = done
    return (
        o_out, o_gt, o_gain.reshape(D), o_shift.reshape(D), o_gq.transpose(1, 0, 2), o_bq, o_go,
        o_gu, o_bu.reshape(2 * F), o_gd, o_bias.reshape(D),
    )


def plain_tables(row_count):
    half_rot = ROT // 2
    positions = jnp.arange(row_count).astype(jnp.float32)
    freqs = 10000.0 ** (-(2.0 * jnp.arange(half_rot).astype(jnp.float32)) / ROT)
    angles = positions[:, None] * freqs[None, :]
    return (jnp.cos(angles)[:, None, :], jnp.sin(angles)[:, None, :])


def plain_rotate(field, cosines, sines):
    half_rot = ROT // 2
    first = field[..., :half_rot]
    second = field[..., half_rot:ROT]
    return jnp.concatenate(
        [first * cosines - second * sines, second * cosines + first * sines, field[..., ROT:]],
        axis=-1,
    )


def gelu_tanh(values):
    return jax.nn.gelu(values, approximate=True)


def causal_scores(query_block, key_rows, block_index):
    block_len = query_block.shape[0]
    query_pos = block_index * block_len + jnp.arange(block_len)
    key_pos = jnp.arange(key_rows.shape[0])
    raw = jnp.einsum("qhd,khd->hqk", query_block, key_rows, preferred_element_type=jnp.float32)
    scaled = raw * HEAD_DIM ** (-0.5)
    return jnp.where(key_pos[None, None, :] <= query_pos[None, :, None], scaled, big_negative)


def attend_forward(queries, key_rows, value_rows, block_len):
    row_count, heads_here, head_size = queries.shape
    n_blocks = row_count // block_len
    query_blocks = queries.reshape(n_blocks, block_len, heads_here, head_size)

    def one_block(item):
        query_block, block_index = item
        scores = causal_scores(query_block, key_rows, block_index)
        top_score = jnp.max(scores, axis=2, keepdims=True)
        exponent = jnp.exp(scores - top_score)
        totals = jnp.sum(exponent, axis=2, keepdims=True)
        probability = (exponent / totals).astype(jnp.bfloat16)
        attended = jnp.einsum(
            "hqk,khd->qhd", probability, value_rows, preferred_element_type=jnp.float32
        )
        return (attended, (top_score + jnp.log(totals))[:, :, 0])

    attended, logsum = lax.map(one_block, (query_blocks, jnp.arange(n_blocks)))
    return (attended.reshape(row_count, heads_here * head_size), logsum)


def attend_backward(queries, key_rows, value_rows, grad_att, logsum, block_len):
    row_count, heads_here, head_size = queries.shape
    n_blocks = row_count // block_len
    query_blocks = queries.reshape(n_blocks, block_len, heads_here, head_size)
    grad_blocks = grad_att.reshape(n_blocks, block_len, heads_here, head_size)
    scaling = HEAD_DIM ** (-0.5)

    def one_block(carry, item):
        grad_keys, grad_values = carry
        query_block, grad_block, lse_block, block_index = item
        scores = causal_scores(query_block, key_rows, block_index)
        probability = jnp.exp(scores - lse_block[:, :, None])
        grad_probs = jnp.einsum(
            "qhd,khd->hqk", grad_block, value_rows, preferred_element_type=jnp.float32
        )
        centre = jnp.sum(grad_probs * probability, axis=2, keepdims=True)
        grad_scores = (probability * (grad_probs - centre) * scaling).astype(jnp.bfloat16)
        grad_query = jnp.einsum(
            "hqk,khd->qhd", grad_scores, key_rows, preferred_element_type=jnp.float32
        )
        grad_keys = grad_keys + jnp.einsum(
            "hqk,qhd->khd", grad_scores, query_block, preferred_element_type=jnp.float32
        )
        grad_values = grad_values + jnp.einsum(
            "hqk,qhd->khd",
            probability.astype(jnp.bfloat16),
            grad_block,
            preferred_element_type=jnp.float32,
        )
        return ((grad_keys, grad_values), grad_query)

    zero_rows = jnp.zeros(key_rows.shape, jnp.float32)
    (grad_keys, grad_values), grad_queries = lax.scan(
        one_block, (zero_rows, zero_rows), (query_blocks, grad_blocks, logsum, jnp.arange(n_blocks))
    )
    return (grad_queries.reshape(row_count, heads_here, head_size), grad_keys, grad_values)


def plain_shards(tokens, ln_gain, ln_bias, w_qkv, b_qkv, w_out, w_up, b_up, w_down, out_bias, cotangent):
    activ = tokens.astype(jnp.float32)
    average = jnp.mean(activ, axis=1, keepdims=True)
    centered = activ - average
    variance = jnp.mean(centered * centered, axis=1, keepdims=True)
    inv_std = lax.rsqrt(variance + epsilon)
    x_hat = centered * inv_std
    normed = lax.all_gather(
        (x_hat * ln_gain + ln_bias).astype(jnp.bfloat16), "tensor", axis=0, tiled=True
    )
    row_count = normed.shape[0]
    block_len = min(row_count, 512)
    qkv_full, out_full, up_full, down_full = (
        lax.all_gather(w_qkv, "dp", axis=0, tiled=True),
        lax.all_gather(w_out, "dp", axis=1, tiled=True),
        lax.all_gather(w_up, "dp", axis=0, tiled=True),
        lax.all_gather(w_down, "dp", axis=1, tiled=True),
    )
    heads_here = w_qkv.shape[2] // HEAD_DIM
    local_width = heads_here * HEAD_DIM
    head_shape = (row_count, heads_here, HEAD_DIM)
    project = (
        jnp.einsum("td,dcf->tcf", normed, qkv_full, preferred_element_type=jnp.float32) + b_qkv
    )
    cosines, sines = plain_tables(row_count)
    queries = plain_rotate(project[:, 0].reshape(head_shape), cosines, sines).astype(jnp.bfloat16)
    key_rows = plain_rotate(project[:, 1].reshape(head_shape), cosines, sines).astype(jnp.bfloat16)
    value_rows = project[:, 2].reshape(head_shape).astype(jnp.bfloat16)
    attended, logsum = attend_forward(queries, key_rows, value_rows, block_len)
    attended = attended.astype(jnp.bfloat16)
    hidden = jnp.dot(normed, up_full, preferred_element_type=jnp.float32) + b_up
    activated = gelu_tanh(hidden).astype(jnp.bfloat16)
    partial_rows = jnp.dot(attended, out_full, preferred_element_type=jnp.float32) + jnp.dot(
        activated, down_full, preferred_element_type=jnp.float32
    )
    summed = lax.psum_scatter(partial_rows, "tensor", scatter_dimension=0, tiled=True)
    output = (activ + summed + out_bias).astype(jnp.bfloat16)
    grad_local = cotangent.astype(jnp.float32)
    grad_rows = lax.all_gather(cotangent, "tensor", axis=0, tiled=True)
    grad_down = jnp.einsum("tf,td->fd", activated, grad_rows, preferred_element_type=jnp.float32)
    grad_act = jnp.einsum("td,fd->tf", grad_rows, down_full, preferred_element_type=jnp.float32)
    gelu_pull = jax.vjp(gelu_tanh, hidden)[1]
    grad_hidden = gelu_pull(grad_act)[0].astype(jnp.bfloat16)
    grad_up = jnp.einsum("td,tf->df", normed, grad_hidden, preferred_element_type=jnp.float32)
    grad_b_up = jnp.sum(grad_hidden.astype(jnp.float32), axis=0)
    grad_normed = jnp.einsum("tf,df->td", grad_hidden, up_full, preferred_element_type=jnp.float32)
    grad_out = jnp.einsum("tf,td->fd", attended, grad_rows, preferred_element_type=jnp.float32)
    grad_att = jnp.einsum(
        "td,fd->tf", grad_rows, out_full, preferred_element_type=jnp.float32
    ).astype(jnp.bfloat16)
    grad_queries, grad_keys, grad_values = attend_backward(
        queries, key_rows, value_rows, grad_att.reshape(head_shape), logsum, block_len
    )
    grad_q_pre = plain_rotate(grad_queries, cosines, -sines).reshape(row_count, local_width)
    grad_k_pre = plain_rotate(grad_keys, cosines, -sines).reshape(row_count, local_width)
    grad_project = jnp.stack(
        [grad_q_pre, grad_k_pre, grad_values.reshape(row_count, local_width)], axis=1
    ).astype(jnp.bfloat16)
    grad_qkv = jnp.einsum("td,tcf->dcf", normed, grad_project, preferred_element_type=jnp.float32)
    grad_b_qkv = jnp.sum(grad_project.astype(jnp.float32), axis=0)
    grad_normed = grad_normed + jnp.einsum(
        "tcf,dcf->td", grad_project, qkv_full, preferred_element_type=jnp.float32
    )
    grad_ln_out = lax.psum_scatter(grad_normed, "tensor", scatter_dimension=0, tiled=True)
    qkv_summed, out_summed, up_summed, down_summed = (
        lax.psum_scatter(grad_qkv, "dp", scatter_dimension=0, tiled=True),
        lax.psum_scatter(grad_out, "dp", scatter_dimension=1, tiled=True),
        lax.psum_scatter(grad_up, "dp", scatter_dimension=0, tiled=True),
        lax.psum_scatter(grad_down, "dp", scatter_dimension=1, tiled=True),
    )
    scaled_grad = grad_ln_out * ln_gain
    grad_tokens = (
        inv_std
        * (
            scaled_grad
            - jnp.mean(scaled_grad, axis=1, keepdims=True)
            - x_hat * jnp.mean(scaled_grad * x_hat, axis=1, keepdims=True)
        )
        + grad_local
    )
    gain_grad, shift_grad, bias_grad = lax.psum(
        (
            jnp.sum(grad_ln_out * x_hat, axis=0),
            jnp.sum(grad_ln_out, axis=0),
            jnp.sum(grad_local, axis=0),
        ),
        ("dp", "tensor"),
    )
    qkv_bias_grad, up_bias_grad = lax.psum((grad_b_qkv, grad_b_up), "dp")
    return (
        output,
        grad_tokens,
        gain_grad,
        shift_grad,
        qkv_summed,
        qkv_bias_grad,
        out_summed,
        up_summed,
        up_bias_grad,
        down_summed,
        bias_grad,
    )


def solution(mesh):
    placed = (
        P(("dp", "tensor"), None),
        P(),
        P(),
        P("dp", None, "tensor"),
        P(None, "tensor"),
        P("tensor", "dp"),
        P("dp", "tensor"),
        P("tensor"),
        P("tensor", "dp"),
        P(),
        P(("dp", "tensor"), None),
    )
    results = (
        P(("dp", "tensor"), None),
        P(("dp", "tensor"), None),
        P(),
        P(),
        P("dp", None, "tensor"),
        P(None, "tensor"),
        P("tensor", "dp"),
        P("dp", "tensor"),
        P("tensor"),
        P("tensor", "dp"),
        P(),
    )
    one_kernel = mesh.shape["dp"] == 8 and mesh.shape["tensor"] == 4
    return jax.shard_map(
        fast_shards if one_kernel else plain_shards,
        mesh=mesh,
        in_specs=placed,
        out_specs=results,
        check_vma=False,
    )
```
